256 devices in a mesh: gx: 4 (over y), gy: 8 (over x, core), gz: 8 (over z).
Axes of the slice: x: 4, y: 4, z: 8, core: 2. Of those that a mesh axis runs over, the one named last changes fastest.
Arguments:
- guess: float32 [64, 256, 1024], P('gx', 'gy', 'gz'), may hold values from -3 to 3
- right_side: float32 [64, 256, 1024], P('gx', 'gy', 'gz'), may hold values from -8 to 8
- screen: float32 [64, 256, 1024], P('gx', 'gy', 'gz'), may hold values from 0.002 to 0.02
Outputs:
- solution: float32 [64, 256, 1024], P('gx', 'gy', 'gz')
The draws below stay inside these ranges and needn't reach their ends.
All inputs are finite; a program needn't handle non-finite values.
Results may differ from the reference program's by a relative error of at most 0.00011.
Values sent between devices are 32-bit elements; how exact they have to be, the bound alone decides.
A program may use at most 64 MiB of HBM per device.

```python
import math
import jax
import jax.numpy as jnp

SWEEPS = 2
MID_SWEEPS = 2
ITERS = 16
NX = 64
NY = 256
NZ = 1024


def draw_right_side(key, part):
    key = jax.random.fold_in(key, 7)
    values = jnp.clip(jax.random.normal(key, (NX, NY, NZ), jnp.float32), -6.0, 6.0)
    return values.astype(jnp.float32)


def block_scale(rng, extent, cuts, least, high):
    factor_of, own = 1.0, jax.random.fold_in(rng, 6)
    for axis_at, parts in cuts:
        heights = jnp.exp(jax.random.uniform(jax.random.fold_in(own, axis_at), (parts,), jnp.float32, least / len(cuts), high / len(cuts)))
        factor_of = factor_of * jnp.repeat(heights, extent[axis_at] // parts).reshape([-1 if axis == axis_at else 1 for axis in range(len(extent))])
    return factor_of


def centred(rng, extent, width, limit, shards=(), dtype=jnp.bfloat16):
    array = width * jax.random.normal(rng, extent, jnp.float32)
    if shards:
        array = array * block_scale(rng, extent, shards, -0.22, 0.18)
    return jnp.clip(array, -limit, limit).astype(dtype)


def setup_inputs(seed: int = 0) -> dict:
    seeds = jax.random.split(jax.random.key(seed), 4)
    guess = centred(seeds[0], (NX, NY, NZ), 0.5, 3.0, ((0, 4), (1, 8), (2, 8)), jnp.float32)
    right_side = draw_right_side(jax.random.fold_in(seeds[3], 71), 0)
    screen = jnp.clip(jnp.exp(math.log(0.02) - 2.30258502 * jax.random.uniform(seeds[2], (NX, NY, NZ), jnp.float32) ** block_scale(seeds[2], (NX, NY, NZ), ((0, 4), (1, 8), (2, 8)), -0.2, 0.2)), 0.002, 0.02)
    return dict(guess=guess, right_side=right_side, screen=screen)


OMEGA = 0.8
CENTER = 14.0


def neighbours(padded):
    rows_x = padded.shape[0] - 2
    rows_y = padded.shape[1] - 2
    rows_z = padded.shape[2] - 2
    total = jnp.zeros((rows_x, rows_y, rows_z), jnp.float32)
    for first in range(3):
        for second in range(3):
            for third in range(3):
                count = abs(first - 1) + abs(second - 1) + abs(third - 1)
                if count == 0:
                    continue
                weight = (1.0, 0.5, 0.25)[count - 1]
                total = total + weight * padded[first:first + rows_x, second:second + rows_y, third:third + rows_z]
    return total


def misfit(field, rhs, coeff):
    return rhs - ((CENTER + coeff) * field - neighbours(jnp.pad(field, 1)))


def relax(field, rhs, coeff):
    return field + OMEGA * misfit(field, rhs, coeff) / (CENTER + coeff)


def restrict(field):
    rows_x, rows_y, rows_z = field.shape
    blocks = field.reshape(rows_x // 2, 2, rows_y // 2, 2, rows_z // 2, 2)
    return 4.0 * jnp.mean(blocks, axis=(1, 3, 5))


def prolong(field):
    return jnp.repeat(jnp.repeat(jnp.repeat(field, 2, axis=0), 2, axis=1), 2, axis=2)


def reference(guess, right_side, screen):
    fine = guess
    for repeat in range(SWEEPS):
        fine = relax(fine, right_side, screen)
    level_rhs = restrict(misfit(fine, right_side, screen))
    level_coeff = restrict(screen)
    level_corr = jnp.zeros_like(level_rhs)
    for repeat in range(MID_SWEEPS):
        level_corr = relax(level_corr, level_rhs, level_coeff)
    coarse_rhs = restrict(restrict(misfit(level_corr, level_rhs, level_coeff)))
    coarse_coeff = restrict(restrict(level_coeff))
    coarse_corr = jnp.zeros_like(coarse_rhs)
    for repeat in range(ITERS):
        coarse_corr = relax(coarse_corr, coarse_rhs, coarse_coeff)
    level_corr = level_corr + prolong(prolong(coarse_corr))
    return fine + prolong(level_corr)
```

```python
import functools
import itertools

import jax
import jax.numpy as jnp
from jax import lax
from jax.experimental import pallas as pl
from jax.experimental.pallas import tpu as pltpu
from jax.sharding import PartitionSpec as P

ITERS = 16
OMEGA = 0.8
CENTER = 14.0
F32 = jnp.float32
MESH = pl.DeviceIdType.MESH
HIGH = lax.Precision.HIGHEST

NX, NY, NZ = 16, 32, 128
PX, PY, PZ = 22, 40, 256
NEIGHBOURS = sorted(
    (o for o in itertools.product((-1, 0, 1), repeat=3) if o != (0, 0, 0)),
    key=lambda o: (-sum(abs(v) for v in o)),
)


def iota(shape, dim):
    return lax.broadcasted_iota(jnp.int32, shape, dim)


def mod(v, n):
    return lax.rem(v + n, n)


def plane_sum(v):
    rows, cols = v.shape
    a = v + v + pltpu.roll(v, 1, 1) + pltpu.roll(v, cols - 1, 1)
    return a + a + pltpu.roll(a, 1, 0) + pltpu.roll(a, rows - 1, 0)


def kernel(
    sizes,
    guess,
    rhs,
    scr,
    out,
    mm,
    cc,
    va,
    vb,
    packs,
    zland,
    rx,
    sx,
    s24,
    c1r,
    s1r,
    ex,
    zpack,
    zmid,
    e1f,
    msg,
    cmsg,
    bf,
    bc,
    cof,
    coc,
    cov,
    eout,
    dummy_f,
    dummy_c,
    load_sem,
    fs,
    fr,
    ms,
    mr,
    gsem,
):
    gx, gy, gz = sizes
    ix, iy, iz = lax.axis_index("gx"), lax.axis_index("gy"), lax.axis_index("gz")

    def device(o):
        return (
            ix if o[0] == 0 else lax.rem(ix + o[0] % gx, gx),
            iy if o[1] == 0 else lax.rem(iy + o[1] % gy, gy),
            iz if o[2] == 0 else lax.rem(iz + o[2] % gz, gz),
        )

    peers = [
        o
        for o in itertools.product(range(gx), range(gy), (-1, 0, 1))
        if o != (0, 0, 0)
    ]
    peers = [(a - gx if a > gx // 2 else a, b - gy if b > gy // 2 else b, c) for a, b, c in peers]
    peers.sort(key=lambda o: -(abs(o[0]) + (abs(o[1]) + 1) // 2 + abs(o[2])))

    own = []
    for a, ref in enumerate((scr, rhs, guess)):
        copy = pltpu.make_async_copy(ref, mm.at[2 - a, pl.ds(3, NX), pl.ds(0, NY), pl.ds(0, NZ)], load_sem.at[a])
        copy.start()
        own.append(copy)
    for a in range(3):
        for p in range(PX):
            mm[a, p, NY:PY, 0:NZ] = jnp.zeros((PY - NY, NZ), F32)
    for side in range(2):
        for xs in range(3):
            zland[side, xs, NY:PY, :] = jnp.zeros((PY - NY, 128), F32)
            zmid[side, xs, 16:24, :] = jnp.zeros((8, 128), F32)
    ex[...] = jnp.zeros_like(ex)
    s24[...] = jnp.zeros_like(s24)

    barrier = pltpu.get_barrier_semaphore()
    for o in peers:
        pl.semaphore_signal(barrier, inc=1, device_id=device(o), device_id_type=MESH)

    r_i, c_i = iota((128, 128), 0), iota((128, 128), 1)
    pool = jnp.where(r_i // 2 == c_i, 0.5, 0.0).astype(F32)
    pool_halo = jnp.where(
        ((r_i < 2) & (c_i == 64)) | ((r_i >= 126) & (c_i == 127)), 0.5, 0.0
    ).astype(F32)
    copy_mid = jnp.where((c_i // 2 == r_i), 1.0, 0.0).astype(F32)
    copy_coarse = jnp.where((c_i // 8 == r_i), 1.0, 0.0).astype(F32)
    z_of = jnp.where(r_i < 64, r_i // 4 + 1, jnp.where(r_i < 68, 17, jnp.where(r_i >= 124, 0, 99)))
    gather_f = jnp.where((c_i % 20 == z_of) & (c_i < 120), 0.25, 0.0).astype(F32)
    gather_c = jnp.where((r_i // 4 == c_i % 16) & (r_i < 64), 0.25, 0.0).astype(F32)

    def dot(a, b):
        return jnp.dot(a, b, precision=HIGH, preferred_element_type=F32)

    for copy in own:
        copy.wait()

    for q in range(8):
        rx[q] = mm[2, 3 + 2 * q, 0:NY, 0:NZ] + mm[2, 4 + 2 * q, 0:NY, 0:NZ]
    s1_own = dot((rx[:, pl.ds(0, 16, 2), :] + rx[:, pl.ds(1, 16, 2), :]).reshape(128, 128), pool).reshape(8, 16, 128)
    lanes16 = iota((16, 128), 1)
    rows16 = iota((16, 128), 0)
    for xc in range(2):
        s4 = s1_own[4 * xc] + s1_own[4 * xc + 1] + s1_own[4 * xc + 2] + s1_own[4 * xc + 3]
        s4 = dot(s4, gather_c)
        s3 = jnp.sum(jnp.where((lanes16 // 16) % 4 == rows16 // 4, s4, 0.0), axis=0, keepdims=True)
        c3 = OMEGA / (CENTER + s3)
        for k in range(3):
            cmsg[k, xc : xc + 1, :] = c3 if k == 0 else pltpu.roll(c3, 16 * k, 1)

    lane = iota((NY, 128), 1)
    head = jnp.zeros((NY, 128), F32)
    tail = jnp.zeros((NY, 128), F32)
    for p in range(NX):
        g = mm[0, 3 + p, 0:NY, 0:NZ]
        f = mm[1, 3 + p, 0:NY, 0:NZ]
        s = mm[2, 3 + p, 0:NY, 0:NZ]

        def put(acc, v, to, at, count):
            first = 8 * p + to
            return jnp.where((lane >= first) & (lane < first + count), pltpu.roll(v, (first - at) % 128, 1), acc)

        head = put(head, g, 0, 0, 3)
        head = put(head, f, 3, 0, 2)
        head = put(head, s, 5, 0, 2)
        tail = put(tail, g, 5, 125, 3)
        tail = put(tail, f, 3, 126, 2)
        tail = put(tail, s, 1, 126, 2)
    packs[0] = head
    packs[1] = tail

    pl.semaphore_wait(barrier, len(peers))

    fine_copies = []

    def send_fine(o, src, dst):
        i = len(fine_copies)
        copy = pltpu.make_async_remote_copy(
            src_ref=src, dst_ref=dst, send_sem=fs.at[i], recv_sem=fr.at[i], device_id=device(o), device_id_type=MESH
        )
        copy.start()
        fine_copies.append(copy)

    def x_part(d, depth):
        if d == 0:
            return (3, NX), (3, NX)
        return ((3 + NX - depth, depth), (3 - depth, depth)) if d == 1 else ((3, depth), (3 + NX, depth))

    def y_part(d, depth):
        if d == 0:
            return (0, NY), (0, NY)
        return ((NY - depth, depth), (PY - depth, depth)) if d == 1 else ((0, depth), (NY, depth))

    for o in ((1, 0, 0), (-1, 0, 0)):
        for a, depth in ((0, 3), (1, 2), (2, 2)):
            (p0, n), (q0, _) = x_part(o[0], depth)
            send_fine(
                o,
                mm.at[a, pl.ds(p0, n), pl.ds(0, NY), pl.ds(0, NZ)],
                mm.at[a, pl.ds(q0, n), pl.ds(0, NY), pl.ds(0, NZ)],
            )
    for o in NEIGHBOURS:
        dx, dy, dz = o
        (s0, sn), (t0, _) = y_part(dy, 3)
        if dz == 0:
            if dy == 0:
                continue
            (p0, n), (q0, _) = x_part(dx, 3)
            send_fine(
                o,
                mm.at[:, pl.ds(p0, n), pl.ds(s0, sn), pl.ds(0, NZ)],
                mm.at[:, pl.ds(q0, n), pl.ds(t0, sn), pl.ds(0, NZ)],
            )
        else:
            side = 1 if dz == 1 else 0
            send_fine(o, packs.at[side, pl.ds(s0, sn), :], zland.at[side, 1 - dx, pl.ds(t0, sn), :])

    c_copies = []
    for o in peers:
        copy = pltpu.make_async_remote_copy(
            src_ref=cmsg.at[1 - o[2]],
            dst_ref=bc.at[1 - o[2], iy, pl.ds(2 * ix, 2), :],
            send_sem=gsem.at[0],
            recv_sem=gsem.at[1],
            device_id=device(o),
            device_id_type=MESH,
        )
        copy.start()
        c_copies.append(copy)
    pltpu.make_async_copy(cmsg.at[1], bc.at[1, iy, pl.ds(2 * ix, 2), :], gsem.at[1]).start()

    for copy in fine_copies:
        copy.wait_recv()

    rows_in = iota((PY, 128), 0)
    lane40 = iota((PY, 128), 1)
    row_ok = ((rows_in < 36) | (iy > 0)) & ((rows_in < NY) | (rows_in >= 36) | (iy < gy - 1))
    col_ok = ((lane40 < 64) & (iz < gz - 1)) | ((lane40 >= 64) & (iz > 0))
    both_ok = row_ok & col_ok
    for p in range(PX):
        if p < 3:
            xs, q, x_ok = 0, NX - 3 + p, ix > 0
        elif p < 3 + NX:
            xs, q, x_ok = 1, p - 3, None
        else:
            xs, q, x_ok = 2, p - 3 - NX, ix < gx - 1
        h = zland[0, xs]
        t = zland[1, xs]
        ok0 = row_ok if x_ok is None else row_ok & x_ok
        ok1 = both_ok if x_ok is None else both_ok & x_ok
        g1 = jnp.where(
            lane40 < 64, pltpu.roll(h, (-8 * q) % 128, 1), pltpu.roll(t, (-8 * q - 8) % 128, 1)
        )
        mm[0, p, :, NZ:PZ] = jnp.where(ok1, g1, 0.0)
        if x_ok is None:
            mm[0, p, NY:PY, 0:NZ] = jnp.where(ok0[NY:PY], mm[0, p, NY:PY, 0:NZ], 0.0)
        else:
            mm[0, p, :, 0:NZ] = jnp.where(ok0, mm[0, p, :, 0:NZ], 0.0)
        if 0 < p < PX - 1:
            f1 = jnp.where(lane40 < 64, pltpu.roll(h, (-8 * q - 3) % 128, 1), pltpu.roll(t, (-8 * q - 5) % 128, 1))
            s1 = jnp.where(lane40 < 64, pltpu.roll(h, (-8 * q - 5) % 128, 1), pltpu.roll(t, (-8 * q - 3) % 128, 1))
            s1 = jnp.where((lane40 < 2) | (lane40 >= 126), s1, 0.0)
            mm[1, p, :, NZ:PZ] = f1
            mm[2, p, :, NZ:PZ] = s1
            cc[p, :, 0:NZ] = jnp.where(ok0, OMEGA / (CENTER + mm[2, p, :, 0:NZ]), 0.0)
            cc[p, :, NZ:PZ] = jnp.where(ok1, OMEGA / (CENTER + s1), 0.0)

    def sweep(src, dst, first, last):
        def body(p, carry):
            b0, b1 = carry
            b2 = plane_sum(src[p + 1])
            v = src[p]
            t = b0 + b1 + b1 + b2
            dst[p] = 0.2 * v + cc[p] * (mm[1, p] + 0.25 * t - 2.0 * v)
            return b1, b2

        lax.fori_loop(first, last, body, (plane_sum(src[first - 1]), plane_sum(src[first])), unroll=2)

    sweep(mm.at[0], va, 1, PX - 1)
    sweep(va, vb, 2, PX - 2)

    def residual(p, b0, b1):
        b2 = plane_sum(vb[p + 1])[0:NY, 0:NZ]
        t = b0 + b1 + b1 + b2
        v = vb[p, 0:NY, 0:NZ]
        return mm[1, p, 0:NY, 0:NZ] - (CENTER + 2.0 + mm[2, p, 0:NY, 0:NZ]) * v + 0.25 * t, b2

    def pair(q, carry):
        b0, b1 = carry
        r0, b2 = residual(3 + 2 * q, b0, b1)
        r1, b3 = residual(4 + 2 * q, b1, b2)
        rx[q] = r0 + r1
        return b2, b3

    lax.fori_loop(0, 8, pair, (plane_sum(vb[2])[0:NY, 0:NZ], plane_sum(vb[3])[0:NY, 0:NZ]))
    f1 = dot((rx[:, pl.ds(0, 16, 2), :] + rx[:, pl.ds(1, 16, 2), :]).reshape(128, 128), pool).reshape(8, 16, 128)

    for q in range(10):
        sx[0, q] = mm[2, 1 + 2 * q, :, 0:NZ] + mm[2, 2 + 2 * q, :, 0:NZ]
        sx[1, q] = mm[2, 1 + 2 * q, :, NZ:PZ] + mm[2, 2 + 2 * q, :, NZ:PZ]
    for half in range(2):
        v = sx[half, :, pl.ds(0, 20, 2), :] + sx[half, :, pl.ds(1, 20, 2), :]
        s24[half, :, 0:20, :] = v
        s24[half, :, 23:24, :] = v[:, 19:20, :]
    s1 = dot(s24[0].reshape(240, 128), pool) + dot(s24[1].reshape(240, 128), pool_halo)
    s1 = s1.reshape(10, 24, 128)
    row24, lane24 = iota((24, 128), 0), iota((24, 128), 1)
    ok24 = (
        ((row24 < 20) | (iy > 0))
        & ((row24 < 16) | (row24 >= 20) | (iy < gy - 1))
        & ((lane24 < 96) | (iz > 0))
        & ((lane24 < 64) | (lane24 >= 96) | (iz < gz - 1))
    )
    for q in range(10):
        ok = ok24 & (ix > 0) if q == 0 else (ok24 & (ix < gx - 1) if q == 9 else ok24)
        s1r[q] = s1[q]
        c1r[q] = jnp.where(ok, OMEGA / (CENTER + s1[q]), 0.0)

    zero8 = jnp.zeros((8, 128), F32)
    f1z = [jnp.concatenate([f1[q], zero8], axis=0) for q in range(8)]
    e_own = [c1r[q + 1] * f1z[q] for q in range(8)]
    for q in range(8):
        ex[q + 1, 0:16, :] = e_own[q][0:16]

    def weigh(b, p):
        terms = [b[i] * w for i, w in ((p - 1, 1.0), (p, 2.0), (p + 1, 1.0)) if i in b]
        return 0.25 * functools.reduce(lambda m, n: m + n, terms)

    sums = {q: plane_sum(e_own[q]) for q in range(8)}
    e_two = {}
    for q in range(-1, 9):
        t = weigh(sums, q)
        if 0 <= q < 8:
            e_two[q] = 0.2 * e_own[q] + c1r[q + 1] * (f1z[q] + t - 2.0 * e_own[q])
        else:
            e_two[q] = c1r[q + 1] * t
    sums = {q: plane_sum(e_two[q]) for q in range(-1, 9)}
    parts = {}
    for q in range(-2, 10):
        r = weigh(sums, q)
        if q in e_two:
            r = r - (CENTER + 2.0 + s1r[q + 1]) * e_two[q]
        if 0 <= q < 8:
            r = r + f1z[q]
        at = (q + 4) // 4
        parts[at] = parts[at] + r if at in parts else r
    y_of = jnp.where(row24 < 16, row24 // 4 + 1, jnp.where(row24 < 18, 5, jnp.where(row24 >= 22, 0, 99)))
    z_at = lane24 % 20
    keep = (lane24 // 20 == y_of) & ((z_at != 0) | (iz > 0)) & ((z_at != 17) | (iz < gz - 1))
    stacked = dot(jnp.concatenate([parts[i] for i in range(4)], axis=0), gather_f)
    for i in range(4):
        row = jnp.sum(jnp.where(keep, stacked[24 * i : 24 * i + 24], 0.0), axis=0, keepdims=True)
        for k in range(3):
            msg[k, i : i + 1, :] = row if k == 0 else pltpu.roll(row, 16 * k, 1)

    slot = bf.at[:, lax.rem(ix, 2), iy, pl.ds(4 * (ix // 2), 4), :]
    for o in peers:
        copy = pltpu.make_async_remote_copy(
            src_ref=msg.at[1 - o[2]],
            dst_ref=slot.at[1 - o[2]],
            send_sem=gsem.at[2],
            recv_sem=gsem.at[3],
            device_id=device(o),
            device_id_type=MESH,
        )
        copy.start()
    pltpu.make_async_copy(msg.at[1], slot.at[1], gsem.at[3]).start()

    ztail = jnp.zeros((16, 128), F32)
    for q in range(8):
        ztail = jnp.where(lanes16 == q, pltpu.roll(e_own[q][0:16], (q - 63) % 128, 1), ztail)
        ztail = jnp.where(lanes16 == 64 + q, pltpu.roll(e_own[q][0:16], 64 + q, 1), ztail)
    zpack[...] = ztail
    mid_copies = []
    for o in NEIGHBOURS:
        dx, dy, dz = o
        (s0, sn), t0 = ((0, 16), 0) if dy == 0 else (((15, 1), 23) if dy == 1 else ((0, 1), 16))
        if dz == 0:
            (p0, n), q0 = ((1, 8), 1) if dx == 0 else (((8, 1), 0) if dx == 1 else ((1, 1), 9))
            src = ex.at[pl.ds(p0, n), pl.ds(s0, sn), :]
            dst = ex.at[pl.ds(q0, n), pl.ds(t0, sn), :]
        else:
            side = 1 if dz == 1 else 0
            src = zpack.at[pl.ds(s0, sn), :]
            dst = zmid.at[side, 1 - dx, pl.ds(t0, sn), :]
        i = len(mid_copies)
        copy = pltpu.make_async_remote_copy(
            src_ref=src, dst_ref=dst, send_sem=ms.at[i], recv_sem=mr.at[i], device_id=device(o), device_id_type=MESH
        )
        copy.start()
        mid_copies.append(copy)

    pltpu.make_async_copy(bc, bc, gsem.at[1]).wait()
    lane8, row8 = iota((8, 128), 1), iota((8, 128), 0)
    block = (lane8 // 16) % 4
    z_ok = (block < 3) & ((block > 0) | (iz > 0)) & ((block < 2) | (iz < gz - 1))
    low = lane8 < 64
    half = {}
    for y in range(32):
        j, yy = y // 4, y % 4
        d = (lane8 // 16 - yy + 8) % 4
        v = jnp.where(d == 0, bc[0, j], jnp.where(d == 1, bc[1, j], bc[2, j]))
        if yy:
            v = pltpu.roll(v, 128 - 16 * yy, 1)
        if y < 16:
            half[y] = v
        else:
            coc[y - 16] = jnp.where(z_ok, jnp.where(low, half[y - 16], v), 0.0)

    for copy in mid_copies:
        copy.wait_recv()
    mid_sums = {}
    for p in range(10):
        if p == 0:
            xs, q, x_ok = 0, 7, ix > 0
        elif p < 9:
            xs, q, x_ok = 1, p - 1, None
        else:
            xs, q, x_ok = 2, 0, ix < gx - 1
        v = ex[p]
        v = jnp.where(lane24 == 64, pltpu.roll(zmid[0, xs], (-q) % 128, 1), v)
        v = jnp.where(lane24 == 127, pltpu.roll(zmid[1, xs], (127 - q) % 128, 1), v)
        ok = ok24 if x_ok is None else ok24 & x_ok
        mid_sums[p] = plane_sum(jnp.where(ok, v, 0.0))
    e1 = []
    for q in range(8):
        t = weigh(mid_sums, q + 1)[0:16]
        e = e_own[q][0:16]
        e1.append(0.2 * e + c1r[q + 1, 0:16] * (f1[q] + t - 2.0 * e))
    e1 = dot(jnp.concatenate(e1, axis=0), copy_mid).reshape(8, 16, 128)
    e1f[:, pl.ds(0, 16, 2), :] = e1
    e1f[:, pl.ds(1, 16, 2), :] = e1

    pltpu.make_async_copy(bf, bf, gsem.at[3]).wait()
    total = {}
    for j in range(gy):
        v = []
        for k in range(3):
            even = jnp.where(row8 < 7, pltpu.roll(bf[k, 0, j], 7, 0), 0.0)
            odd = jnp.where(row8 > 0, pltpu.roll(bf[k, 1, j], 1, 0), 0.0)
            v.append(even + odd)
        for yy in range(6):
            y = 4 * j + yy - 1
            if not 0 <= y < 32:
                continue
            w = None
            for k in range(3):
                at = (lane8 - (20 * yy + 16 * k) + 256) % 128
                part = jnp.where(at < 18, v[k], 0.0)
                w = part if w is None else w + part
            w = pltpu.roll(w, (64 * (y // 16) - 20 * yy - 1) % 128, 1)
            total[y] = total[y] + w if y in total else w
    for m in range(16):
        cof[m] = jnp.where(z_ok, jnp.where(low, total[m], total[m + 16]), 0.0)
        cov[m] = coc[m] * cof[m]

    def coarse(i, v):
        wrap_up = jnp.where(low, 0.0, pltpu.roll(v[15], 64, 1))
        wrap_down = jnp.where(low, pltpu.roll(v[0], 64, 1), 0.0)
        new = []
        for m in range(16):
            up = v[m - 1] if m else wrap_up
            down = v[m + 1] if m < 15 else wrap_down
            a = up + down + 2.0 * v[m]
            b = 2.0 * a + jnp.where(row8 == 0, 0.0, pltpu.roll(a, 1, 0)) + jnp.where(row8 == 7, 0.0, pltpu.roll(a, 7, 0))
            t = 2.0 * b + pltpu.roll(b, 1, 1) + pltpu.roll(b, 127, 1)
            new.append(0.2 * v[m] + coc[m] * (cof[m] + 0.25 * t - 2.0 * v[m]))
        return tuple(new)

    v = lax.fori_loop(0, ITERS - 1, coarse, tuple(cov[m] for m in range(16)))
    for m in range(16):
        cov[m] = v[m]

    mine = cov[pl.ds(4 * lax.rem(iy, 4), 4)]
    mine = mine.reshape(32, 128)
    mine = jnp.where(iy < 4, pltpu.roll(mine, 112, 1), pltpu.roll(mine, 48, 1))
    eout[...] = dot(mine, copy_coarse).reshape(4, 8, 128)
    for xc in range(2):
        for t in range(4):
            e3 = jnp.broadcast_to(eout[t, pl.ds(2 * ix + xc, 1), :], (8, 128))
            for p in range(8 * xc, 8 * xc + 8):
                rows = slice(8 * t, 8 * t + 8)
                out[p, rows, :] = vb[3 + p, rows, 0:NZ] + e1f[p // 2, rows, :] + e3

    for copy in fine_copies + mid_copies:
        copy.wait_send()
    pltpu.make_async_copy(dummy_c, dummy_c, gsem.at[0]).wait()
    pltpu.make_async_copy(dummy_f, dummy_f, gsem.at[2]).wait()


def on_device(sizes, guess, right_side, screen):
    vm = pltpu.VMEM
    n_peers = sizes[0] * sizes[1] * 3 - 1
    return pl.pallas_call(
        functools.partial(kernel, sizes),
        out_shape=jax.ShapeDtypeStruct((NX, NY, NZ), F32),
        in_specs=[pl.BlockSpec(memory_space=pltpu.HBM)] * 3,
        out_specs=pl.BlockSpec(memory_space=pltpu.VMEM),
        scratch_shapes=[
            vm((3, PX, PY, PZ), F32),
            vm((PX, PY, PZ), F32),
            vm((PX, PY, PZ), F32),
            vm((PX, PY, PZ), F32),
            vm((2, NY, 128), F32),
            vm((2, 3, PY, 128), F32),
            vm((8, NY, 128), F32),
            vm((2, 10, PY, 128), F32),
            vm((2, 10, 24, 128), F32),
            vm((10, 24, 128), F32),
            vm((10, 24, 128), F32),
            vm((10, 24, 128), F32),
            vm((16, 128), F32),
            vm((2, 3, 24, 128), F32),
            vm((8, NY, 128), F32),
            vm((3, 4, 128), F32),
            vm((3, 2, 128), F32),
            vm((3, 2, 8, 8, 128), F32),
            vm((3, 8, 8, 128), F32),
            vm((16, 8, 128), F32),
            vm((16, 8, 128), F32),
            vm((16, 8, 128), F32),
            vm((4, 8, 128), F32),
            vm((n_peers, 4, 128), F32),
            vm((n_peers, 2, 128), F32),
            pltpu.SemaphoreType.DMA((3,)),
            pltpu.SemaphoreType.DMA((30,)),
            pltpu.SemaphoreType.DMA((30,)),
            pltpu.SemaphoreType.DMA((26,)),
            pltpu.SemaphoreType.DMA((26,)),
            pltpu.SemaphoreType.DMA((4,)),
        ],
        compiler_params=pltpu.CompilerParams(
            collective_id=0, has_side_effects=True, vmem_limit_bytes=48 * 1024 * 1024
        ),
        name="multigrid",
    )(guess, right_side, screen)


def solution(mesh):
    placed = P("gx", "gy", "gz")
    sizes = tuple(mesh.shape[a] for a in ("gx", "gy", "gz"))
    return jax.shard_map(
        functools.partial(on_device, sizes), mesh=mesh, in_specs=(placed,) * 3, out_specs=placed, check_vma=False
    )
```

```python
import functools
import itertools

import jax
import jax.numpy as jnp
from jax import lax
from jax.experimental import pallas as pl
from jax.experimental.pallas import tpu as pltpu
from jax.sharding import PartitionSpec as P

ITERS = 16
OMEGA = 0.8
CENTER = 14.0
F32 = jnp.float32
MESH = pl.DeviceIdType.MESH

NX, NY, NZ = 16, 32, 128
PX, PY, PZ = 22, 40, 256
NEIGHBOURS = sorted(
    (o for o in itertools.product((-1, 0, 1), repeat=3) if o != (0, 0, 0)),
    key=lambda o: (-sum(abs(v) for v in o)),
)


def iota(shape, dim):
    return lax.broadcasted_iota(jnp.int32, shape, dim)


def mod(v, n):
    return lax.rem(v + n, n)


def plane_sum(v):
    rows, cols = v.shape
    a = v + v + pltpu.roll(v, 1, 1) + pltpu.roll(v, cols - 1, 1)
    return a + a + pltpu.roll(a, 1, 0) + pltpu.roll(a, rows - 1, 0)


def kernel(
    sizes,
    guess,
    rhs,
    scr,
    out,
    mm,
    cc,
    va,
    vb,
    packs,
    zland,
    rx,
    sx,
    s24,
    c1r,
    s1r,
    ex,
    zpack,
    zmid,
    e1f,
    base,
    msg,
    bf,
    cof,
    coc,
    cov,
    eout,
    dummy,
    load_sem,
    fs,
    fr,
    ms,
    mr,
    gsem,
):
    gx, gy, gz = sizes
    ix, iy, iz = lax.axis_index("gx"), lax.axis_index("gy"), lax.axis_index("gz")

    def device(o):
        return (
            ix if o[0] == 0 else lax.rem(ix + o[0] % gx, gx),
            iy if o[1] == 0 else lax.rem(iy + o[1] % gy, gy),
            iz if o[2] == 0 else lax.rem(iz + o[2] % gz, gz),
        )

    peers = [
        o
        for o in itertools.product(range(gx), range(gy), (-1, 0, 1))
        if o != (0, 0, 0)
    ]
    peers = [(a - gx if a > gx // 2 else a, b - gy if b > gy // 2 else b, c) for a, b, c in peers]

    def hops(o):
        return abs(o[0]) + (abs(o[1]) + 1) // 2 + abs(o[2])

    peers.sort(key=lambda o: -hops(o))

    def has(dz):
        return iz < gz - 1 if dz == 1 else iz > 0

    def by_side(offsets, act):
        for o in offsets:
            if o[2] == 0:
                act(o)
        for dz in (1, -1):

            @pl.when(has(dz))
            def _(dz=dz):
                for o in offsets:
                    if o[2] == dz:
                        act(o)

    heard = [(1, 3, 0), (1, 2, 0), (1, -2, 0), (0, 3, 0), (0, 2, 0), (0, -2, 0)] + NEIGHBOURS
    barrier = pltpu.get_barrier_semaphore()
    by_side(
        [(-o[0], -o[1], -o[2]) for o in heard],
        lambda o: pl.semaphore_signal(barrier, inc=1, device_id=device(o), device_id_type=MESH),
    )
    sides = (iz > 0).astype(jnp.int32) + (iz < gz - 1).astype(jnp.int32)

    own = []
    for a, ref in ((2, scr), (0, guess), (1, rhs)):
        copy = pltpu.make_async_copy(ref, mm.at[a, pl.ds(3, NX), pl.ds(0, NY), pl.ds(0, NZ)], load_sem.at[a])
        copy.start()
        own.append(copy)
    for a in range(3):
        for p in range(PX):
            mm[a, p, NY + 3 : PY - 3, 0:NZ] = jnp.zeros((PY - NY - 6, NZ), F32)
    for side in range(2):
        for xs in range(3):
            zland[side, xs, NY + 3 : PY - 3, :] = jnp.zeros((PY - NY - 6, 128), F32)
            zmid[side, xs, 17:23, :] = jnp.zeros((6, 128), F32)
    for q in range(10):
        ex[q, 17:23, :] = jnp.zeros((6, 128), F32)
    s24[...] = jnp.zeros_like(s24)

    for side, dz in ((0, 1), (1, -1)):

        @pl.when(jnp.logical_not(has(dz)))
        def _(side=side, dz=dz):
            zland[side] = jnp.zeros((3, PY, 128), F32)
            zmid[side] = jnp.zeros((3, 24, 128), F32)
            bf[1 + dz] = jnp.zeros((gy, gx, 8, 128), F32)

    r_i, c_i = iota((128, 128), 0), iota((128, 128), 1)
    pool = jnp.where(r_i // 2 == c_i, 0.5, 0.0).astype(F32)
    pool_halo = jnp.where(
        ((r_i < 2) & (c_i == 64)) | ((r_i >= 126) & (c_i == 127)), 0.5, 0.0
    ).astype(F32)
    copy_mid = jnp.where((c_i // 2 == r_i), 1.0, 0.0).astype(F32)
    copy_coarse = jnp.where((c_i // 8 == r_i), 1.0, 0.0).astype(F32)
    z_of = jnp.where(r_i < 64, r_i // 4 + 1, jnp.where(r_i < 68, 17, jnp.where(r_i >= 124, 0, 99)))
    gather_f = jnp.where((c_i % 20 == z_of) & (c_i < 120), 0.25, 0.0).astype(F32)
    gather_c = jnp.where((r_i // 4 == c_i % 16) & (r_i < 64), 0.25, 0.0).astype(F32)

    def dot(a, b):
        b = b.astype(jnp.bfloat16)
        total = None
        for i in range(3):
            part = a.astype(jnp.bfloat16)
            term = jnp.dot(part, b, preferred_element_type=F32)
            total = term if total is None else total + term
            a = a - part.astype(F32)
        return total

    for copy in own:
        copy.wait()

    lane = iota((NY, 128), 1)
    head = jnp.zeros((NY, 128), F32)
    tail = jnp.zeros((NY, 128), F32)
    for p in range(NX):
        g = mm[0, 3 + p, 0:NY, 0:NZ]
        f = mm[1, 3 + p, 0:NY, 0:NZ]
        s = mm[2, 3 + p, 0:NY, 0:NZ]

        def put(acc, v, to, at, count):
            first = 8 * p + to
            return jnp.where((lane >= first) & (lane < first + count), pltpu.roll(v, (first - at) % 128, 1), acc)

        head = put(head, g, 0, 0, 3)
        head = put(head, f, 3, 0, 2)
        head = put(head, s, 5, 0, 2)
        tail = put(tail, g, 5, 125, 3)
        tail = put(tail, f, 3, 126, 2)
        tail = put(tail, s, 1, 126, 2)
    packs[0] = head
    packs[1] = tail

    pl.semaphore_wait(barrier, len(heard) - 18 + 9 * sides)

    fine_copies = []
    given = (guess, rhs, scr)

    def describe(o, refs, sems, i):
        src, dst = refs()
        return pltpu.make_async_remote_copy(
            src_ref=src,
            dst_ref=dst,
            send_sem=sems[0].at[i],
            recv_sem=sems[1].at[i],
            device_id=device(o),
            device_id_type=MESH,
        )

    def send_fine(o, refs):
        fine_copies.append((o, refs, (fs, fr), len(fine_copies)))
        describe(*fine_copies[-1]).start()

    def finish(copies, sending):
        def one(copy):
            describe(*copy).wait_send() if sending else describe(*copy).wait_recv()

        for copy in copies:
            if copy[0][2] == 0:
                one(copy)
        for dz in (1, -1):

            @pl.when(has(dz if sending else -dz))
            def _(dz=dz):
                for copy in copies:
                    if copy[0][2] == dz:
                        one(copy)

    def x_part(d, depth):
        if d == 0:
            return (3, NX), (3, NX)
        return ((3 + NX - depth, depth), (3 - depth, depth)) if d == 1 else ((3, depth), (3 + NX, depth))

    def y_part(d, depth):
        if d == 0:
            return (0, NY), (0, NY)
        return ((NY - depth, depth), (PY - depth, depth)) if d == 1 else ((0, depth), (NY, depth))

    for o in ((1, 0, 0), (-1, 0, 0)):
        for a, depth in ((0, 3), (1, 2), (2, 2)):
            (p0, n), (q0, _) = x_part(o[0], depth)
            send_fine(
                o,
                lambda a=a, p0=p0, n=n, q0=q0: (
                    given[a].at[pl.ds(p0 - 3, n)],
                    mm.at[a, pl.ds(q0, n), pl.ds(0, NY), pl.ds(0, NZ)],
                ),
            )
    for o in NEIGHBOURS:
        dx, dy, dz = o
        if dz == 0 and dx != 0 and dy != 0:
            (s0, sn), (t0, _) = y_part(dy, 3)
            (p0, n), (q0, _) = x_part(dx, 3)
            for a in range(3):
                send_fine(
                    o,
                    lambda a=a, p0=p0, n=n, q0=q0, s0=s0, sn=sn, t0=t0: (
                        given[a].at[pl.ds(p0 - 3, n), pl.ds(s0, sn), :],
                        mm.at[a, pl.ds(q0, n), pl.ds(t0, sn), pl.ds(0, NZ)],
                    ),
                )

    for o in NEIGHBOURS:
        dx, dy, dz = o
        if dz == 0 and dx == 0:
            (s0, sn), (t0, _) = y_part(dy, 3)
            (p0, n), (q0, _) = x_part(dx, 3)
            for a in range(3):
                send_fine(
                    o,
                    lambda a=a, p0=p0, n=n, q0=q0, s0=s0, sn=sn, t0=t0: (
                        given[a].at[pl.ds(p0 - 3, n), pl.ds(s0, sn), :],
                        mm.at[a, pl.ds(q0, n), pl.ds(t0, sn), pl.ds(0, NZ)],
                    ),
                )

    def send_pack(o):
        dx, dy, dz = o
        (s0, sn), (t0, _) = y_part(dy, 3)
        side = 1 if dz == 1 else 0
        send_fine(
            o, lambda: (packs.at[side, pl.ds(s0, sn), :], zland.at[side, 1 - dx, pl.ds(t0, sn), :])
        )

    by_side([o for o in sorted(NEIGHBOURS, key=lambda o: o[0] != 0) if o[2] != 0], send_pack)

    for q in range(8):
        rx[q] = mm[2, 3 + 2 * q, 0:NY, 0:NZ] + mm[2, 4 + 2 * q, 0:NY, 0:NZ]
    s1_own = dot((rx[:, pl.ds(0, 16, 2), :] + rx[:, pl.ds(1, 16, 2), :]).reshape(128, 128), pool).reshape(8, 16, 128)
    lanes16 = iota((16, 128), 1)
    rows16 = iota((16, 128), 0)
    s4 = [s1_own[4 * i] + s1_own[4 * i + 1] + s1_own[4 * i + 2] + s1_own[4 * i + 3] for i in range(2)]
    s4 = dot(jnp.concatenate(s4, axis=0), gather_c)
    s4 = [jnp.where(lanes16 // 16 == rows16 // 4 + 4 * i, s4[16 * i : 16 * i + 16], 0.0) for i in range(2)]
    c3 = OMEGA / (CENTER + jnp.sum(s4[0] + s4[1], axis=0, keepdims=True))
    for k in range(3):
        msg[k, 4:5, :] = c3 if k == 0 else pltpu.roll(c3, 16 * k, 1)

    finish([c for c in fine_copies if c[0][0] == 0], False)

    rows_in = iota((PY, 128), 0)
    lane40 = iota((PY, 128), 1)
    row_ok = ((rows_in < 36) | (iy > 0)) & ((rows_in < NY) | (rows_in >= 36) | (iy < gy - 1))
    col_ok = ((lane40 < 64) & (iz < gz - 1)) | ((lane40 >= 64) & (iz > 0))
    both_ok = row_ok & col_ok
    def columns(p):
        if p < 3:
            xs, q, x_ok = 0, NX - 3 + p, ix > 0
        elif p < 3 + NX:
            xs, q, x_ok = 1, p - 3, None
        else:
            xs, q, x_ok = 2, p - 3 - NX, ix < gx - 1
        h = zland[0, xs]
        t = zland[1, xs]
        ok0 = row_ok if x_ok is None else row_ok & x_ok
        ok1 = both_ok if x_ok is None else both_ok & x_ok
        g1 = jnp.where(
            lane40 < 64, pltpu.roll(h, (-8 * q) % 128, 1), pltpu.roll(t, (-8 * q - 8) % 128, 1)
        )
        mm[0, p, :, NZ:PZ] = jnp.where(ok1, g1, 0.0)
        if x_ok is None:
            mm[0, p, NY:PY, 0:NZ] = jnp.where(ok0[NY:PY], mm[0, p, NY:PY, 0:NZ], 0.0)
        else:
            mm[0, p, :, 0:NZ] = jnp.where(ok0, mm[0, p, :, 0:NZ], 0.0)
        if 0 < p < PX - 1:
            f1 = jnp.where(lane40 < 64, pltpu.roll(h, (-8 * q - 3) % 128, 1), pltpu.roll(t, (-8 * q - 5) % 128, 1))
            s1 = jnp.where(lane40 < 64, pltpu.roll(h, (-8 * q - 5) % 128, 1), pltpu.roll(t, (-8 * q - 3) % 128, 1))
            s1 = jnp.where((lane40 < 2) | (lane40 >= 126), s1, 0.0)
            mm[1, p, :, NZ:PZ] = f1
            mm[2, p, :, NZ:PZ] = s1
            cc[p, :, 0:NZ] = jnp.where(ok0, OMEGA / (CENTER + mm[2, p, :, 0:NZ]), 0.0)
            cc[p, :, NZ:PZ] = jnp.where(ok1, OMEGA / (CENTER + s1), 0.0)

    for p in range(3, 3 + NX):
        columns(p)

    def update(src, dst, p, b0, b1, b2):
        v = src[p]
        t = b0 + b1 + b1 + b2
        dst[p] = 0.2 * v + cc[p] * (mm[1, p] + 0.25 * t - 2.0 * v)

    def inner(src, dst, first, last):
        def body(p, carry):
            b0, b1 = carry
            b2 = plane_sum(src[p + 1])
            update(src, dst, p, b0, b1, b2)
            return b1, b2

        b0, b1 = plane_sum(src[first - 1]), plane_sum(src[first])
        b2, b3 = b0, b1
        for p in range(first, last):
            b2, b3 = body(p, (b2, b3))
        return {first - 1: b0, first: b1, last - 1: b2, last: b3}

    def outer(src, dst, planes, sums):
        for p in planes:
            for i in (p - 1, p, p + 1):
                if i not in sums:
                    sums[i] = plane_sum(src[i])
            update(src, dst, p, sums[p - 1], sums[p], sums[p + 1])

    def own_sum(p):
        return plane_sum(vb[p])[0:NY, 0:NZ]

    def residual(p, b0, b1, b2):
        t = b0 + b1 + b1 + b2
        v = vb[p, 0:NY, 0:NZ]
        return mm[1, p, 0:NY, 0:NZ] - (CENTER + 2.0 + mm[2, p, 0:NY, 0:NZ]) * v + 0.25 * t

    def pair(q, carry):
        b0, b1 = carry
        b2 = own_sum(4 + 2 * q)
        b3 = own_sum(5 + 2 * q)
        rx[q] = residual(3 + 2 * q, b0, b1, b2) + residual(4 + 2 * q, b1, b2, b3)
        return b2, b3

    first_sums = inner(mm.at[0], va, 4, 18)
    second_sums = inner(va, vb, 5, 17)
    third_sums = {6: own_sum(6), 7: own_sum(7)}
    sums = third_sums[6], third_sums[7]
    for q in range(2, 6):
        sums = pair(q, sums)
    third_sums[14], third_sums[15] = sums

    row24, lane24 = iota((24, 128), 0), iota((24, 128), 1)
    ok24 = (
        ((row24 < 20) | (iy > 0))
        & ((row24 < 16) | (row24 >= 20) | (iy < gy - 1))
        & ((lane24 < 96) | (iz > 0))
        & ((lane24 < 64) | (lane24 >= 96) | (iz < gz - 1))
    )

    def mid_screen(planes):
        for q in planes:
            sx[0, q] = mm[2, 1 + 2 * q, :, 0:NZ] + mm[2, 2 + 2 * q, :, 0:NZ]
            sx[1, q] = mm[2, 1 + 2 * q, :, NZ:PZ] + mm[2, 2 + 2 * q, :, NZ:PZ]
            for half in range(2):
                v = sx[half, q, pl.ds(0, 20, 2), :] + sx[half, q, pl.ds(1, 20, 2), :]
                s24[half, q, 0:20, :] = v
                s24[half, q, 23:24, :] = v[19:20, :]
        a = [jnp.concatenate([s24[half, q] for q in planes], axis=0) for half in range(2)]
        s1 = dot(a[0], pool) + dot(a[1], pool_halo)
        for i, q in enumerate(planes):
            ok = ok24 & (ix > 0) if q == 0 else (ok24 & (ix < gx - 1) if q == 9 else ok24)
            s1r[q] = s1[24 * i : 24 * i + 24]
            c1r[q] = jnp.where(ok, OMEGA / (CENTER + s1[24 * i : 24 * i + 24]), 0.0)

    mid_screen(tuple(range(1, 9)))

    finish([c for c in fine_copies if c[0][0] != 0], False)

    for p in (0, 1, 2, 19, 20, 21):
        columns(p)
    outer(mm.at[0], va, (3, 2, 1, 18, 19, 20), first_sums)
    outer(va, vb, (4, 3, 2, 17, 18, 19), second_sums)
    for q in (1, 0, 6, 7):
        for i in range(2 + 2 * q, 6 + 2 * q):
            if i not in third_sums:
                third_sums[i] = own_sum(i)
        b = [third_sums[i] for i in range(2 + 2 * q, 6 + 2 * q)]
        rx[q] = residual(3 + 2 * q, *b[:3]) + residual(4 + 2 * q, *b[1:])

    mid_screen((0, 9))

    f1 = dot((rx[:, pl.ds(0, 16, 2), :] + rx[:, pl.ds(1, 16, 2), :]).reshape(128, 128), pool).reshape(8, 16, 128)

    zero8 = jnp.zeros((8, 128), F32)
    f1z = [jnp.concatenate([f1[q], zero8], axis=0) for q in range(8)]
    e_own = [c1r[q + 1] * f1z[q] for q in range(8)]
    for q in range(8):
        ex[q + 1, 0:16, :] = e_own[q][0:16]

    def weigh(b, p):
        terms = [b[i] * w for i, w in ((p - 1, 1.0), (p, 2.0), (p + 1, 1.0)) if i in b]
        return 0.25 * functools.reduce(lambda m, n: m + n, terms)

    sums = {q: plane_sum(e_own[q]) for q in range(8)}
    e_two = {}
    for q in range(-1, 9):
        t = weigh(sums, q)
        if 0 <= q < 8:
            e_two[q] = 0.2 * e_own[q] + c1r[q + 1] * (f1z[q] + t - 2.0 * e_own[q])
        else:
            e_two[q] = c1r[q + 1] * t
    sums = {q: plane_sum(e_two[q]) for q in range(-1, 9)}
    parts = {}
    for q in range(-2, 10):
        r = weigh(sums, q)
        if q in e_two:
            r = r - (CENTER + 2.0 + s1r[q + 1]) * e_two[q]
        if 0 <= q < 8:
            r = r + f1z[q]
        at = (q + 4) // 4
        parts[at] = parts[at] + r if at in parts else r
    y_of = jnp.where(row24 < 16, row24 // 4 + 1, jnp.where(row24 < 18, 5, jnp.where(row24 >= 22, 0, 99)))
    z_at = lane24 % 20
    keep = (lane24 // 20 == y_of) & ((z_at != 0) | (iz > 0)) & ((z_at != 17) | (iz < gz - 1))
    stacked = dot(jnp.concatenate([parts[i] for i in range(4)], axis=0), gather_f)
    for i in range(4):
        row = jnp.sum(jnp.where(keep, stacked[24 * i : 24 * i + 24], 0.0), axis=0, keepdims=True)
        for k in range(3):
            msg[k, i : i + 1, :] = row if k == 0 else pltpu.roll(row, 16 * k, 1)

    slot = bf.at[:, iy, ix, pl.ds(0, 5), :]
    def send_parts(to):
        def one(o):
            pltpu.make_async_remote_copy(
                src_ref=msg.at[1 - o[2]],
                dst_ref=slot.at[1 - o[2]],
                send_sem=gsem.at[1 + o[2]],
                recv_sem=gsem.at[4 - o[2]],
                device_id=device(o),
                device_id_type=MESH,
            ).start()

        by_side(to, one)

    send_parts([o for o in peers if hops(o) > 2])
    pltpu.make_async_copy(msg.at[1], slot.at[1], gsem.at[4]).start()

    ztail = jnp.zeros((16, 128), F32)
    for q in range(8):
        ztail = jnp.where(lanes16 == q, pltpu.roll(e_own[q][0:16], (q - 63) % 128, 1), ztail)
        ztail = jnp.where(lanes16 == 64 + q, pltpu.roll(e_own[q][0:16], 64 + q, 1), ztail)
    zpack[...] = ztail
    mid_copies = []

    def send_mid(o):
        dx, dy, dz = o
        (s0, sn), t0 = ((0, 16), 0) if dy == 0 else (((15, 1), 23) if dy == 1 else ((0, 1), 16))
        if dz == 0:
            (p0, n), q0 = ((1, 8), 1) if dx == 0 else (((8, 1), 0) if dx == 1 else ((1, 1), 9))

            def refs():
                return ex.at[pl.ds(p0, n), pl.ds(s0, sn), :], ex.at[pl.ds(q0, n), pl.ds(t0, sn), :]

        else:
            side = 1 if dz == 1 else 0

            def refs():
                return zpack.at[pl.ds(s0, sn), :], zmid.at[side, 1 - dx, pl.ds(t0, sn), :]

        mid_copies.append((o, refs, (ms, mr), len(mid_copies)))
        describe(*mid_copies[-1]).start()

    by_side(NEIGHBOURS, send_mid)

    send_parts([o for o in peers if hops(o) <= 2])

    finish(mid_copies, False)
    mid_sums = {}
    for p in range(10):
        if p == 0:
            xs, q, x_ok = 0, 7, ix > 0
        elif p < 9:
            xs, q, x_ok = 1, p - 1, None
        else:
            xs, q, x_ok = 2, 0, ix < gx - 1
        v = ex[p]
        v = jnp.where(lane24 == 64, pltpu.roll(zmid[0, xs], (-q) % 128, 1), v)
        v = jnp.where(lane24 == 127, pltpu.roll(zmid[1, xs], (127 - q) % 128, 1), v)
        ok = ok24 if x_ok is None else ok24 & x_ok
        mid_sums[p] = plane_sum(jnp.where(ok, v, 0.0))
    e1 = []
    for q in range(8):
        t = weigh(mid_sums, q + 1)[0:16]
        e = e_own[q][0:16]
        e1.append(0.2 * e + c1r[q + 1, 0:16] * (f1[q] + t - 2.0 * e))
    e1 = dot(jnp.concatenate(e1, axis=0), copy_mid).reshape(8, 16, 128)
    e1f[:, pl.ds(0, 16, 2), :] = e1
    e1f[:, pl.ds(1, 16, 2), :] = e1
    for p in range(NX):
        base[p] = vb[3 + p, 0:NY, 0:NZ] + e1f[p // 2]

    def wait_parts(k):
        landed = bf.at[k, :, :, pl.ds(0, 5), :]
        pltpu.make_async_copy(landed, landed, gsem.at[3 + k]).wait()

    wait_parts(1)
    for k in (0, 2):
        pl.when(has(k - 1))(functools.partial(wait_parts, k))

    lane8, row8 = iota((8, 128), 1), iota((8, 128), 0)
    block = (lane8 // 16) % 4
    z_ok = (block < 3) & ((block > 0) | (iz > 0)) & ((block < 2) | (iz < gz - 1))
    low = lane8 < 64
    total, screens = {}, {}
    for j in range(gy):
        v, c = [], []
        for k in range(3):
            f = w = None
            for i in range(gx):
                tile = bf[k, j, i]
                at = row8 - (2 * i - 1)
                part = jnp.where((at >= 0) & (at < 4), pltpu.roll(tile, (2 * i - 1) % 8, 0), 0.0)
                f = part if f is None else f + part
                row = jnp.broadcast_to(tile[4:5], (8, 128))
                w = row if w is None else jnp.where(row8 < 2 * i, w, row)
            v.append(f)
            c.append(jnp.where(row8 % 2 == 0, w, pltpu.roll(w, 64, 1)))
        for yy in range(4):
            d = (lane8 // 16 - yy + 8) % 8
            w = jnp.where(d == 0, c[0], jnp.where(d == 1, c[1], c[2]))
            y = 4 * j + yy
            shift = (64 * (y // 16) - 16 * yy) % 128
            screens[y] = pltpu.roll(w, shift, 1) if shift else w
        for yy in range(6):
            y = 4 * j + yy - 1
            if not 0 <= y < 32:
                continue
            w = None
            for k in range(3):
                at = (lane8 - (20 * yy + 16 * k) + 256) % 128
                part = jnp.where(at < 18, v[k], 0.0)
                w = part if w is None else w + part
            w = pltpu.roll(w, (64 * (y // 16) - 20 * yy - 1) % 128, 1)
            total[y] = total[y] + w if y in total else w
    for m in range(16):
        cof[m] = jnp.where(z_ok, jnp.where(low, total[m], total[m + 16]), 0.0)
        coc[m] = jnp.where(z_ok, jnp.where(low, screens[m], screens[m + 16]), 0.0)
        cov[m] = coc[m] * cof[m]

    def coarse(i, v):
        wrap_up = jnp.where(low, 0.0, pltpu.roll(v[15], 64, 1))
        wrap_down = jnp.where(low, pltpu.roll(v[0], 64, 1), 0.0)
        new = []
        for m in range(16):
            up = v[m - 1] if m else wrap_up
            down = v[m + 1] if m < 15 else wrap_down
            a = up + down + 2.0 * v[m]
            b = 2.0 * a + jnp.where(row8 == 0, 0.0, pltpu.roll(a, 1, 0)) + jnp.where(row8 == 7, 0.0, pltpu.roll(a, 7, 0))
            t = 2.0 * b + pltpu.roll(b, 1, 1) + pltpu.roll(b, 127, 1)
            new.append(0.2 * v[m] + coc[m] * (cof[m] + 0.25 * t - 2.0 * v[m]))
        return tuple(new)

    v = lax.fori_loop(0, ITERS - 1, coarse, tuple(cov[m] for m in range(16)))
    for m in range(16):
        cov[m] = v[m]

    mine = cov[pl.ds(4 * lax.rem(iy, 4), 4)]
    mine = mine.reshape(32, 128)
    mine = jnp.where(iy < 4, pltpu.roll(mine, 112, 1), pltpu.roll(mine, 48, 1))
    eout[...] = dot(mine, copy_coarse).reshape(4, 8, 128)
    for xc in range(2):
        for t in range(4):
            e3 = jnp.broadcast_to(eout[t, pl.ds(2 * ix + xc, 1), :], (8, 128))
            for p in range(8 * xc, 8 * xc + 8):
                rows = slice(8 * t, 8 * t + 8)
                out[p, rows, :] = base[p, rows, :] + e3

    finish(fine_copies + mid_copies, True)

    def wait_sent(dz):
        sent = dummy.at[pl.ds(0, gx * gy - (dz == 0)), pl.ds(0, 5), :]
        pltpu.make_async_copy(sent, sent, gsem.at[1 + dz]).wait()

    wait_sent(0)
    for dz in (1, -1):
        pl.when(has(dz))(functools.partial(wait_sent, dz))


def on_device(sizes, guess, right_side, screen):
    vm = pltpu.VMEM
    return pl.pallas_call(
        functools.partial(kernel, sizes),
        out_shape=jax.ShapeDtypeStruct((NX, NY, NZ), F32),
        in_specs=[pl.BlockSpec(memory_space=pltpu.HBM)] * 3,
        out_specs=pl.BlockSpec(memory_space=pltpu.VMEM),
        scratch_shapes=[
            vm((3, PX, PY, PZ), F32),
            vm((PX, PY, PZ), F32),
            vm((PX, PY, PZ), F32),
            vm((PX, PY, PZ), F32),
            vm((2, NY, 128), F32),
            vm((2, 3, PY, 128), F32),
            vm((8, NY, 128), F32),
            vm((2, 10, PY, 128), F32),
            vm((2, 10, 24, 128), F32),
            vm((10, 24, 128), F32),
            vm((10, 24, 128), F32),
            vm((10, 24, 128), F32),
            vm((16, 128), F32),
            vm((2, 3, 24, 128), F32),
            vm((8, NY, 128), F32),
            vm((NX, NY, NZ), F32),
            vm((3, 5, 128), F32),
            vm((3, sizes[1], sizes[0], 8, 128), F32),
            vm((16, 8, 128), F32),
            vm((16, 8, 128), F32),
            vm((16, 8, 128), F32),
            vm((4, 8, 128), F32),
            vm((sizes[0] * sizes[1], 8, 128), F32),
            pltpu.SemaphoreType.DMA((3,)),
            pltpu.SemaphoreType.DMA((42,)),
            pltpu.SemaphoreType.DMA((42,)),
            pltpu.SemaphoreType.DMA((26,)),
            pltpu.SemaphoreType.DMA((26,)),
            pltpu.SemaphoreType.DMA((6,)),
        ],
        compiler_params=pltpu.CompilerParams(
            collective_id=0, has_side_effects=True, vmem_limit_bytes=60 * 1024 * 1024
        ),
        name="multigrid",
    )(guess, right_side, screen)


def solution(mesh):
    placed = P("gx", "gy", "gz")
    sizes = tuple(mesh.shape[a] for a in ("gx", "gy", "gz"))
    return jax.shard_map(
        functools.partial(on_device, sizes), mesh=mesh, in_specs=(placed,) * 3, out_specs=placed, check_vma=False
    )
```

```python
import functools
import itertools

import jax
import jax.numpy as jnp
from jax import lax
from jax.experimental import pallas as pl
from jax.experimental.pallas import tpu as pltpu
from jax.sharding import PartitionSpec as P

ITERS = 16
OMEGA = 0.8
CENTER = 14.0
F32 = jnp.float32
MESH = pl.DeviceIdType.MESH

NX, NY, NZ = 16, 32, 128
PX, PY, PZ = 22, 40, 256
NEIGHBOURS = sorted(
    (o for o in itertools.product((-1, 0, 1), repeat=3) if o != (0, 0, 0)),
    key=lambda o: (-sum(abs(v) for v in o)),
)


def iota(shape, dim):
    return lax.broadcasted_iota(jnp.int32, shape, dim)


def mod(v, n):
    return lax.rem(v + n, n)


def plane_sum(v):
    rows, cols = v.shape
    a = v + v + pltpu.roll(v, 1, 1) + pltpu.roll(v, cols - 1, 1)
    return a + a + pltpu.roll(a, 1, 0) + pltpu.roll(a, rows - 1, 0)


def kernel(
    sizes,
    guess,
    rhs,
    scr,
    out,
    mm,
    cc,
    va,
    vb,
    packs,
    edges,
    zland,
    eland,
    rx,
    sx,
    s24,
    c1r,
    s1r,
    ex,
    zpack,
    zmid,
    e1f,
    base,
    msg,
    bf,
    cof,
    coc,
    cov,
    eout,
    dummy,
    load_sem,
    fs,
    fr,
    ms,
    mr,
    gsem,
):
    gx, gy, gz = sizes
    ix, iy, iz = lax.axis_index("gx"), lax.axis_index("gy"), lax.axis_index("gz")

    def device(o):
        return (
            ix if o[0] == 0 else lax.rem(ix + o[0] % gx, gx),
            iy if o[1] == 0 else lax.rem(iy + o[1] % gy, gy),
            iz if o[2] == 0 else lax.rem(iz + o[2] % gz, gz),
        )

    peers = [
        o
        for o in itertools.product(range(gx), range(gy), (-1, 0, 1))
        if o != (0, 0, 0)
    ]
    peers = [(a - gx if a > gx // 2 else a, b - gy if b > gy // 2 else b, c) for a, b, c in peers]

    def hops(o):
        return abs(o[0]) + (abs(o[1]) + 1) // 2 + abs(o[2])

    peers.sort(key=lambda o: -hops(o))

    def has(dz):
        return iz < gz - 1 if dz == 1 else iz > 0

    def by_side(offsets, act):
        for o in offsets:
            if o[2] == 0:
                act(o)
        for dz in (1, -1):

            @pl.when(has(dz))
            def _(dz=dz):
                for o in offsets:
                    if o[2] == dz:
                        act(o)

    heard = [(1, 3, 0), (1, 2, 0), (1, -2, 0), (0, 3, 0), (0, 2, 0), (0, -2, 0)] + NEIGHBOURS
    barrier = pltpu.get_barrier_semaphore()
    by_side(
        [(-o[0], -o[1], -o[2]) for o in heard],
        lambda o: pl.semaphore_signal(barrier, inc=1, device_id=device(o), device_id_type=MESH),
    )
    sides = (iz > 0).astype(jnp.int32) + (iz < gz - 1).astype(jnp.int32)

    own = []
    for a, ref in ((2, scr), (0, guess), (1, rhs)):
        copy = pltpu.make_async_copy(ref, mm.at[a, pl.ds(3, NX), pl.ds(0, NY), pl.ds(0, NZ)], load_sem.at[a])
        copy.start()
        own.append(copy)
    for a in range(3):
        for p in range(PX):
            depth = 2 if a else 3
            mm[a, p, NY + depth : PY - depth, 0:NZ] = jnp.zeros((PY - NY - 2 * depth, NZ), F32)
    for side in range(2):
        for xs in range(3):
            zland[side, xs, NY + 3 : PY - 3, :] = jnp.zeros((PY - NY - 6, 128), F32)
            zmid[side, xs, 17:23, :] = jnp.zeros((6, 128), F32)
    for q in range(10):
        ex[q, 17:23, :] = jnp.zeros((6, 128), F32)
    s24[...] = jnp.zeros_like(s24)

    for side, dz in ((0, 1), (1, -1)):

        @pl.when(jnp.logical_not(has(dz)))
        def _(side=side, dz=dz):
            zland[side] = jnp.zeros((3, PY, 128), F32)
            eland[side] = jnp.zeros((2, 8, 128), F32)
            zmid[side] = jnp.zeros((3, 24, 128), F32)
            bf[1 + dz] = jnp.zeros((gy, gx, 8, 128), F32)

    r_i, c_i = iota((128, 128), 0), iota((128, 128), 1)
    pool = jnp.where(r_i // 2 == c_i, 0.5, 0.0).astype(F32)
    pool_halo = jnp.where(
        ((r_i < 2) & (c_i == 64)) | ((r_i >= 126) & (c_i == 127)), 0.5, 0.0
    ).astype(F32)
    copy_mid = jnp.where((c_i // 2 == r_i), 1.0, 0.0).astype(F32)
    copy_coarse = jnp.where((c_i // 8 == r_i), 1.0, 0.0).astype(F32)
    z_of = jnp.where(r_i < 64, r_i // 4 + 1, jnp.where(r_i < 68, 17, jnp.where(r_i >= 124, 0, 99)))
    gather_f = jnp.where((c_i % 20 == z_of) & (c_i < 120), 0.25, 0.0).astype(F32)
    gather_c = jnp.where((r_i // 4 == c_i % 16) & (r_i < 64), 0.25, 0.0).astype(F32)

    def dot(a, b):
        b = b.astype(jnp.bfloat16)
        total = None
        for i in range(3):
            part = a.astype(jnp.bfloat16)
            term = jnp.dot(part, b, preferred_element_type=F32)
            total = term if total is None else total + term
            a = a - part.astype(F32)
        return total

    pl.semaphore_wait(barrier, len(heard) - 18 + 9 * sides)

    fine_copies = []
    given = (guess, rhs, scr)

    def describe(o, refs, sems, i):
        src, dst = refs()
        return pltpu.make_async_remote_copy(
            src_ref=src,
            dst_ref=dst,
            send_sem=sems[0].at[i],
            recv_sem=sems[1].at[i],
            device_id=device(o),
            device_id_type=MESH,
        )

    def send_fine(o, refs):
        fine_copies.append((o, refs, (fs, fr), len(fine_copies)))
        describe(*fine_copies[-1]).start()

    def finish(copies, sending):
        def one(copy):
            describe(*copy).wait_send() if sending else describe(*copy).wait_recv()

        for copy in copies:
            if copy[0][2] == 0:
                one(copy)
        for dz in (1, -1):

            @pl.when(has(dz if sending else -dz))
            def _(dz=dz):
                for copy in copies:
                    if copy[0][2] == dz:
                        one(copy)

    def x_part(d, depth):
        if d == 0:
            return (3, NX), (3, NX)
        return ((3 + NX - depth, depth), (3 - depth, depth)) if d == 1 else ((3, depth), (3 + NX, depth))

    def y_part(d, depth):
        if d == 0:
            return (0, NY), (0, NY)
        return ((NY - depth, depth), (PY - depth, depth)) if d == 1 else ((0, depth), (NY, depth))

    def send_rows(o):
        for a, depth in ((0, 3), (1, 2), (2, 2)):
            (p0, n), (q0, _) = x_part(o[0], depth)
            (s0, sn), (t0, _) = y_part(o[1], depth)
            send_fine(
                o,
                lambda a=a, p0=p0, n=n, q0=q0, s0=s0, sn=sn, t0=t0: (
                    given[a].at[pl.ds(p0 - 3, n), pl.ds(s0, sn), :],
                    mm.at[a, pl.ds(q0, n), pl.ds(t0, sn), pl.ds(0, NZ)],
                ),
            )

    for o in ((0, 1, 0), (0, -1, 0), (1, 1, 0), (1, -1, 0), (-1, 1, 0), (-1, -1, 0), (1, 0, 0), (-1, 0, 0)):
        send_rows(o)

    for copy in own:
        copy.wait()

    lane = iota((NY, 128), 1)
    head = jnp.zeros((NY, 128), F32)
    tail = jnp.zeros((NY, 128), F32)
    for p in range(NX):
        for a, to, depth in ((0, 0, 3), (1, 3, 2), (2, 5, 2)):
            turned = mm[a, 3 + p, 0:NY, 0:NZ]
            at = 8 * p + to
            turned = pltpu.roll(turned, at, 1) if at else turned
            head = jnp.where((lane >= at) & (lane < at + depth), turned, head)
            behind = (lane >= at - depth) & (lane < at) if at else lane >= 128 - depth
            tail = jnp.where(behind, turned, tail)
    packs[0] = head
    packs[1] = tail
    lane8 = iota((8, 128), 1)
    for side, pack in ((0, head), (1, tail)):
        for e, first in ((0, 0), (1, NX - 3)):
            small = jnp.zeros((8, 128), F32)
            for t in range(4):
                moved = pltpu.roll(pack[8 * t : 8 * t + 8], (32 * t - 8 * first + 8) % 128, 1)
                small = jnp.where(lane8 // 32 == t, moved, small)
            edges[side, e] = small

    def send_pack(o):
        dx, dy, dz = o
        (s0, sn), (t0, _) = y_part(dy, 3)
        side = 1 if dz == 1 else 0
        if dx and not dy:
            send_fine(o, lambda: (edges.at[side, (dx + 1) // 2], eland.at[side, (1 - dx) // 2]))
        else:
            send_fine(o, lambda: (packs.at[side, pl.ds(s0, sn), :], zland.at[side, 1 - dx, pl.ds(t0, sn), :]))

    by_side([o for o in sorted(NEIGHBOURS, key=lambda o: o[0] != 0) if o[2] != 0], send_pack)

    for q in range(8):
        rx[q] = mm[2, 3 + 2 * q, 0:NY, 0:NZ] + mm[2, 4 + 2 * q, 0:NY, 0:NZ]
    s1_own = dot((rx[:, pl.ds(0, 16, 2), :] + rx[:, pl.ds(1, 16, 2), :]).reshape(128, 128), pool).reshape(8, 16, 128)
    lanes16 = iota((16, 128), 1)
    rows16 = iota((16, 128), 0)
    s4 = [s1_own[4 * i] + s1_own[4 * i + 1] + s1_own[4 * i + 2] + s1_own[4 * i + 3] for i in range(2)]
    s4 = dot(jnp.concatenate(s4, axis=0), gather_c)
    s4 = [jnp.where(lanes16 // 16 == rows16 // 4 + 4 * i, s4[16 * i : 16 * i + 16], 0.0) for i in range(2)]
    c3 = OMEGA / (CENTER + jnp.sum(s4[0] + s4[1], axis=0, keepdims=True))
    for k in range(3):
        msg[k, 4:5, :] = c3 if k == 0 else pltpu.roll(c3, 16 * k, 1)

    finish([c for c in fine_copies if c[0][0] == 0], False)

    rows_in = iota((PY, 128), 0)
    lane40 = iota((PY, 128), 1)
    row_ok = ((rows_in < 36) | (iy > 0)) & ((rows_in < NY) | (rows_in >= 36) | (iy < gy - 1))
    col_ok = ((lane40 < 64) & (iz < gz - 1)) | ((lane40 >= 64) & (iz > 0))
    both_ok = row_ok & col_ok
    def turn(v, back):
        return pltpu.roll(v, 128 - back, 1) if back else v

    def columns(p):
        if p < 3:
            xs, q, x_ok = 0, NX - 3 + p, ix > 0
        elif p < 3 + NX:
            xs, q, x_ok = 1, p - 3, None
        else:
            xs, q, x_ok = 2, p - 3 - NX, ix < gx - 1
        h = zland[0, xs]
        t = zland[1, xs]
        ok0 = row_ok if x_ok is None else row_ok & x_ok
        ok1 = both_ok if x_ok is None else both_ok & x_ok
        g1 = turn(jnp.where(lane40 % 8 < 3, h, t), 8 * q)
        mm[0, p, :, NZ:PZ] = jnp.where(ok1, g1, 0.0)
        if x_ok is None:
            mm[0, p, NY:PY, 0:NZ] = jnp.where(ok0[NY:PY], mm[0, p, NY:PY, 0:NZ], 0.0)
        else:
            mm[0, p, :, 0:NZ] = jnp.where(ok0, mm[0, p, :, 0:NZ], 0.0)
        if 0 < p < PX - 1:
            f1 = turn(jnp.where((lane40 % 8 == 3) | (lane40 % 8 == 4), h, t), 8 * q + 3)
            s1 = turn(jnp.where((lane40 % 8 == 5) | (lane40 % 8 == 6), h, t), 8 * q + 5)
            s1 = jnp.where((lane40 < 2) | (lane40 >= 126), s1, 0.0)
            mm[1, p, :, NZ:PZ] = f1
            mm[2, p, :, NZ:PZ] = s1
            cc[p, :, 0:NZ] = jnp.where(ok0, OMEGA / (CENTER + mm[2, p, :, 0:NZ]), 0.0)
            cc[p, :, NZ:PZ] = jnp.where(ok1, OMEGA / (CENTER + s1), 0.0)

    for p in range(3, 3 + NX):
        columns(p)

    def update(src, dst, p, b0, b1, b2):
        v = src[p]
        t = b0 + b1 + b1 + b2
        dst[p] = 0.2 * v + cc[p] * (mm[1, p] + 0.25 * t - 2.0 * v)

    def inner(src, dst, first, last):
        def body(p, carry):
            b0, b1 = carry
            b2 = plane_sum(src[p + 1])
            update(src, dst, p, b0, b1, b2)
            return b1, b2

        b0, b1 = plane_sum(src[first - 1]), plane_sum(src[first])
        b2, b3 = b0, b1
        for p in range(first, last):
            b2, b3 = body(p, (b2, b3))
        return {first - 1: b0, first: b1, last - 1: b2, last: b3}

    def outer(src, dst, planes, sums):
        for p in planes:
            for i in (p - 1, p, p + 1):
                if i not in sums:
                    sums[i] = plane_sum(src[i])
            update(src, dst, p, sums[p - 1], sums[p], sums[p + 1])

    def own_sum(p):
        return plane_sum(vb[p])[0:NY, 0:NZ]

    def residual(p, b0, b1, b2):
        t = b0 + b1 + b1 + b2
        v = vb[p, 0:NY, 0:NZ]
        return mm[1, p, 0:NY, 0:NZ] - (CENTER + 2.0 + mm[2, p, 0:NY, 0:NZ]) * v + 0.25 * t

    def pair(q, carry):
        b0, b1 = carry
        b2 = own_sum(4 + 2 * q)
        b3 = own_sum(5 + 2 * q)
        rx[q] = residual(3 + 2 * q, b0, b1, b2) + residual(4 + 2 * q, b1, b2, b3)
        return b2, b3

    first_sums = inner(mm.at[0], va, 4, 18)
    second_sums = inner(va, vb, 5, 17)
    third_sums = {6: own_sum(6), 7: own_sum(7)}
    sums = third_sums[6], third_sums[7]
    for q in range(2, 6):
        sums = pair(q, sums)
    third_sums[14], third_sums[15] = sums

    row24, lane24 = iota((24, 128), 0), iota((24, 128), 1)
    ok24 = (
        ((row24 < 20) | (iy > 0))
        & ((row24 < 16) | (row24 >= 20) | (iy < gy - 1))
        & ((lane24 < 96) | (iz > 0))
        & ((lane24 < 64) | (lane24 >= 96) | (iz < gz - 1))
    )

    def mid_screen(planes):
        for q in planes:
            sx[0, q] = mm[2, 1 + 2 * q, :, 0:NZ] + mm[2, 2 + 2 * q, :, 0:NZ]
            sx[1, q] = mm[2, 1 + 2 * q, :, NZ:PZ] + mm[2, 2 + 2 * q, :, NZ:PZ]
            for half in range(2):
                v = sx[half, q, pl.ds(0, 20, 2), :] + sx[half, q, pl.ds(1, 20, 2), :]
                s24[half, q, 0:20, :] = v
                s24[half, q, 23:24, :] = v[19:20, :]
        a = [jnp.concatenate([s24[half, q] for q in planes], axis=0) for half in range(2)]
        s1 = dot(a[0], pool) + dot(a[1], pool_halo)
        for i, q in enumerate(planes):
            ok = ok24 & (ix > 0) if q == 0 else (ok24 & (ix < gx - 1) if q == 9 else ok24)
            s1r[q] = s1[24 * i : 24 * i + 24]
            c1r[q] = jnp.where(ok, OMEGA / (CENTER + s1[24 * i : 24 * i + 24]), 0.0)

    mid_screen(tuple(range(1, 9)))

    finish([c for c in fine_copies if c[0][0] != 0], False)

    for side in range(2):
        for e, first in ((0, NX - 3), (1, 0)):
            for t in range(4):
                zland[side, 2 * e, 8 * t : 8 * t + 8, :] = pltpu.roll(eland[side, e], (8 * first - 8 - 32 * t) % 128, 1)
    for p in (0, 1, 2, 19, 20, 21):
        columns(p)
    outer(mm.at[0], va, (3, 2, 1, 18, 19, 20), first_sums)
    outer(va, vb, (4, 3, 2, 17, 18, 19), second_sums)
    for q in (1, 0, 6, 7):
        for i in range(2 + 2 * q, 6 + 2 * q):
            if i not in third_sums:
                third_sums[i] = own_sum(i)
        b = [third_sums[i] for i in range(2 + 2 * q, 6 + 2 * q)]
        rx[q] = residual(3 + 2 * q, *b[:3]) + residual(4 + 2 * q, *b[1:])

    mid_screen((0, 9))

    f1 = dot((rx[:, pl.ds(0, 16, 2), :] + rx[:, pl.ds(1, 16, 2), :]).reshape(128, 128), pool).reshape(8, 16, 128)

    zero8 = jnp.zeros((8, 128), F32)
    f1z = [jnp.concatenate([f1[q], zero8], axis=0) for q in range(8)]
    e_own = [c1r[q + 1] * f1z[q] for q in range(8)]
    for q in range(8):
        ex[q + 1, 0:16, :] = e_own[q][0:16]

    def weigh(b, p):
        terms = [b[i] * w for i, w in ((p - 1, 1.0), (p, 2.0), (p + 1, 1.0)) if i in b]
        return 0.25 * functools.reduce(lambda m, n: m + n, terms)

    sums = {q: plane_sum(e_own[q]) for q in range(8)}
    e_two = {}
    for q in range(-1, 9):
        t = weigh(sums, q)
        if 0 <= q < 8:
            e_two[q] = 0.2 * e_own[q] + c1r[q + 1] * (f1z[q] + t - 2.0 * e_own[q])
        else:
            e_two[q] = c1r[q + 1] * t
    sums = {q: plane_sum(e_two[q]) for q in range(-1, 9)}
    parts = {}
    for q in range(-2, 10):
        r = weigh(sums, q)
        if q in e_two:
            r = r - (CENTER + 2.0 + s1r[q + 1]) * e_two[q]
        if 0 <= q < 8:
            r = r + f1z[q]
        at = (q + 4) // 4
        parts[at] = parts[at] + r if at in parts else r
    y_of = jnp.where(row24 < 16, row24 // 4 + 1, jnp.where(row24 < 18, 5, jnp.where(row24 >= 22, 0, 99)))
    z_at = lane24 % 20
    keep = (lane24 // 20 == y_of) & ((z_at != 0) | (iz > 0)) & ((z_at != 17) | (iz < gz - 1))
    stacked = dot(jnp.concatenate([parts[i] for i in range(4)], axis=0), gather_f)
    for i in range(4):
        row = jnp.sum(jnp.where(keep, stacked[24 * i : 24 * i + 24], 0.0), axis=0, keepdims=True)
        for k in range(3):
            msg[k, i : i + 1, :] = row if k == 0 else pltpu.roll(row, 16 * k, 1)

    slot = bf.at[:, iy, ix, pl.ds(0, 5), :]
    def send_parts(to):
        def one(o):
            pltpu.make_async_remote_copy(
                src_ref=msg.at[1 - o[2]],
                dst_ref=slot.at[1 - o[2]],
                send_sem=gsem.at[1 + o[2]],
                recv_sem=gsem.at[4 - o[2]],
                device_id=device(o),
                device_id_type=MESH,
            ).start()

        by_side(to, one)

    send_parts([o for o in peers if hops(o) > 2])
    pltpu.make_async_copy(msg.at[1], slot.at[1], gsem.at[4]).start()

    ztail = jnp.zeros((16, 128), F32)
    for q in range(8):
        ztail = jnp.where(lanes16 == q, pltpu.roll(e_own[q][0:16], (q - 63) % 128, 1), ztail)
        ztail = jnp.where(lanes16 == 64 + q, pltpu.roll(e_own[q][0:16], 64 + q, 1), ztail)
    zpack[...] = ztail
    mid_copies = []

    def send_mid(o):
        dx, dy, dz = o
        (s0, sn), t0 = ((0, 16), 0) if dy == 0 else (((15, 1), 23) if dy == 1 else ((0, 1), 16))
        if dz == 0:
            (p0, n), q0 = ((1, 8), 1) if dx == 0 else (((8, 1), 0) if dx == 1 else ((1, 1), 9))

            def refs():
                return ex.at[pl.ds(p0, n), pl.ds(s0, sn), :], ex.at[pl.ds(q0, n), pl.ds(t0, sn), :]

        else:
            side = 1 if dz == 1 else 0

            def refs():
                return zpack.at[pl.ds(s0, sn), :], zmid.at[side, 1 - dx, pl.ds(t0, sn), :]

        mid_copies.append((o, refs, (ms, mr), len(mid_copies)))
        describe(*mid_copies[-1]).start()

    by_side(NEIGHBOURS, send_mid)

    send_parts([o for o in peers if hops(o) <= 2])

    finish(mid_copies, False)
    mid_sums = {}
    for p in range(10):
        if p == 0:
            xs, q, x_ok = 0, 7, ix > 0
        elif p < 9:
            xs, q, x_ok = 1, p - 1, None
        else:
            xs, q, x_ok = 2, 0, ix < gx - 1
        v = ex[p]
        v = jnp.where(lane24 == 64, pltpu.roll(zmid[0, xs], (-q) % 128, 1), v)
        v = jnp.where(lane24 == 127, pltpu.roll(zmid[1, xs], (127 - q) % 128, 1), v)
        ok = ok24 if x_ok is None else ok24 & x_ok
        mid_sums[p] = plane_sum(jnp.where(ok, v, 0.0))
    e1 = []
    for q in range(8):
        t = weigh(mid_sums, q + 1)[0:16]
        e = e_own[q][0:16]
        e1.append(0.2 * e + c1r[q + 1, 0:16] * (f1[q] + t - 2.0 * e))
    e1 = dot(jnp.concatenate(e1, axis=0), copy_mid).reshape(8, 16, 128)
    e1f[:, pl.ds(0, 16, 2), :] = e1
    e1f[:, pl.ds(1, 16, 2), :] = e1
    for p in range(NX):
        base[p] = vb[3 + p, 0:NY, 0:NZ] + e1f[p // 2]

    def wait_parts(k):
        landed = bf.at[k, :, :, pl.ds(0, 5), :]
        pltpu.make_async_copy(landed, landed, gsem.at[3 + k]).wait()

    wait_parts(1)
    for k in (0, 2):
        pl.when(has(k - 1))(functools.partial(wait_parts, k))

    row8 = iota((8, 128), 0)
    block = (lane8 // 16) % 4
    z_ok = (block < 3) & ((block > 0) | (iz > 0)) & ((block < 2) | (iz < gz - 1))
    low = lane8 < 64
    total, screens = {}, {}
    for j in range(gy):
        v, c = [], []
        for k in range(3):
            f = w = None
            for i in range(gx):
                tile = bf[k, j, i]
                at = row8 - (2 * i - 1)
                part = jnp.where((at >= 0) & (at < 4), pltpu.roll(tile, (2 * i - 1) % 8, 0), 0.0)
                f = part if f is None else f + part
                row = jnp.broadcast_to(tile[4:5], (8, 128))
                w = row if w is None else jnp.where(row8 < 2 * i, w, row)
            v.append(f)
            c.append(jnp.where(row8 % 2 == 0, w, pltpu.roll(w, 64, 1)))
        for yy in range(4):
            d = (lane8 // 16 - yy + 8) % 8
            w = jnp.where(d == 0, c[0], jnp.where(d == 1, c[1], c[2]))
            y = 4 * j + yy
            shift = (64 * (y // 16) - 16 * yy) % 128
            screens[y] = pltpu.roll(w, shift, 1) if shift else w
        for yy in range(6):
            y = 4 * j + yy - 1
            if not 0 <= y < 32:
                continue
            w = None
            for k in range(3):
                at = (lane8 - (20 * yy + 16 * k) + 256) % 128
                part = jnp.where(at < 18, v[k], 0.0)
                w = part if w is None else w + part
            w = pltpu.roll(w, (64 * (y // 16) - 20 * yy - 1) % 128, 1)
            total[y] = total[y] + w if y in total else w
    for m in range(16):
        cof[m] = jnp.where(z_ok, jnp.where(low, total[m], total[m + 16]), 0.0)
        coc[m] = jnp.where(z_ok, jnp.where(low, screens[m], screens[m + 16]), 0.0)
        cov[m] = coc[m] * cof[m]

    def coarse(i, v):
        twice = [m + m for m in v]
        sums = [twice[m] + pltpu.roll(v[m], 1, 1) + pltpu.roll(v[m], 127, 1) for m in range(16)]

        def other_half(m):
            u = pltpu.roll(v[m], 64, 1)
            return u + u + pltpu.roll(v[m], 65, 1) + pltpu.roll(v[m], 63, 1)

        wrap_up = jnp.where(low, 0.0, other_half(15))
        wrap_down = jnp.where(low, other_half(0), 0.0)
        new = []
        for m in range(16):
            a = (sums[m - 1] if m else wrap_up) + (sums[m + 1] if m < 15 else wrap_down) + (sums[m] + sums[m])
            b = (a + a) + jnp.where(row8 == 0, 0.0, pltpu.roll(a, 1, 0)) + jnp.where(row8 == 7, 0.0, pltpu.roll(a, 7, 0))
            c = coc[m]
            new.append(0.2 * v[m] + c * (cof[m] - twice[m]) + (0.25 * c) * b)
        return tuple(new)

    v = lax.fori_loop(0, ITERS - 1, coarse, tuple(cov[m] for m in range(16)), unroll=3)
    for m in range(16):
        cov[m] = v[m]

    mine = cov[pl.ds(4 * lax.rem(iy, 4), 4)]
    mine = mine.reshape(32, 128)
    mine = jnp.where(iy < 4, pltpu.roll(mine, 112, 1), pltpu.roll(mine, 48, 1))
    eout[...] = dot(mine, copy_coarse).reshape(4, 8, 128)
    for xc in range(2):
        for t in range(4):
            e3 = jnp.broadcast_to(eout[t, pl.ds(2 * ix + xc, 1), :], (8, 128))
            for p in range(8 * xc, 8 * xc + 8):
                rows = slice(8 * t, 8 * t + 8)
                out[p, rows, :] = base[p, rows, :] + e3

    finish(fine_copies + mid_copies, True)

    def wait_sent(dz):
        sent = dummy.at[pl.ds(0, gx * gy - (dz == 0)), pl.ds(0, 5), :]
        pltpu.make_async_copy(sent, sent, gsem.at[1 + dz]).wait()

    wait_sent(0)
    for dz in (1, -1):
        pl.when(has(dz))(functools.partial(wait_sent, dz))


def on_device(sizes, guess, right_side, screen):
    vm = pltpu.VMEM
    return pl.pallas_call(
        functools.partial(kernel, sizes),
        out_shape=jax.ShapeDtypeStruct((NX, NY, NZ), F32),
        in_specs=[pl.BlockSpec(memory_space=pltpu.HBM)] * 3,
        out_specs=pl.BlockSpec(memory_space=pltpu.VMEM),
        scratch_shapes=[
            vm((3, PX, PY, PZ), F32),
            vm((PX, PY, PZ), F32),
            vm((PX, PY, PZ), F32),
            vm((PX, PY, PZ), F32),
            vm((2, NY, 128), F32),
            vm((2, 2, 8, 128), F32),
            vm((2, 3, PY, 128), F32),
            vm((2, 2, 8, 128), F32),
            vm((8, NY, 128), F32),
            vm((2, 10, PY, 128), F32),
            vm((2, 10, 24, 128), F32),
            vm((10, 24, 128), F32),
            vm((10, 24, 128), F32),
            vm((10, 24, 128), F32),
            vm((16, 128), F32),
            vm((2, 3, 24, 128), F32),
            vm((8, NY, 128), F32),
            vm((NX, NY, NZ), F32),
            vm((3, 5, 128), F32),
            vm((3, sizes[1], sizes[0], 8, 128), F32),
            vm((16, 8, 128), F32),
            vm((16, 8, 128), F32),
            vm((16, 8, 128), F32),
            vm((4, 8, 128), F32),
            vm((sizes[0] * sizes[1], 8, 128), F32),
            pltpu.SemaphoreType.DMA((3,)),
            pltpu.SemaphoreType.DMA((42,)),
            pltpu.SemaphoreType.DMA((42,)),
            pltpu.SemaphoreType.DMA((26,)),
            pltpu.SemaphoreType.DMA((26,)),
            pltpu.SemaphoreType.DMA((6,)),
        ],
        compiler_params=pltpu.CompilerParams(
            collective_id=0, has_side_effects=True, vmem_limit_bytes=107 * 512 * 1024
        ),
        name="multigrid",
    )(guess, right_side, screen)


def solution(mesh):
    placed = P("gx", "gy", "gz")
    sizes = tuple(mesh.shape[a] for a in ("gx", "gy", "gz"))
    return jax.shard_map(
        functools.partial(on_device, sizes), mesh=mesh, in_specs=(placed,) * 3, out_specs=placed, check_vma=False
    )
```

```python
import functools
import itertools

import jax
import jax.numpy as jnp
from jax import lax
from jax.experimental import pallas as pl
from jax.experimental.pallas import tpu as pltpu
from jax.sharding import PartitionSpec as P

ITERS = 16
OMEGA = 0.8
CENTER = 14.0
F32 = jnp.float32
MESH = pl.DeviceIdType.MESH

NX, NY, NZ = 16, 32, 128
PX, PY, PZ = 22, 40, 256
NEIGHBOURS = sorted(
    (o for o in itertools.product((-1, 0, 1), repeat=3) if o != (0, 0, 0)),
    key=lambda o: (-sum(abs(v) for v in o)),
)


def iota(shape, dim):
    return lax.broadcasted_iota(jnp.int32, shape, dim)


def plane_sum(v):
    rows, cols = v.shape
    a = v + v + pltpu.roll(v, 1, 1) + pltpu.roll(v, cols - 1, 1)
    return a + a + pltpu.roll(a, 1, 0) + pltpu.roll(a, rows - 1, 0)


def kernel(
    sizes,
    guess,
    rhs,
    scr,
    out,
    mm,
    cc,
    va,
    vb,
    packs,
    edges,
    zland,
    eland,
    rx,
    sx,
    s24,
    c1r,
    s1r,
    ex,
    zpack,
    zmid,
    e1f,
    base,
    msg,
    bf,
    cof,
    coc,
    cov,
    eout,
    dummy,
    load_sem,
    fs,
    fr,
    ms,
    mr,
    gsem,
    ready,
):
    gx, gy, gz = sizes
    ix, iy, iz = lax.axis_index("gx"), lax.axis_index("gy"), lax.axis_index("gz")

    def device(o):
        return (
            ix if o[0] == 0 else lax.rem(ix + o[0] % gx, gx),
            iy if o[1] == 0 else lax.rem(iy + o[1] % gy, gy),
            iz if o[2] == 0 else lax.rem(iz + o[2] % gz, gz),
        )

    peers = [
        o
        for o in itertools.product(range(gx), range(gy), (-1, 0, 1))
        if o != (0, 0, 0)
    ]
    peers = [(a - gx if a > gx // 2 else a, b - gy if b > gy // 2 else b, c) for a, b, c in peers]

    def hops(o):
        return abs(o[0]) + (abs(o[1]) + 1) // 2 + abs(o[2])

    peers.sort(key=lambda o: -hops(o))

    def has(axis, d):
        at, n = ((ix, gx), (iy, gy), (iz, gz))[axis]
        return at < n - d if d > 0 else at >= -d

    def visit(items, act, sign=1):
        def level(items, axis):
            if axis == 3:
                for item in items:
                    act(item)
                return
            for d in sorted({item[0][axis] for item in items}, key=abs):
                some = [item for item in items if item[0][axis] == d]
                if d == 0:
                    level(some, axis + 1)
                else:
                    pl.when(has(axis, sign * d))(functools.partial(level, some, axis + 1))

        level(items, 0)

    def count(axis, d):
        return 1 + has(axis, d).astype(jnp.int32) + has(axis, -d).astype(jnp.int32)

    rows_off = [(a, b, 0) for a in (0, 1, -1) for b in (2, -2)]
    barrier = pltpu.get_barrier_semaphore()

    def signal(semaphore):
        return lambda item: pl.semaphore_signal(semaphore, inc=1, device_id=device(item[0]), device_id_type=MESH)

    visit([(o,) for o in NEIGHBOURS + rows_off], signal(barrier))
    near = count(0, 1) * count(1, 1) * count(2, 1) - 1 + count(0, 1) * (count(1, 2) - 1)

    told = [(a, b, 0) for a in (0, 1, -1) for b in (0, 2, -2) if a or b]

    def tell(step):
        visit([(o,) for o in told], signal(ready.at[step]))

    def hear(step):
        pl.semaphore_wait(ready.at[step], count(0, 1) * count(1, 2) - 1)

    own = []
    for a, ref in ((2, scr), (0, guess), (1, rhs)):
        copy = pltpu.make_async_copy(ref, mm.at[a, pl.ds(3, NX), pl.ds(0, NY), pl.ds(0, NZ)], load_sem.at[a])
        copy.start()
        own.append(copy)
    for a in range(3):
        for p in range(PX):
            depth = 2 if a else 3
            mm[a, p, NY + depth : PY - depth, 0:NZ] = jnp.zeros((PY - NY - 2 * depth, NZ), F32)
    for side in range(2):
        for xs in range(3):
            zland[side, xs, NY + 3 : PY - 3, :] = jnp.zeros((PY - NY - 6, 128), F32)
            zmid[side, xs, 17:23, :] = jnp.zeros((6, 128), F32)
    for q in range(10):
        ex[q, 17:23, :] = jnp.zeros((6, 128), F32)
    s24[...] = jnp.zeros_like(s24)

    def blank(ref, *at):
        ref[at] = jnp.zeros(ref.at[at].shape, F32)

    whole = slice(None)
    for e, d in ((0, -1), (1, 1)):

        @pl.when(jnp.logical_not(has(0, d)))
        def _(e=e):
            planes = slice(3 + NX, PX) if e else slice(0, 3)
            for a in range(3):
                blank(mm, a, planes, whole, slice(0, NZ))
            for side in range(2):
                blank(zland, side, 2 * e)
                blank(eland, side, e)
                blank(zmid, side, 2 * e)
            blank(ex, 9 * e)

        @pl.when(jnp.logical_not(has(1, d)))
        def _(e=e):
            rows = slice(NY, NY + 3) if e else slice(PY - 3, PY)
            row = slice(16, 17) if e else slice(23, 24)
            for a in range(3):
                blank(mm, a, whole, rows, slice(0, NZ))
            for side in range(2):
                blank(zland, side, whole, rows)
                blank(zmid, side, whole, row)
            blank(ex, whole, row)

        @pl.when(jnp.logical_not(has(2, d)))
        def _(e=e, d=d):
            blank(zland, 1 - e)
            blank(eland, 1 - e)
            blank(zmid, 1 - e)
            blank(bf, 1 + d)

    r_i, c_i = iota((128, 128), 0), iota((128, 128), 1)
    pool = jnp.where(r_i // 2 == c_i, 0.5, 0.0).astype(F32)
    pool_halo = jnp.where(
        ((r_i < 2) & (c_i == 64)) | ((r_i >= 126) & (c_i == 127)), 0.5, 0.0
    ).astype(F32)
    copy_mid = jnp.where((c_i // 2 == r_i), 1.0, 0.0).astype(F32)
    copy_coarse = jnp.where((c_i // 8 == r_i), 1.0, 0.0).astype(F32)
    z_of = jnp.where(r_i < 64, r_i // 4 + 1, jnp.where(r_i < 68, 17, jnp.where(r_i >= 124, 0, 99)))
    gather_f = jnp.where((c_i % 20 == z_of) & (c_i < 120), 0.25, 0.0).astype(F32)
    gather_c = jnp.where((r_i // 4 == c_i % 16) & (r_i < 64), 0.25, 0.0).astype(F32)

    def dot(a, b):
        b = b.astype(jnp.bfloat16)
        total = None
        for i in range(3):
            part = a.astype(jnp.bfloat16)
            term = jnp.dot(part, b, preferred_element_type=F32)
            total = term if total is None else total + term
            a = a - part.astype(F32)
        return total

    pl.semaphore_wait(barrier, near)
    tell(0)

    for copy in own:
        copy.wait()

    fine_copies = []
    given = (guess, rhs, scr)

    def describe(o, refs, sems, i):
        src, dst = refs()
        return pltpu.make_async_remote_copy(
            src_ref=src,
            dst_ref=dst,
            send_sem=sems[0].at[i],
            recv_sem=sems[1].at[i],
            device_id=device(o),
            device_id_type=MESH,
        )

    def started(copies, sems):
        def start(copy):
            copies.append(copy + (sems, len(copies)))
            describe(*copies[-1]).start()

        return start

    def finish(copies, sending):
        def one(copy):
            describe(*copy).wait_send() if sending else describe(*copy).wait_recv()

        visit(copies, one, 1 if sending else -1)

    def x_part(d, depth):
        if d == 0:
            return (3, NX), (3, NX)
        return ((3 + NX - depth, depth), (3 - depth, depth)) if d == 1 else ((3, depth), (3 + NX, depth))

    def y_part(d, depth):
        if d == 0:
            return (0, NY), (0, NY)
        return ((NY - depth, depth), (PY - depth, depth)) if d == 1 else ((0, depth), (NY, depth))

    def rows_of(o):
        copies = []
        for a, depth in ((0, 3), (1, 2), (2, 2)):
            (p0, n), (q0, _) = x_part(o[0], depth)
            (s0, sn), (t0, _) = y_part(o[1], depth)

            def refs(a=a, p0=p0, n=n, q0=q0, s0=s0, sn=sn, t0=t0):
                return (
                    mm.at[a, pl.ds(p0, n), pl.ds(s0, sn), pl.ds(0, NZ)],
                    mm.at[a, pl.ds(q0, n), pl.ds(t0, sn), pl.ds(0, NZ)],
                )

            copies.append((o, refs))
        return copies

    visit([c for o in NEIGHBOURS if o[2] == 0 for c in rows_of(o)], started(fine_copies, (fs, fr)))

    lane = iota((NY, 128), 1)
    head = jnp.zeros((NY, 128), F32)
    tail = jnp.zeros((NY, 128), F32)
    for p in range(NX):
        for a, to, depth in ((0, 0, 3), (1, 3, 2), (2, 5, 2)):
            turned = mm[a, 3 + p, 0:NY, 0:NZ]
            at = 8 * p + to
            turned = pltpu.roll(turned, at, 1) if at else turned
            head = jnp.where((lane >= at) & (lane < at + depth), turned, head)
            behind = (lane >= at - depth) & (lane < at) if at else lane >= 128 - depth
            tail = jnp.where(behind, turned, tail)
    packs[0] = head
    packs[1] = tail
    lane8 = iota((8, 128), 1)
    for side, pack in ((0, head), (1, tail)):
        for e, first in ((0, 0), (1, NX - 3)):
            small = jnp.zeros((8, 128), F32)
            for t in range(4):
                moved = pltpu.roll(pack[8 * t : 8 * t + 8], (32 * t - 8 * first + 8) % 128, 1)
                small = jnp.where(lane8 // 32 == t, moved, small)
            edges[side, e] = small

    def pack_of(o):
        dx, dy, dz = o
        (s0, sn), (t0, _) = y_part(dy, 3)
        side = 1 if dz == 1 else 0
        if dx and not dy:
            return o, lambda: (edges.at[side, (dx + 1) // 2], eland.at[side, (1 - dx) // 2])
        return o, lambda: (packs.at[side, pl.ds(s0, sn), :], zland.at[side, 1 - dx, pl.ds(t0, sn), :])

    visit([pack_of(o) for o in NEIGHBOURS if o[2] != 0], started(fine_copies, (fs, fr)))
    hear(0)
    tell(1)

    for q in range(8):
        rx[q] = mm[2, 3 + 2 * q, 0:NY, 0:NZ] + mm[2, 4 + 2 * q, 0:NY, 0:NZ]
    s1_own = dot((rx[:, pl.ds(0, 16, 2), :] + rx[:, pl.ds(1, 16, 2), :]).reshape(128, 128), pool).reshape(8, 16, 128)
    lanes16 = iota((16, 128), 1)
    rows16 = iota((16, 128), 0)
    s4 = [s1_own[4 * i] + s1_own[4 * i + 1] + s1_own[4 * i + 2] + s1_own[4 * i + 3] for i in range(2)]
    s4 = dot(jnp.concatenate(s4, axis=0), gather_c)
    s4 = [jnp.where(lanes16 // 16 == rows16 // 4 + 4 * i, s4[16 * i : 16 * i + 16], 0.0) for i in range(2)]
    c3 = OMEGA / (CENTER + jnp.sum(s4[0] + s4[1], axis=0, keepdims=True))
    for k in range(3):
        msg[k, 4:5, :] = c3 if k == 0 else pltpu.roll(c3, 16 * k, 1)

    finish([c for c in fine_copies if c[0][0] == 0], False)
    hear(1)
    tell(2)

    rows_in = iota((PY, 128), 0)
    lane40 = iota((PY, 128), 1)
    row_ok = ((rows_in < 36) | (iy > 0)) & ((rows_in < NY) | (rows_in >= 36) | (iy < gy - 1))
    col_ok = ((lane40 < 64) & (iz < gz - 1)) | ((lane40 >= 64) & (iz > 0))
    both_ok = row_ok & col_ok
    def turn(v, back):
        return pltpu.roll(v, 128 - back, 1) if back else v

    def columns(p):
        if p < 3:
            xs, q, x_ok = 0, NX - 3 + p, ix > 0
        elif p < 3 + NX:
            xs, q, x_ok = 1, p - 3, None
        else:
            xs, q, x_ok = 2, p - 3 - NX, ix < gx - 1
        h = zland[0, xs]
        t = zland[1, xs]
        ok0 = row_ok if x_ok is None else row_ok & x_ok
        ok1 = both_ok if x_ok is None else both_ok & x_ok
        g1 = turn(jnp.where(lane40 % 8 < 3, h, t), 8 * q)
        mm[0, p, :, NZ:PZ] = jnp.where(ok1, g1, 0.0)
        if x_ok is None:
            mm[0, p, NY:PY, 0:NZ] = jnp.where(ok0[NY:PY], mm[0, p, NY:PY, 0:NZ], 0.0)
        else:
            mm[0, p, :, 0:NZ] = jnp.where(ok0, mm[0, p, :, 0:NZ], 0.0)
        if 0 < p < PX - 1:
            f1 = turn(jnp.where((lane40 % 8 == 3) | (lane40 % 8 == 4), h, t), 8 * q + 3)
            s1 = turn(jnp.where((lane40 % 8 == 5) | (lane40 % 8 == 6), h, t), 8 * q + 5)
            s1 = jnp.where((lane40 < 2) | (lane40 >= 126), s1, 0.0)
            mm[1, p, :, NZ:PZ] = f1
            mm[2, p, :, NZ:PZ] = s1
            cc[p, :, 0:NZ] = jnp.where(ok0, OMEGA / (CENTER + mm[2, p, :, 0:NZ]), 0.0)
            cc[p, :, NZ:PZ] = jnp.where(ok1, OMEGA / (CENTER + s1), 0.0)

    for p in range(3, 3 + NX):
        columns(p)

    def update(src, dst, p, b0, b1, b2):
        v = src[p]
        t = b0 + b1 + b1 + b2
        dst[p] = 0.2 * v + cc[p] * (mm[1, p] + 0.25 * t - 2.0 * v)

    def inner(src, dst, first, last):
        def body(p, carry):
            b0, b1 = carry
            b2 = plane_sum(src[p + 1])
            update(src, dst, p, b0, b1, b2)
            return b1, b2

        b0, b1 = plane_sum(src[first - 1]), plane_sum(src[first])
        b2, b3 = b0, b1
        for p in range(first, last):
            b2, b3 = body(p, (b2, b3))
        return {first - 1: b0, first: b1, last - 1: b2, last: b3}

    def outer(src, dst, planes, sums):
        for p in planes:
            for i in (p - 1, p, p + 1):
                if i not in sums:
                    sums[i] = plane_sum(src[i])
            update(src, dst, p, sums[p - 1], sums[p], sums[p + 1])

    def own_sum(p):
        return plane_sum(vb[p])[0:NY, 0:NZ]

    def residual(p, b0, b1, b2):
        t = b0 + b1 + b1 + b2
        v = vb[p, 0:NY, 0:NZ]
        return mm[1, p, 0:NY, 0:NZ] - (CENTER + 2.0 + mm[2, p, 0:NY, 0:NZ]) * v + 0.25 * t

    def pair(q, carry):
        b0, b1 = carry
        b2 = own_sum(4 + 2 * q)
        b3 = own_sum(5 + 2 * q)
        rx[q] = residual(3 + 2 * q, b0, b1, b2) + residual(4 + 2 * q, b1, b2, b3)
        return b2, b3

    first_sums = inner(mm.at[0], va, 4, 18)
    second_sums = inner(va, vb, 5, 17)
    third_sums = {6: own_sum(6), 7: own_sum(7)}
    sums = third_sums[6], third_sums[7]
    for q in range(2, 6):
        sums = pair(q, sums)
    third_sums[14], third_sums[15] = sums

    row24, lane24 = iota((24, 128), 0), iota((24, 128), 1)
    ok24 = (
        ((row24 < 20) | (iy > 0))
        & ((row24 < 16) | (row24 >= 20) | (iy < gy - 1))
        & ((lane24 < 96) | (iz > 0))
        & ((lane24 < 64) | (lane24 >= 96) | (iz < gz - 1))
    )

    def mid_screen(planes):
        for q in planes:
            sx[0, q] = mm[2, 1 + 2 * q, :, 0:NZ] + mm[2, 2 + 2 * q, :, 0:NZ]
            sx[1, q] = mm[2, 1 + 2 * q, :, NZ:PZ] + mm[2, 2 + 2 * q, :, NZ:PZ]
            for half in range(2):
                v = sx[half, q, pl.ds(0, 20, 2), :] + sx[half, q, pl.ds(1, 20, 2), :]
                s24[half, q, 0:20, :] = v
                s24[half, q, 23:24, :] = v[19:20, :]
        a = [jnp.concatenate([s24[half, q] for q in planes], axis=0) for half in range(2)]
        s1 = dot(a[0], pool) + dot(a[1], pool_halo)
        for i, q in enumerate(planes):
            ok = ok24 & (ix > 0) if q == 0 else (ok24 & (ix < gx - 1) if q == 9 else ok24)
            s1r[q] = s1[24 * i : 24 * i + 24]
            c1r[q] = jnp.where(ok, OMEGA / (CENTER + s1[24 * i : 24 * i + 24]), 0.0)

    mid_screen(tuple(range(1, 9)))

    finish([c for c in fine_copies if c[0][0] != 0], False)
    hear(2)

    for side in range(2):
        for e, first in ((0, NX - 3), (1, 0)):
            for t in range(4):
                zland[side, 2 * e, 8 * t : 8 * t + 8, :] = pltpu.roll(eland[side, e], (8 * first - 8 - 32 * t) % 128, 1)
    for p in (0, 1, 2, 19, 20, 21):
        columns(p)
    outer(mm.at[0], va, (3, 2, 1, 18, 19, 20), first_sums)
    outer(va, vb, (4, 3, 2, 17, 18, 19), second_sums)
    for q in (1, 0, 6, 7):
        for i in range(2 + 2 * q, 6 + 2 * q):
            if i not in third_sums:
                third_sums[i] = own_sum(i)
        b = [third_sums[i] for i in range(2 + 2 * q, 6 + 2 * q)]
        rx[q] = residual(3 + 2 * q, *b[:3]) + residual(4 + 2 * q, *b[1:])

    mid_screen((0, 9))

    f1 = dot((rx[:, pl.ds(0, 16, 2), :] + rx[:, pl.ds(1, 16, 2), :]).reshape(128, 128), pool).reshape(8, 16, 128)

    zero8 = jnp.zeros((8, 128), F32)
    f1z = [jnp.concatenate([f1[q], zero8], axis=0) for q in range(8)]
    e_own = [c1r[q + 1] * f1z[q] for q in range(8)]
    for q in range(8):
        ex[q + 1, 0:16, :] = e_own[q][0:16]

    def weigh(b, p):
        terms = [b[i] * w for i, w in ((p - 1, 1.0), (p, 2.0), (p + 1, 1.0)) if i in b]
        return 0.25 * functools.reduce(lambda m, n: m + n, terms)

    sums = {q: plane_sum(e_own[q]) for q in range(8)}
    e_two = {}
    for q in range(-1, 9):
        t = weigh(sums, q)
        if 0 <= q < 8:
            e_two[q] = 0.2 * e_own[q] + c1r[q + 1] * (f1z[q] + t - 2.0 * e_own[q])
        else:
            e_two[q] = c1r[q + 1] * t
    sums = {q: plane_sum(e_two[q]) for q in range(-1, 9)}
    parts = {}
    for q in range(-2, 10):
        r = weigh(sums, q)
        if q in e_two:
            r = r - (CENTER + 2.0 + s1r[q + 1]) * e_two[q]
        if 0 <= q < 8:
            r = r + f1z[q]
        at = (q + 4) // 4
        parts[at] = parts[at] + r if at in parts else r
    y_of = jnp.where(row24 < 16, row24 // 4 + 1, jnp.where(row24 < 18, 5, jnp.where(row24 >= 22, 0, 99)))
    z_at = lane24 % 20
    keep = (lane24 // 20 == y_of) & ((z_at != 0) | (iz > 0)) & ((z_at != 17) | (iz < gz - 1))
    stacked = dot(jnp.concatenate([parts[i] for i in range(4)], axis=0), gather_f)
    for i in range(4):
        row = jnp.sum(jnp.where(keep, stacked[24 * i : 24 * i + 24], 0.0), axis=0, keepdims=True)
        for k in range(3):
            msg[k, i : i + 1, :] = row if k == 0 else pltpu.roll(row, 16 * k, 1)

    slot = bf.at[:, iy, ix, pl.ds(0, 5), :]
    def send_parts(to):
        def one(item):
            o = item[1]
            pltpu.make_async_remote_copy(
                src_ref=msg.at[1 - o[2]],
                dst_ref=slot.at[1 - o[2]],
                send_sem=gsem.at[1 + o[2]],
                recv_sem=gsem.at[4 - o[2]],
                device_id=device(o),
                device_id_type=MESH,
            ).start()

        visit([((0, 0, o[2]), o) for o in to], one)

    send_parts([o for o in peers if hops(o) > 2])
    pltpu.make_async_copy(msg.at[1], slot.at[1], gsem.at[4]).start()

    ztail = jnp.zeros((16, 128), F32)
    for q in range(8):
        ztail = jnp.where(lanes16 == q, pltpu.roll(e_own[q][0:16], (q - 63) % 128, 1), ztail)
        ztail = jnp.where(lanes16 == 64 + q, pltpu.roll(e_own[q][0:16], 64 + q, 1), ztail)
    zpack[...] = ztail
    mid_copies = []

    def mid_of(o):
        dx, dy, dz = o
        (s0, sn), t0 = ((0, 16), 0) if dy == 0 else (((15, 1), 23) if dy == 1 else ((0, 1), 16))
        if dz == 0:
            (p0, n), q0 = ((1, 8), 1) if dx == 0 else (((8, 1), 0) if dx == 1 else ((1, 1), 9))
            return o, lambda: (ex.at[pl.ds(p0, n), pl.ds(s0, sn), :], ex.at[pl.ds(q0, n), pl.ds(t0, sn), :])
        side = 1 if dz == 1 else 0
        return o, lambda: (zpack.at[pl.ds(s0, sn), :], zmid.at[side, 1 - dx, pl.ds(t0, sn), :])

    visit([mid_of(o) for o in NEIGHBOURS], started(mid_copies, (ms, mr)))
    send_parts([o for o in peers if hops(o) <= 2])

    finish(mid_copies, False)
    mid_sums = {}
    for p in range(10):
        if p == 0:
            xs, q, x_ok = 0, 7, ix > 0
        elif p < 9:
            xs, q, x_ok = 1, p - 1, None
        else:
            xs, q, x_ok = 2, 0, ix < gx - 1
        v = ex[p]
        v = jnp.where(lane24 == 64, pltpu.roll(zmid[0, xs], (-q) % 128, 1), v)
        v = jnp.where(lane24 == 127, pltpu.roll(zmid[1, xs], (127 - q) % 128, 1), v)
        ok = ok24 if x_ok is None else ok24 & x_ok
        mid_sums[p] = plane_sum(jnp.where(ok, v, 0.0))
    e1 = []
    for q in range(8):
        t = weigh(mid_sums, q + 1)[0:16]
        e = e_own[q][0:16]
        e1.append(0.2 * e + c1r[q + 1, 0:16] * (f1[q] + t - 2.0 * e))
    e1 = dot(jnp.concatenate(e1, axis=0), copy_mid).reshape(8, 16, 128)
    e1f[:, pl.ds(0, 16, 2), :] = e1
    e1f[:, pl.ds(1, 16, 2), :] = e1
    for p in range(NX):
        base[p] = vb[3 + p, 0:NY, 0:NZ] + e1f[p // 2]

    def wait_parts(k):
        landed = bf.at[k, :, :, pl.ds(0, 5), :]
        pltpu.make_async_copy(landed, landed, gsem.at[3 + k]).wait()

    wait_parts(1)
    for k in (0, 2):
        pl.when(has(2, k - 1))(functools.partial(wait_parts, k))

    row8 = iota((8, 128), 0)
    block = (lane8 // 16) % 4
    z_ok = (block < 3) & ((block > 0) | (iz > 0)) & ((block < 2) | (iz < gz - 1))
    low = lane8 < 64
    total, screens = {}, {}
    for j in range(gy):
        v, c = [], []
        for k in range(3):
            f = w = None
            for i in range(gx):
                tile = bf[k, j, i]
                at = row8 - (2 * i - 1)
                part = jnp.where((at >= 0) & (at < 4), pltpu.roll(tile, (2 * i - 1) % 8, 0), 0.0)
                f = part if f is None else f + part
                row = jnp.broadcast_to(tile[4:5], (8, 128))
                w = row if w is None else jnp.where(row8 < 2 * i, w, row)
            v.append(f)
            c.append(jnp.where(row8 % 2 == 0, w, pltpu.roll(w, 64, 1)))
        for yy in range(4):
            d = (lane8 // 16 - yy + 8) % 8
            w = jnp.where(d == 0, c[0], jnp.where(d == 1, c[1], c[2]))
            y = 4 * j + yy
            shift = (64 * (y // 16) - 16 * yy) % 128
            screens[y] = pltpu.roll(w, shift, 1) if shift else w
        for yy in range(6):
            y = 4 * j + yy - 1
            if not 0 <= y < 32:
                continue
            w = None
            for k in range(3):
                at = (lane8 - (20 * yy + 16 * k) + 256) % 128
                part = jnp.where(at < 18, v[k], 0.0)
                w = part if w is None else w + part
            w = pltpu.roll(w, (64 * (y // 16) - 20 * yy - 1) % 128, 1)
            total[y] = total[y] + w if y in total else w
    for m in range(16):
        cof[m] = jnp.where(z_ok, jnp.where(low, total[m], total[m + 16]), 0.0)
        coc[m] = jnp.where(z_ok, jnp.where(low, screens[m], screens[m + 16]), 0.0)
        cov[m] = coc[m] * cof[m]

    def coarse(i, v):
        twice = [m + m for m in v]
        sums = [twice[m] + pltpu.roll(v[m], 1, 1) + pltpu.roll(v[m], 127, 1) for m in range(16)]

        def other_half(m):
            u = pltpu.roll(v[m], 64, 1)
            return u + u + pltpu.roll(v[m], 65, 1) + pltpu.roll(v[m], 63, 1)

        wrap_up = jnp.where(low, 0.0, other_half(15))
        wrap_down = jnp.where(low, other_half(0), 0.0)
        new = []
        for m in range(16):
            a = (sums[m - 1] if m else wrap_up) + (sums[m + 1] if m < 15 else wrap_down) + (sums[m] + sums[m])
            b = (a + a) + jnp.where(row8 == 0, 0.0, pltpu.roll(a, 1, 0)) + jnp.where(row8 == 7, 0.0, pltpu.roll(a, 7, 0))
            c = coc[m]
            new.append(0.2 * v[m] + c * (cof[m] - twice[m]) + (0.25 * c) * b)
        return tuple(new)

    v = lax.fori_loop(0, ITERS - 1, coarse, tuple(cov[m] for m in range(16)), unroll=3)
    for m in range(16):
        cov[m] = v[m]

    mine = cov[pl.ds(4 * lax.rem(iy, 4), 4)]
    mine = mine.reshape(32, 128)
    mine = jnp.where(iy < 4, pltpu.roll(mine, 112, 1), pltpu.roll(mine, 48, 1))
    eout[...] = dot(mine, copy_coarse).reshape(4, 8, 128)
    for xc in range(2):
        for t in range(4):
            e3 = jnp.broadcast_to(eout[t, pl.ds(2 * ix + xc, 1), :], (8, 128))
            for p in range(8 * xc, 8 * xc + 8):
                rows = slice(8 * t, 8 * t + 8)
                out[p, rows, :] = base[p, rows, :] + e3

    finish(fine_copies + mid_copies, True)

    def wait_sent(dz):
        sent = dummy.at[pl.ds(0, gx * gy - (dz == 0)), pl.ds(0, 5), :]
        pltpu.make_async_copy(sent, sent, gsem.at[1 + dz]).wait()

    wait_sent(0)
    for dz in (1, -1):
        pl.when(has(2, dz))(functools.partial(wait_sent, dz))


def on_device(sizes, guess, right_side, screen):
    vm = pltpu.VMEM
    return pl.pallas_call(
        functools.partial(kernel, sizes),
        out_shape=jax.ShapeDtypeStruct((NX, NY, NZ), F32),
        in_specs=[pl.BlockSpec(memory_space=pltpu.HBM)] * 3,
        out_specs=pl.BlockSpec(memory_space=pltpu.VMEM),
        scratch_shapes=[
            vm((3, PX, PY, PZ), F32),
            vm((PX, PY, PZ), F32),
            vm((PX, PY, PZ), F32),
            vm((PX, PY, PZ), F32),
            vm((2, NY, 128), F32),
            vm((2, 2, 8, 128), F32),
            vm((2, 3, PY, 128), F32),
            vm((2, 2, 8, 128), F32),
            vm((8, NY, 128), F32),
            vm((2, 10, PY, 128), F32),
            vm((2, 10, 24, 128), F32),
            vm((10, 24, 128), F32),
            vm((10, 24, 128), F32),
            vm((10, 24, 128), F32),
            vm((16, 128), F32),
            vm((2, 3, 24, 128), F32),
            vm((8, NY, 128), F32),
            vm((NX, NY, NZ), F32),
            vm((3, 5, 128), F32),
            vm((3, sizes[1], sizes[0], 8, 128), F32),
            vm((16, 8, 128), F32),
            vm((16, 8, 128), F32),
            vm((16, 8, 128), F32),
            vm((4, 8, 128), F32),
            vm((sizes[0] * sizes[1], 8, 128), F32),
            pltpu.SemaphoreType.DMA((3,)),
            pltpu.SemaphoreType.DMA((42,)),
            pltpu.SemaphoreType.DMA((42,)),
            pltpu.SemaphoreType.DMA((26,)),
            pltpu.SemaphoreType.DMA((26,)),
            pltpu.SemaphoreType.DMA((6,)),
            pltpu.SemaphoreType.REGULAR((3,)),
        ],
        compiler_params=pltpu.CompilerParams(
            collective_id=0, has_side_effects=True, vmem_limit_bytes=107 * 512 * 1024
        ),
        name="multigrid",
    )(guess, right_side, screen)


def solution(mesh):
    placed = P("gx", "gy", "gz")
    sizes = tuple(mesh.shape[a] for a in ("gx", "gy", "gz"))
    return jax.shard_map(
        functools.partial(on_device, sizes), mesh=mesh, in_specs=(placed,) * 3, out_specs=placed, check_vma=False
    )
```

```python
import functools
import itertools

import jax
import jax.numpy as jnp
from jax import lax
from jax.experimental import pallas as pl
from jax.experimental.pallas import tpu as pltpu
from jax.sharding import PartitionSpec as P

ITERS = 16
OMEGA = 0.8
CENTER = 14.0
F32 = jnp.float32
MESH = pl.DeviceIdType.MESH

NX, NY, NZ = 16, 32, 128
PX, PY, PZ = 22, 40, 256
NEIGHBOURS = sorted(
    (o for o in itertools.product((-1, 0, 1), repeat=3) if o != (0, 0, 0)),
    key=lambda o: (-sum(abs(v) for v in o)),
)


def iota(shape, dim):
    return lax.broadcasted_iota(jnp.int32, shape, dim)


def row_sum(v):
    rows = v.shape[0]
    return v + v + pltpu.roll(v, 1, 0) + pltpu.roll(v, rows - 1, 0)


def column_sum(v):
    cols = v.shape[1]
    return v + v + pltpu.roll(v, 1, 1) + pltpu.roll(v, cols - 1, 1)


def plane_sum(v):
    rows, cols = v.shape
    a = v + v + pltpu.roll(v, 1, 1) + pltpu.roll(v, cols - 1, 1)
    return a + a + pltpu.roll(a, 1, 0) + pltpu.roll(a, rows - 1, 0)


def kernel(
    sizes,
    guess,
    rhs,
    scr,
    out,
    mm,
    cc,
    va,
    vb,
    packs,
    edges,
    zland,
    eland,
    rx,
    sx,
    s24,
    c1r,
    s1r,
    ex,
    zpack,
    zmid,
    e1f,
    base,
    msg,
    bf,
    cof,
    coc,
    cov,
    eout,
    dummy,
    load_sem,
    fs,
    fr,
    ms,
    mr,
    gsem,
    ready,
):
    gx, gy, gz = sizes
    ix, iy, iz = lax.axis_index("gx"), lax.axis_index("gy"), lax.axis_index("gz")

    def device(o):
        return (
            ix if o[0] == 0 else lax.rem(ix + o[0] % gx, gx),
            iy if o[1] == 0 else lax.rem(iy + o[1] % gy, gy),
            iz if o[2] == 0 else lax.rem(iz + o[2] % gz, gz),
        )

    peers = [
        o
        for o in itertools.product(range(gx), range(gy), (-1, 0, 1))
        if o != (0, 0, 0)
    ]
    peers = [(a - gx if a > gx // 2 else a, b - gy if b > gy // 2 else b, c) for a, b, c in peers]

    def hops(o):
        return abs(o[0]) + (abs(o[1]) + 1) // 2 + abs(o[2])

    peers.sort(key=lambda o: -hops(o))

    def has(axis, d):
        at, n = ((ix, gx), (iy, gy), (iz, gz))[axis]
        return at < n - d if d > 0 else at >= -d

    def visit(items, act, sign=1):
        def level(items, axis):
            if axis == 3:
                for item in items:
                    act(item)
                return
            for d in sorted({item[0][axis] for item in items}, key=abs):
                some = [item for item in items if item[0][axis] == d]
                if d == 0:
                    level(some, axis + 1)
                else:
                    pl.when(has(axis, sign * d))(functools.partial(level, some, axis + 1))

        level(items, 0)

    def count(axis, d):
        return 1 + has(axis, d).astype(jnp.int32) + has(axis, -d).astype(jnp.int32)

    rows_off = [(a, b, 0) for a in (0, 1, -1) for b in (2, -2)]
    barrier = pltpu.get_barrier_semaphore()

    def signal(semaphore):
        return lambda item: pl.semaphore_signal(semaphore, inc=1, device_id=device(item[0]), device_id_type=MESH)

    visit([(o,) for o in NEIGHBOURS + rows_off], signal(barrier))
    near = count(0, 1) * count(1, 1) * count(2, 1) - 1 + count(0, 1) * (count(1, 2) - 1)

    told = [(a, b, 0) for a in (0, 1, -1) for b in (0, 2, -2) if a or b]

    def tell(step):
        visit([(o,) for o in told], signal(ready.at[step]))

    def hear(step):
        pl.semaphore_wait(ready.at[step], count(0, 1) * count(1, 2) - 1)

    own = []
    for a, ref in ((2, scr), (0, guess), (1, rhs)):
        copy = pltpu.make_async_copy(ref, mm.at[a, pl.ds(3, NX), pl.ds(0, NY), pl.ds(0, NZ)], load_sem.at[a])
        copy.start()
        own.append(copy)
    for a in range(3):
        for p in range(PX):
            depth = 2 if a else 3
            mm[a, p, NY + depth : PY - depth, 0:NZ] = jnp.zeros((PY - NY - 2 * depth, NZ), F32)
    for side in range(2):
        for xs in range(3):
            zland[side, xs, NY + 3 : PY - 3, :] = jnp.zeros((PY - NY - 6, 128), F32)
            zmid[side, xs, 17:23, :] = jnp.zeros((6, 128), F32)
    for q in range(10):
        ex[q, 17:23, :] = jnp.zeros((6, 128), F32)
    s24[...] = jnp.zeros_like(s24)

    def blank(ref, *at):
        ref[at] = jnp.zeros(ref.at[at].shape, F32)

    whole = slice(None)
    for e, d in ((0, -1), (1, 1)):

        @pl.when(jnp.logical_not(has(0, d)))
        def _(e=e):
            planes = slice(3 + NX, PX) if e else slice(0, 3)
            for a in range(3):
                blank(mm, a, planes, whole, slice(0, NZ))
            for side in range(2):
                blank(zland, side, 2 * e)
                blank(eland, side, e)
                blank(zmid, side, 2 * e)
            blank(ex, 9 * e)

        @pl.when(jnp.logical_not(has(1, d)))
        def _(e=e):
            rows = slice(NY, NY + 3) if e else slice(PY - 3, PY)
            row = slice(16, 17) if e else slice(23, 24)
            for a in range(3):
                blank(mm, a, whole, rows, slice(0, NZ))
            for side in range(2):
                blank(zland, side, whole, rows)
                blank(zmid, side, whole, row)
            blank(ex, whole, row)

        @pl.when(jnp.logical_not(has(2, d)))
        def _(e=e, d=d):
            blank(zland, 1 - e)
            blank(eland, 1 - e)
            blank(zmid, 1 - e)
            blank(bf, 1 + d)

    r_i, c_i = iota((128, 128), 0), iota((128, 128), 1)
    pool = jnp.where(r_i // 2 == c_i, 0.5, 0.0).astype(F32)
    pool_halo = jnp.where(
        ((r_i < 2) & (c_i == 64)) | ((r_i >= 126) & (c_i == 127)), 0.5, 0.0
    ).astype(F32)
    copy_mid = jnp.where((c_i // 2 == r_i), 1.0, 0.0).astype(F32)
    copy_coarse = jnp.where((c_i // 8 == r_i), 1.0, 0.0).astype(F32)
    z_of = jnp.where(r_i < 64, r_i // 4 + 1, jnp.where(r_i < 68, 17, jnp.where(r_i >= 124, 0, 99)))
    gather_f = jnp.where((c_i % 20 == z_of) & (c_i < 120), 0.25, 0.0).astype(F32)
    gather_c = jnp.where((r_i // 4 == c_i % 16) & (r_i < 64), 0.25, 0.0).astype(F32)

    def dot(a, b):
        parts = []
        for i in range(3):
            parts.append(a.astype(jnp.bfloat16))
            a = a - parts[-1].astype(F32)
        b = jnp.concatenate([b.astype(jnp.bfloat16)] * 3, axis=0)
        return jnp.dot(jnp.concatenate(parts, axis=1), b, preferred_element_type=F32)

    for copy in own:
        copy.wait()

    lane = iota((NY, 128), 1)
    head = jnp.zeros((NY, 128), F32)
    tail = jnp.zeros((NY, 128), F32)
    for p in range(NX):
        for a, to, depth in ((0, 0, 3), (1, 3, 2), (2, 5, 2)):
            turned = mm[a, 3 + p, 0:NY, 0:NZ]
            at = 8 * p + to
            turned = pltpu.roll(turned, at, 1) if at else turned
            head = jnp.where((lane >= at) & (lane < at + depth), turned, head)
            behind = (lane >= at - depth) & (lane < at) if at else lane >= 128 - depth
            tail = jnp.where(behind, turned, tail)
    packs[0] = head
    packs[1] = tail
    lane8 = iota((8, 128), 1)
    for side, pack in ((0, head), (1, tail)):
        for e, first in ((0, 0), (1, NX - 3)):
            small = jnp.zeros((8, 128), F32)
            for t in range(4):
                moved = pltpu.roll(pack[8 * t : 8 * t + 8], (32 * t - 8 * first + 8) % 128, 1)
                small = jnp.where(lane8 // 32 == t, moved, small)
            edges[side, e] = small

    pl.semaphore_wait(barrier, near)
    tell(0)

    fine_copies = []
    given = (guess, rhs, scr)

    def describe(o, refs, sems, i):
        src, dst = refs()
        return pltpu.make_async_remote_copy(
            src_ref=src,
            dst_ref=dst,
            send_sem=sems[0].at[i],
            recv_sem=sems[1].at[i],
            device_id=device(o),
            device_id_type=MESH,
        )

    def started(copies, sems):
        def start(copy):
            copies.append(copy + (sems, len(copies)))
            describe(*copies[-1]).start()

        return start

    def finish(copies, sending):
        def one(copy):
            describe(*copy).wait_send() if sending else describe(*copy).wait_recv()

        visit(copies, one, 1 if sending else -1)

    def x_part(d, depth):
        if d == 0:
            return (3, NX), (3, NX)
        return ((3 + NX - depth, depth), (3 - depth, depth)) if d == 1 else ((3, depth), (3 + NX, depth))

    def y_part(d, depth):
        if d == 0:
            return (0, NY), (0, NY)
        return ((NY - depth, depth), (PY - depth, depth)) if d == 1 else ((0, depth), (NY, depth))

    def rows_of(o):
        copies = []
        for a, depth in ((0, 3), (1, 2), (2, 2)):
            (p0, n), (q0, _) = x_part(o[0], depth)
            (s0, sn), (t0, _) = y_part(o[1], depth)

            def refs(a=a, p0=p0, n=n, q0=q0, s0=s0, sn=sn, t0=t0):
                return (
                    mm.at[a, pl.ds(p0, n), pl.ds(s0, sn), pl.ds(0, NZ)],
                    mm.at[a, pl.ds(q0, n), pl.ds(t0, sn), pl.ds(0, NZ)],
                )

            copies.append((o, refs))
        return copies

    visit([c for o in NEIGHBOURS if o[2] == 0 for c in rows_of(o)], started(fine_copies, (fs, fr)))

    def pack_of(o):
        dx, dy, dz = o
        (s0, sn), (t0, _) = y_part(dy, 3)
        side = 1 if dz == 1 else 0
        if dx and not dy:
            return o, lambda: (edges.at[side, (dx + 1) // 2], eland.at[side, (1 - dx) // 2])
        return o, lambda: (packs.at[side, pl.ds(s0, sn), :], zland.at[side, 1 - dx, pl.ds(t0, sn), :])

    visit([pack_of(o) for o in NEIGHBOURS if o[2] != 0], started(fine_copies, (fs, fr)))
    for q in range(8):
        rx[q] = mm[2, 3 + 2 * q, 0:NY, 0:NZ] + mm[2, 4 + 2 * q, 0:NY, 0:NZ]
    s1_own = dot((rx[:, pl.ds(0, 16, 2), :] + rx[:, pl.ds(1, 16, 2), :]).reshape(128, 128), pool).reshape(8, 16, 128)
    lanes16 = iota((16, 128), 1)
    rows16 = iota((16, 128), 0)
    s4 = [s1_own[4 * i] + s1_own[4 * i + 1] + s1_own[4 * i + 2] + s1_own[4 * i + 3] for i in range(2)]
    s4 = dot(jnp.concatenate(s4, axis=0), gather_c)
    s4 = [jnp.where(lanes16 // 16 == rows16 // 4 + 4 * i, s4[16 * i : 16 * i + 16], 0.0) for i in range(2)]
    c3 = OMEGA / (CENTER + jnp.sum(s4[0] + s4[1], axis=0, keepdims=True))
    for k in range(3):
        msg[k, 4:5, :] = c3 if k == 0 else pltpu.roll(c3, 16 * k, 1)

    hear(0)
    tell(1)

    finish([c for c in fine_copies if c[0][0] == 0], False)
    hear(1)
    tell(2)

    rows_in = iota((PY, 128), 0)
    lane40 = iota((PY, 128), 1)
    row_ok = ((rows_in < 36) | (iy > 0)) & ((rows_in < NY) | (rows_in >= 36) | (iy < gy - 1))
    col_ok = ((lane40 < 64) & (iz < gz - 1)) | ((lane40 >= 64) & (iz > 0))
    both_ok = row_ok & col_ok
    def turn(v, back):
        return pltpu.roll(v, 128 - back, 1) if back else v

    def columns(p):
        if p < 3:
            xs, q, x_ok = 0, NX - 3 + p, ix > 0
        elif p < 3 + NX:
            xs, q, x_ok = 1, p - 3, None
        else:
            xs, q, x_ok = 2, p - 3 - NX, ix < gx - 1
        h = zland[0, xs]
        t = zland[1, xs]
        ok0 = row_ok if x_ok is None else row_ok & x_ok
        ok1 = both_ok if x_ok is None else both_ok & x_ok
        g1 = turn(jnp.where(lane40 % 8 < 3, h, t), 8 * q)
        mm[0, p, :, NZ:PZ] = jnp.where(ok1, g1, 0.0)
        if x_ok is None:
            mm[0, p, NY:PY, 0:NZ] = jnp.where(ok0[NY:PY], mm[0, p, NY:PY, 0:NZ], 0.0)
        else:
            mm[0, p, :, 0:NZ] = jnp.where(ok0, mm[0, p, :, 0:NZ], 0.0)
        if 0 < p < PX - 1:
            f1 = turn(jnp.where((lane40 % 8 == 3) | (lane40 % 8 == 4), h, t), 8 * q + 3)
            s1 = turn(jnp.where((lane40 % 8 == 5) | (lane40 % 8 == 6), h, t), 8 * q + 5)
            s1 = jnp.where((lane40 < 2) | (lane40 >= 126), s1, 0.0)
            mm[1, p, :, NZ:PZ] = f1
            mm[2, p, :, NZ:PZ] = s1
            cc[p, :, 0:NZ] = jnp.where(ok0, OMEGA / (CENTER + mm[2, p, :, 0:NZ]), 0.0)
            cc[p, :, NZ:PZ] = jnp.where(ok1, OMEGA / (CENTER + s1), 0.0)

    for p in range(3, 3 + NX):
        columns(p)

    def update(src, dst, p, b0, b1, b2):
        v = src[p]
        t = column_sum(b0 + b1 + b1 + b2)
        dst[p] = 0.2 * v + cc[p] * (mm[1, p] + 0.25 * t - 2.0 * v)

    def inner(src, dst, first, last):
        def body(p, carry):
            b0, b1 = carry
            b2 = row_sum(src[p + 1])
            update(src, dst, p, b0, b1, b2)
            return b1, b2

        b0, b1 = row_sum(src[first - 1]), row_sum(src[first])
        b2, b3 = b0, b1
        for p in range(first, last):
            b2, b3 = body(p, (b2, b3))
        return {first - 1: b0, first: b1, last - 1: b2, last: b3}

    def outer(src, dst, planes, sums):
        for p in planes:
            for i in (p - 1, p, p + 1):
                if i not in sums:
                    sums[i] = row_sum(src[i])
            update(src, dst, p, sums[p - 1], sums[p], sums[p + 1])

    def own_sum(p):
        return row_sum(vb[p])[0:NY]

    def residual(p, b0, b1, b2):
        t = column_sum(b0 + b1 + b1 + b2)[:, 0:NZ]
        v = vb[p, 0:NY, 0:NZ]
        return mm[1, p, 0:NY, 0:NZ] - (CENTER + 2.0 + mm[2, p, 0:NY, 0:NZ]) * v + 0.25 * t

    def pair(q, carry):
        b0, b1 = carry
        b2 = own_sum(4 + 2 * q)
        b3 = own_sum(5 + 2 * q)
        rx[q] = residual(3 + 2 * q, b0, b1, b2) + residual(4 + 2 * q, b1, b2, b3)
        return b2, b3

    first_sums = inner(mm.at[0], va, 4, 18)
    second_sums = inner(va, vb, 5, 17)
    third_sums = {6: own_sum(6), 7: own_sum(7)}
    sums = third_sums[6], third_sums[7]
    for q in range(2, 6):
        sums = pair(q, sums)
    third_sums[14], third_sums[15] = sums

    row24, lane24 = iota((24, 128), 0), iota((24, 128), 1)
    ok24 = (
        ((row24 < 20) | (iy > 0))
        & ((row24 < 16) | (row24 >= 20) | (iy < gy - 1))
        & ((lane24 < 96) | (iz > 0))
        & ((lane24 < 64) | (lane24 >= 96) | (iz < gz - 1))
    )

    def mid_screen(planes):
        for q in planes:
            sx[0, q] = mm[2, 1 + 2 * q, :, 0:NZ] + mm[2, 2 + 2 * q, :, 0:NZ]
            sx[1, q] = mm[2, 1 + 2 * q, :, NZ:PZ] + mm[2, 2 + 2 * q, :, NZ:PZ]
            for half in range(2):
                v = sx[half, q, pl.ds(0, 20, 2), :] + sx[half, q, pl.ds(1, 20, 2), :]
                s24[half, q, 0:20, :] = v
                s24[half, q, 23:24, :] = v[19:20, :]
        a = [jnp.concatenate([s24[half, q] for q in planes], axis=0) for half in range(2)]
        s1 = dot(a[0], pool) + dot(a[1], pool_halo)
        for i, q in enumerate(planes):
            ok = ok24 & (ix > 0) if q == 0 else (ok24 & (ix < gx - 1) if q == 9 else ok24)
            s1r[q] = s1[24 * i : 24 * i + 24]
            c1r[q] = jnp.where(ok, OMEGA / (CENTER + s1[24 * i : 24 * i + 24]), 0.0)

    mid_screen(tuple(range(1, 9)))

    finish([c for c in fine_copies if c[0][0] != 0], False)
    hear(2)

    for side in range(2):
        for e, first in ((0, NX - 3), (1, 0)):
            for t in range(4):
                zland[side, 2 * e, 8 * t : 8 * t + 8, :] = pltpu.roll(eland[side, e], (8 * first - 8 - 32 * t) % 128, 1)
    for p in (0, 1, 2, 19, 20, 21):
        columns(p)
    outer(mm.at[0], va, (3, 2, 1, 18, 19, 20), first_sums)
    outer(va, vb, (4, 3, 2, 17, 18, 19), second_sums)
    for q in (1, 0, 6, 7):
        for i in range(2 + 2 * q, 6 + 2 * q):
            if i not in third_sums:
                third_sums[i] = own_sum(i)
        b = [third_sums[i] for i in range(2 + 2 * q, 6 + 2 * q)]
        rx[q] = residual(3 + 2 * q, *b[:3]) + residual(4 + 2 * q, *b[1:])

    mid_screen((0, 9))

    f1 = dot((rx[:, pl.ds(0, 16, 2), :] + rx[:, pl.ds(1, 16, 2), :]).reshape(128, 128), pool).reshape(8, 16, 128)

    zero8 = jnp.zeros((8, 128), F32)
    f1z = [jnp.concatenate([f1[q], zero8], axis=0) for q in range(8)]
    e_own = [c1r[q + 1] * f1z[q] for q in range(8)]
    for q in range(8):
        ex[q + 1, 0:16, :] = e_own[q][0:16]

    def weigh(b, p):
        terms = [b[i] * w for i, w in ((p - 1, 1.0), (p, 2.0), (p + 1, 1.0)) if i in b]
        return 0.25 * functools.reduce(lambda m, n: m + n, terms)

    sums = {q: plane_sum(e_own[q]) for q in range(8)}
    e_two = {}
    for q in range(-1, 9):
        t = weigh(sums, q)
        if 0 <= q < 8:
            e_two[q] = 0.2 * e_own[q] + c1r[q + 1] * (f1z[q] + t - 2.0 * e_own[q])
        else:
            e_two[q] = c1r[q + 1] * t
    sums = {q: plane_sum(e_two[q]) for q in range(-1, 9)}
    parts = {}
    for q in range(-2, 10):
        r = weigh(sums, q)
        if q in e_two:
            r = r - (CENTER + 2.0 + s1r[q + 1]) * e_two[q]
        if 0 <= q < 8:
            r = r + f1z[q]
        at = (q + 4) // 4
        parts[at] = parts[at] + r if at in parts else r
    y_of = jnp.where(row24 < 16, row24 // 4 + 1, jnp.where(row24 < 18, 5, jnp.where(row24 >= 22, 0, 99)))
    z_at = lane24 % 20
    keep = (lane24 // 20 == y_of) & ((z_at != 0) | (iz > 0)) & ((z_at != 17) | (iz < gz - 1))
    stacked = dot(jnp.concatenate([parts[i] for i in range(4)], axis=0), gather_f)
    for i in range(4):
        row = jnp.sum(jnp.where(keep, stacked[24 * i : 24 * i + 24], 0.0), axis=0, keepdims=True)
        for k in range(3):
            msg[k, i : i + 1, :] = row if k == 0 else pltpu.roll(row, 16 * k, 1)

    slot = bf.at[:, iy, ix, pl.ds(0, 5), :]
    def send_parts(to):
        def one(item):
            o = item[1]
            pltpu.make_async_remote_copy(
                src_ref=msg.at[1 - o[2]],
                dst_ref=slot.at[1 - o[2]],
                send_sem=gsem.at[1 + o[2]],
                recv_sem=gsem.at[4 - o[2]],
                device_id=device(o),
                device_id_type=MESH,
            ).start()

        visit([((0, 0, o[2]), o) for o in to], one)

    send_parts([o for o in peers if hops(o) > 2])
    pltpu.make_async_copy(msg.at[1], slot.at[1], gsem.at[4]).start()

    ztail = jnp.zeros((16, 128), F32)
    for q in range(8):
        ztail = jnp.where(lanes16 == q, pltpu.roll(e_own[q][0:16], (q - 63) % 128, 1), ztail)
        ztail = jnp.where(lanes16 == 64 + q, pltpu.roll(e_own[q][0:16], 64 + q, 1), ztail)
    zpack[...] = ztail
    mid_copies = []

    def mid_of(o):
        dx, dy, dz = o
        (s0, sn), t0 = ((0, 16), 0) if dy == 0 else (((15, 1), 23) if dy == 1 else ((0, 1), 16))
        if dz == 0:
            (p0, n), q0 = ((1, 8), 1) if dx == 0 else (((8, 1), 0) if dx == 1 else ((1, 1), 9))
            return o, lambda: (ex.at[pl.ds(p0, n), pl.ds(s0, sn), :], ex.at[pl.ds(q0, n), pl.ds(t0, sn), :])
        side = 1 if dz == 1 else 0
        return o, lambda: (zpack.at[pl.ds(s0, sn), :], zmid.at[side, 1 - dx, pl.ds(t0, sn), :])

    visit([mid_of(o) for o in NEIGHBOURS], started(mid_copies, (ms, mr)))
    send_parts([o for o in peers if hops(o) <= 2])

    finish(fine_copies + mid_copies, True)

    def wait_sent(dz):
        sent = dummy.at[pl.ds(0, gx * gy - (dz == 0)), pl.ds(0, 5), :]
        pltpu.make_async_copy(sent, sent, gsem.at[1 + dz]).wait()

    wait_sent(0)
    for dz in (1, -1):
        pl.when(has(2, dz))(functools.partial(wait_sent, dz))

    def wait_parts(k):
        landed = bf.at[k, :, :, pl.ds(0, 5), :]
        pltpu.make_async_copy(landed, landed, gsem.at[3 + k]).wait()

    wait_parts(1)
    for k in (0, 2):
        pl.when(has(2, k - 1))(functools.partial(wait_parts, k))

    finish(mid_copies, False)

    row8 = iota((8, 128), 0)
    block = (lane8 // 16) % 4
    z_ok = (block < 3) & ((block > 0) | (iz > 0)) & ((block < 2) | (iz < gz - 1))
    low = lane8 < 64
    total, screens = {}, {}
    for j in range(gy):
        v, c = [], []
        for k in range(3):
            f = w = None
            for i in range(gx):
                tile = bf[k, j, i]
                at = row8 - (2 * i - 1)
                part = jnp.where((at >= 0) & (at < 4), pltpu.roll(tile, (2 * i - 1) % 8, 0), 0.0)
                f = part if f is None else f + part
                row = jnp.broadcast_to(tile[4:5], (8, 128))
                w = row if w is None else jnp.where(row8 < 2 * i, w, row)
            v.append(f)
            c.append(jnp.where(row8 % 2 == 0, w, pltpu.roll(w, 64, 1)))
        for yy in range(4):
            d = (lane8 // 16 - yy + 8) % 8
            w = jnp.where(d == 0, c[0], jnp.where(d == 1, c[1], c[2]))
            y = 4 * j + yy
            shift = (64 * (y // 16) - 16 * yy) % 128
            screens[y] = pltpu.roll(w, shift, 1) if shift else w
        for yy in range(6):
            y = 4 * j + yy - 1
            if not 0 <= y < 32:
                continue
            w = None
            for k in range(3):
                at = (lane8 - (20 * yy + 16 * k) + 256) % 128
                part = jnp.where(at < 18, v[k], 0.0)
                w = part if w is None else w + part
            w = pltpu.roll(w, (64 * (y // 16) - 20 * yy - 1) % 128, 1)
            total[y] = total[y] + w if y in total else w
    for m in range(16):
        cof[m] = jnp.where(z_ok, jnp.where(low, total[m], total[m + 16]), 0.0)
        coc[m] = jnp.where(z_ok, jnp.where(low, screens[m], screens[m + 16]), 0.0)
        cov[m] = coc[m] * cof[m]

    def coarse(i, v):
        twice = [m + m for m in v]
        sums = [twice[m] + pltpu.roll(v[m], 1, 1) + pltpu.roll(v[m], 127, 1) for m in range(16)]

        def other_half(m):
            u = pltpu.roll(v[m], 64, 1)
            return u + u + pltpu.roll(v[m], 65, 1) + pltpu.roll(v[m], 63, 1)

        wrap_up = jnp.where(low, 0.0, other_half(15))
        wrap_down = jnp.where(low, other_half(0), 0.0)
        new = []
        for m in range(16):
            a = (sums[m - 1] if m else wrap_up) + (sums[m + 1] if m < 15 else wrap_down) + (sums[m] + sums[m])
            b = (a + a) + jnp.where(row8 == 0, 0.0, pltpu.roll(a, 1, 0)) + jnp.where(row8 == 7, 0.0, pltpu.roll(a, 7, 0))
            c = coc[m]
            new.append(0.2 * v[m] + c * (cof[m] - twice[m]) + (0.25 * c) * b)
        return tuple(new)

    mid_sums = {}
    for p in range(10):
        if p == 0:
            xs, q, x_ok = 0, 7, ix > 0
        elif p < 9:
            xs, q, x_ok = 1, p - 1, None
        else:
            xs, q, x_ok = 2, 0, ix < gx - 1
        v = ex[p]
        v = jnp.where(lane24 == 64, pltpu.roll(zmid[0, xs], (-q) % 128, 1), v)
        v = jnp.where(lane24 == 127, pltpu.roll(zmid[1, xs], (127 - q) % 128, 1), v)
        ok = ok24 if x_ok is None else ok24 & x_ok
        mid_sums[p] = plane_sum(jnp.where(ok, v, 0.0))
    e1 = []
    for q in range(8):
        t = weigh(mid_sums, q + 1)[0:16]
        e = e_own[q][0:16]
        e1.append(0.2 * e + c1r[q + 1, 0:16] * (f1[q] + t - 2.0 * e))
    e1 = dot(jnp.concatenate(e1, axis=0), copy_mid).reshape(8, 16, 128)
    e1f[:, pl.ds(0, 16, 2), :] = e1
    e1f[:, pl.ds(1, 16, 2), :] = e1
    for p in range(NX):
        base[p] = vb[3 + p, 0:NY, 0:NZ] + e1f[p // 2]

    v = tuple(cov[m] for m in range(16))
    for i in range(ITERS - 1):
        v = coarse(i, v)
    for m in range(16):
        cov[m] = v[m]

    mine = cov[pl.ds(4 * lax.rem(iy, 4), 4)]
    mine = mine.reshape(32, 128)
    mine = jnp.where(iy < 4, pltpu.roll(mine, 112, 1), pltpu.roll(mine, 48, 1))
    eout[...] = dot(mine, copy_coarse).reshape(4, 8, 128)
    for xc in range(2):
        for t in range(4):
            e3 = jnp.broadcast_to(eout[t, pl.ds(2 * ix + xc, 1), :], (8, 128))
            for p in range(8 * xc, 8 * xc + 8):
                rows = slice(8 * t, 8 * t + 8)
                out[p, rows, :] = base[p, rows, :] + e3


def on_device(sizes, guess, right_side, screen):
    vm = pltpu.VMEM
    return pl.pallas_call(
        functools.partial(kernel, sizes),
        out_shape=jax.ShapeDtypeStruct((NX, NY, NZ), F32),
        in_specs=[pl.BlockSpec(memory_space=pltpu.HBM)] * 3,
        out_specs=pl.BlockSpec(memory_space=pltpu.VMEM),
        scratch_shapes=[
            vm((3, PX, PY, PZ), F32),
            vm((PX, PY, PZ), F32),
            vm((PX, PY, PZ), F32),
            vm((PX, PY, PZ), F32),
            vm((2, NY, 128), F32),
            vm((2, 2, 8, 128), F32),
            vm((2, 3, PY, 128), F32),
            vm((2, 2, 8, 128), F32),
            vm((8, NY, 128), F32),
            vm((2, 10, PY, 128), F32),
            vm((2, 10, 24, 128), F32),
            vm((10, 24, 128), F32),
            vm((10, 24, 128), F32),
            vm((10, 24, 128), F32),
            vm((16, 128), F32),
            vm((2, 3, 24, 128), F32),
            vm((8, NY, 128), F32),
            vm((NX, NY, NZ), F32),
            vm((3, 5, 128), F32),
            vm((3, sizes[1], sizes[0], 8, 128), F32),
            vm((16, 8, 128), F32),
            vm((16, 8, 128), F32),
            vm((16, 8, 128), F32),
            vm((4, 8, 128), F32),
            vm((sizes[0] * sizes[1], 8, 128), F32),
            pltpu.SemaphoreType.DMA((3,)),
            pltpu.SemaphoreType.DMA((42,)),
            pltpu.SemaphoreType.DMA((42,)),
            pltpu.SemaphoreType.DMA((26,)),
            pltpu.SemaphoreType.DMA((26,)),
            pltpu.SemaphoreType.DMA((6,)),
            pltpu.SemaphoreType.REGULAR((3,)),
        ],
        compiler_params=pltpu.CompilerParams(
            collective_id=0, has_side_effects=True, vmem_limit_bytes=107 * 512 * 1024
        ),
        name="multigrid",
    )(guess, right_side, screen)


def solution(mesh):
    placed = P("gx", "gy", "gz")
    sizes = tuple(mesh.shape[a] for a in ("gx", "gy", "gz"))
    return jax.shard_map(
        functools.partial(on_device, sizes), mesh=mesh, in_specs=(placed,) * 3, out_specs=placed, check_vma=False
    )
```

```python
import functools
import itertools

import jax
import jax.numpy as jnp
from jax import lax
from jax.experimental import pallas as pl
from jax.experimental.pallas import tpu as pltpu
from jax.sharding import PartitionSpec as P

ITERS = 16
OMEGA = 0.8
CENTER = 14.0
F32 = jnp.float32
MESH = pl.DeviceIdType.MESH

NX, NY, NZ = 16, 32, 128
PX, PY, PZ = 22, 40, 256
NEIGHBOURS = sorted(
    (o for o in itertools.product((-1, 0, 1), repeat=3) if o != (0, 0, 0)),
    key=lambda o: (-sum(abs(v) for v in o)),
)


def iota(shape, dim):
    return lax.broadcasted_iota(jnp.int32, shape, dim)


def row_sum(v):
    rows = v.shape[0]
    return v + v + pltpu.roll(v, 1, 0) + pltpu.roll(v, rows - 1, 0)


def column_sum(v):
    cols = v.shape[1]
    return v + v + pltpu.roll(v, 1, 1) + pltpu.roll(v, cols - 1, 1)


def plane_sum(v):
    rows, cols = v.shape
    a = v + v + pltpu.roll(v, 1, 1) + pltpu.roll(v, cols - 1, 1)
    return a + a + pltpu.roll(a, 1, 0) + pltpu.roll(a, rows - 1, 0)


def kernel(
    sizes,
    guess,
    rhs,
    scr,
    out,
    mm,
    cc,
    va,
    vb,
    packs,
    edges,
    zland,
    eland,
    rx,
    sx,
    s24,
    c1r,
    s1r,
    ex,
    zpack,
    zmid,
    e1f,
    base,
    msg,
    bf,
    cof,
    coc,
    cov,
    eout,
    dummy,
    load_sem,
    fs,
    fr,
    ms,
    mr,
    gsem,
    ready,
):
    gx, gy, gz = sizes
    ix, iy, iz = lax.axis_index("gx"), lax.axis_index("gy"), lax.axis_index("gz")

    def device(o):
        return (
            ix if o[0] == 0 else lax.rem(ix + o[0] % gx, gx),
            iy if o[1] == 0 else lax.rem(iy + o[1] % gy, gy),
            iz if o[2] == 0 else lax.rem(iz + o[2] % gz, gz),
        )

    peers = [
        o
        for o in itertools.product(range(gx), range(gy), (-1, 0, 1))
        if o != (0, 0, 0)
    ]
    peers = [(a - gx if a > gx // 2 else a, b - gy if b > gy // 2 else b, c) for a, b, c in peers]

    def hops(o):
        return abs(o[0]) + (abs(o[1]) + 1) // 2 + abs(o[2])

    peers.sort(key=lambda o: -hops(o))

    def has(axis, d):
        at, n = ((ix, gx), (iy, gy), (iz, gz))[axis]
        return at < n - d if d > 0 else at >= -d

    def visit(items, act, sign=1):
        def level(items, axis):
            if axis == 3:
                for item in items:
                    act(item)
                return
            for d in sorted({item[0][axis] for item in items}, key=lambda d: (abs(d), d)):
                some = [item for item in items if item[0][axis] == d]
                if d == 0:
                    level(some, axis + 1)
                else:
                    pl.when(has(axis, sign * d))(functools.partial(level, some, axis + 1))

        level(items, 0)

    def count(axis, d):
        return 1 + has(axis, d).astype(jnp.int32) + has(axis, -d).astype(jnp.int32)

    rows_off = [(a, b, 0) for a in (0, 1, -1) for b in (2, -2)]
    barrier = pltpu.get_barrier_semaphore()

    def signal(semaphore):
        return lambda item: pl.semaphore_signal(semaphore, inc=1, device_id=device(item[0]), device_id_type=MESH)

    visit([(o,) for o in NEIGHBOURS + rows_off], signal(barrier))
    near = count(0, 1) * count(1, 1) * count(2, 1) - 1 + count(0, 1) * (count(1, 2) - 1)

    told = [(a, b, 0) for a in (0, 1, -1) for b in (0, 2, -2) if a or b]

    def tell(step):
        visit([(o,) for o in told], signal(ready.at[step]))

    def hear(step):
        pl.semaphore_wait(ready.at[step], count(0, 1) * count(1, 2) - 1)

    own = []
    for a, ref in ((2, scr), (0, guess), (1, rhs)):
        copy = pltpu.make_async_copy(ref, mm.at[a, pl.ds(3, NX), pl.ds(0, NY), pl.ds(0, NZ)], load_sem.at[a])
        copy.start()
        own.append(copy)
    for a in range(3):
        for p in range(PX):
            depth = 2 if a else 3
            mm[a, p, NY + depth : PY - depth, 0:NZ] = jnp.zeros((PY - NY - 2 * depth, NZ), F32)
    for side in range(2):
        for xs in range(3):
            zland[side, xs, NY + 3 : PY - 3, :] = jnp.zeros((PY - NY - 6, 128), F32)
            zmid[side, xs, 17:23, :] = jnp.zeros((6, 128), F32)
    for q in range(10):
        ex[q, 17:23, :] = jnp.zeros((6, 128), F32)
    s24[...] = jnp.zeros_like(s24)

    def blank(ref, *at):
        ref[at] = jnp.zeros(ref.at[at].shape, F32)

    whole = slice(None)
    for e, d in ((0, -1), (1, 1)):

        @pl.when(jnp.logical_not(has(0, d)))
        def _(e=e):
            planes = slice(3 + NX, PX) if e else slice(0, 3)
            for a in range(3):
                blank(mm, a, planes, whole, slice(0, NZ))
            for side in range(2):
                blank(zland, side, 2 * e)
                blank(eland, side, e)
                blank(zmid, side, 2 * e)
            blank(ex, 9 * e)

        @pl.when(jnp.logical_not(has(1, d)))
        def _(e=e):
            rows = slice(NY, NY + 3) if e else slice(PY - 3, PY)
            row = slice(16, 17) if e else slice(23, 24)
            for a in range(3):
                blank(mm, a, whole, rows, slice(0, NZ))
            for side in range(2):
                blank(zland, side, whole, rows)
                blank(zmid, side, whole, row)
            blank(ex, whole, row)

        @pl.when(jnp.logical_not(has(2, d)))
        def _(e=e, d=d):
            blank(zland, 1 - e)
            blank(eland, 1 - e)
            blank(zmid, 1 - e)
            blank(bf, 1 + d)

    r_i, c_i = iota((128, 128), 0), iota((128, 128), 1)
    pool = jnp.where(r_i // 2 == c_i, 0.5, 0.0).astype(F32)
    pool_halo = jnp.where(
        ((r_i < 2) & (c_i == 64)) | ((r_i >= 126) & (c_i == 127)), 0.5, 0.0
    ).astype(F32)
    copy_mid = jnp.where((c_i // 2 == r_i), 1.0, 0.0).astype(F32)
    first = jnp.where(iy < gy // 2, 16, 80)
    copy_coarse = jnp.where((c_i // 8 + first == r_i), 1.0, 0.0).astype(F32)
    z_of = jnp.where(r_i < 64, r_i // 4 + 1, jnp.where(r_i < 68, 17, jnp.where(r_i >= 124, 0, 99)))
    c_f = (c_i + 96) % 128
    gather_f = jnp.where((c_f % 20 == z_of) & (c_f < 120), 0.25, 0.0).astype(F32)
    gather_c = jnp.where((r_i // 4 == c_i % 16) & (r_i < 64), 0.25, 0.0).astype(F32)

    def dot(a, b):
        parts = []
        for i in range(3):
            parts.append(a.astype(jnp.bfloat16))
            a = a - parts[-1].astype(F32)
        b = jnp.concatenate([b.astype(jnp.bfloat16)] * 3, axis=0)
        return jnp.dot(jnp.concatenate(parts, axis=1), b, preferred_element_type=F32)

    for copy in own:
        copy.wait()

    lane = iota((NY, 128), 1)
    head = jnp.zeros((NY, 128), F32)
    tail = jnp.zeros((NY, 128), F32)
    for p in range(NX):
        for a, to, depth in ((0, 0, 3), (1, 3, 2), (2, 5, 2)):
            turned = mm[a, 3 + p, 0:NY, 0:NZ]
            at = 8 * p + to
            turned = pltpu.roll(turned, at, 1) if at else turned
            head = jnp.where((lane >= at) & (lane < at + depth), turned, head)
            behind = (lane >= at - depth) & (lane < at) if at else lane >= 128 - depth
            tail = jnp.where(behind, turned, tail)
    packs[0] = head
    packs[1] = tail
    lane8 = iota((8, 128), 1)
    for side, pack in ((0, head), (1, tail)):
        for e, first in ((0, 0), (1, NX - 3)):
            small = jnp.zeros((8, 128), F32)
            for t in range(4):
                moved = pltpu.roll(pack[8 * t : 8 * t + 8], (32 * t - 8 * first + 8) % 128, 1)
                small = jnp.where(lane8 // 32 == t, moved, small)
            edges[side, e] = small

    pl.semaphore_wait(barrier, near)

    fine_copies = []
    given = (guess, rhs, scr)

    def describe(o, refs, sems, i):
        src, dst = refs()
        return pltpu.make_async_remote_copy(
            src_ref=src,
            dst_ref=dst,
            send_sem=sems[0].at[i],
            recv_sem=sems[1].at[i],
            device_id=device(o),
            device_id_type=MESH,
        )

    def started(copies, sems):
        def start(copy):
            copies.append(copy + (sems, len(copies)))
            describe(*copies[-1]).start()

        return start

    def finish(copies, sending):
        def one(copy):
            describe(*copy).wait_send() if sending else describe(*copy).wait_recv()

        visit(copies, one, 1 if sending else -1)

    def x_part(d, depth):
        if d == 0:
            return (3, NX), (3, NX)
        return ((3 + NX - depth, depth), (3 - depth, depth)) if d == 1 else ((3, depth), (3 + NX, depth))

    def y_part(d, depth):
        if d == 0:
            return (0, NY), (0, NY)
        return ((NY - depth, depth), (PY - depth, depth)) if d == 1 else ((0, depth), (NY, depth))

    def rows_of(o):
        copies = []
        for a, depth in ((0, 3), (1, 2), (2, 2)):
            (p0, n), (q0, _) = x_part(o[0], depth)
            (s0, sn), (t0, _) = y_part(o[1], depth)

            def refs(a=a, p0=p0, n=n, q0=q0, s0=s0, sn=sn, t0=t0):
                return (
                    mm.at[a, pl.ds(p0, n), pl.ds(s0, sn), pl.ds(0, NZ)],
                    mm.at[a, pl.ds(q0, n), pl.ds(t0, sn), pl.ds(0, NZ)],
                )

            copies.append((o, refs))
        return copies


    def pack_of(o):
        dx, dy, dz = o
        (s0, sn), (t0, _) = y_part(dy, 3)
        side = 1 if dz == 1 else 0
        if dx and not dy:
            return o, lambda: (edges.at[side, (dx + 1) // 2], eland.at[side, (1 - dx) // 2])
        return o, lambda: (packs.at[side, pl.ds(s0, sn), :], zland.at[side, 1 - dx, pl.ds(t0, sn), :])

    visit([pack_of(o) for o in NEIGHBOURS if o[2] != 0], started(fine_copies, (fs, fr)))
    visit([c for o in NEIGHBOURS if o[2] == 0 for c in rows_of(o)], started(fine_copies, (fs, fr)))
    tell(0)
    for q in range(8):
        rx[q] = mm[2, 3 + 2 * q, 0:NY, 0:NZ] + mm[2, 4 + 2 * q, 0:NY, 0:NZ]
    s1_own = dot((rx[:, pl.ds(0, 16, 2), :] + rx[:, pl.ds(1, 16, 2), :]).reshape(128, 128), pool).reshape(8, 16, 128)
    lanes16 = iota((16, 128), 1)
    rows16 = iota((16, 128), 0)
    s4 = [s1_own[4 * i] + s1_own[4 * i + 1] + s1_own[4 * i + 2] + s1_own[4 * i + 3] for i in range(2)]
    s4 = dot(jnp.concatenate(s4, axis=0), gather_c)
    s4 = [jnp.where(lanes16 // 16 == rows16 // 4 + 4 * i, s4[16 * i : 16 * i + 16], 0.0) for i in range(2)]
    c3 = OMEGA / (CENTER + jnp.sum(s4[0] + s4[1], axis=0, keepdims=True))
    for k in range(3):
        msg[k, 4:5, :] = c3 if k == 0 else pltpu.roll(c3, 16 * k, 1)

    hear(0)
    tell(1)

    finish([c for c in fine_copies if c[0][0] == 0], False)
    hear(1)
    tell(2)

    rows_in = iota((PY, 128), 0)
    lane40 = iota((PY, 128), 1)
    row_ok = ((rows_in < 36) | (iy > 0)) & ((rows_in < NY) | (rows_in >= 36) | (iy < gy - 1))
    col_ok = ((lane40 < 64) & (iz < gz - 1)) | ((lane40 >= 64) & (iz > 0))
    both_ok = row_ok & col_ok
    def turn(v, back):
        return pltpu.roll(v, 128 - back, 1) if back else v

    def columns(p):
        if p < 3:
            xs, q, x_ok = 0, NX - 3 + p, ix > 0
        elif p < 3 + NX:
            xs, q, x_ok = 1, p - 3, None
        else:
            xs, q, x_ok = 2, p - 3 - NX, ix < gx - 1
        h = zland[0, xs]
        t = zland[1, xs]
        ok0 = row_ok if x_ok is None else row_ok & x_ok
        ok1 = both_ok if x_ok is None else both_ok & x_ok
        g1 = turn(jnp.where(lane40 % 8 < 3, h, t), 8 * q)
        mm[0, p, :, NZ:PZ] = jnp.where(ok1, g1, 0.0)
        if x_ok is None:
            mm[0, p, NY:PY, 0:NZ] = jnp.where(ok0[NY:PY], mm[0, p, NY:PY, 0:NZ], 0.0)
        else:
            mm[0, p, :, 0:NZ] = jnp.where(ok0, mm[0, p, :, 0:NZ], 0.0)
        if 0 < p < PX - 1:
            f1 = turn(jnp.where((lane40 % 8 == 3) | (lane40 % 8 == 4), h, t), 8 * q + 3)
            s1 = turn(jnp.where((lane40 % 8 == 5) | (lane40 % 8 == 6), h, t), 8 * q + 5)
            s1 = jnp.where((lane40 < 2) | (lane40 >= 126), s1, 0.0)
            mm[1, p, :, NZ:PZ] = f1
            mm[2, p, :, NZ:PZ] = s1
            cc[p, :, 0:NZ] = jnp.where(ok0, OMEGA / (CENTER + mm[2, p, :, 0:NZ]), 0.0)
            cc[p, :, NZ:PZ] = jnp.where(ok1, OMEGA / (CENTER + s1), 0.0)

    for p in range(3, 3 + NX):
        columns(p)

    def update(src, dst, p, b0, b1, b2):
        v = src[p]
        t = column_sum(b0 + b1 + b1 + b2)
        dst[p] = 0.2 * v + cc[p] * (mm[1, p] + 0.25 * t - 2.0 * v)

    def inner(src, dst, first, last):
        def body(p, carry):
            b0, b1 = carry
            b2 = row_sum(src[p + 1])
            update(src, dst, p, b0, b1, b2)
            return b1, b2

        b0, b1 = row_sum(src[first - 1]), row_sum(src[first])
        b2, b3 = b0, b1
        for p in range(first, last):
            b2, b3 = body(p, (b2, b3))
        return {first - 1: b0, first: b1, last - 1: b2, last: b3}

    def outer(src, dst, planes, sums):
        for p in planes:
            for i in (p - 1, p, p + 1):
                if i not in sums:
                    sums[i] = row_sum(src[i])
            update(src, dst, p, sums[p - 1], sums[p], sums[p + 1])

    def own_sum(p):
        return row_sum(vb[p])[0:NY]

    def residual(p, b0, b1, b2):
        t = column_sum(b0 + b1 + b1 + b2)[:, 0:NZ]
        v = vb[p, 0:NY, 0:NZ]
        return mm[1, p, 0:NY, 0:NZ] - (CENTER + 2.0 + mm[2, p, 0:NY, 0:NZ]) * v + 0.25 * t

    def pair(q, carry):
        b0, b1 = carry
        b2 = own_sum(4 + 2 * q)
        b3 = own_sum(5 + 2 * q)
        rx[q] = residual(3 + 2 * q, b0, b1, b2) + residual(4 + 2 * q, b1, b2, b3)
        return b2, b3

    first_sums = inner(mm.at[0], va, 4, 18)
    second_sums = inner(va, vb, 5, 17)
    third_sums = {6: own_sum(6), 7: own_sum(7)}
    sums = third_sums[6], third_sums[7]
    for q in range(2, 6):
        sums = pair(q, sums)
    third_sums[14], third_sums[15] = sums

    row24, lane24 = iota((24, 128), 0), iota((24, 128), 1)
    ok24 = (
        ((row24 < 20) | (iy > 0))
        & ((row24 < 16) | (row24 >= 20) | (iy < gy - 1))
        & ((lane24 < 96) | (iz > 0))
        & ((lane24 < 64) | (lane24 >= 96) | (iz < gz - 1))
    )

    def mid_screen(planes):
        for q in planes:
            sx[0, q] = mm[2, 1 + 2 * q, :, 0:NZ] + mm[2, 2 + 2 * q, :, 0:NZ]
            sx[1, q] = mm[2, 1 + 2 * q, :, NZ:PZ] + mm[2, 2 + 2 * q, :, NZ:PZ]
            for half in range(2):
                v = sx[half, q, pl.ds(0, 20, 2), :] + sx[half, q, pl.ds(1, 20, 2), :]
                s24[half, q, 0:20, :] = v
                s24[half, q, 23:24, :] = v[19:20, :]
        a = [jnp.concatenate([s24[half, q] for q in planes], axis=0) for half in range(2)]
        s1 = dot(a[0], pool) + dot(a[1], pool_halo)
        for i, q in enumerate(planes):
            ok = ok24 & (ix > 0) if q == 0 else (ok24 & (ix < gx - 1) if q == 9 else ok24)
            s1r[q] = s1[24 * i : 24 * i + 24]
            c1r[q] = jnp.where(ok, OMEGA / (CENTER + s1[24 * i : 24 * i + 24]), 0.0)

    mid_screen(tuple(range(1, 9)))

    finish([c for c in fine_copies if c[0][0] != 0], False)
    hear(2)

    for side in range(2):
        for e, first in ((0, NX - 3), (1, 0)):
            for t in range(4):
                zland[side, 2 * e, 8 * t : 8 * t + 8, :] = pltpu.roll(eland[side, e], (8 * first - 8 - 32 * t) % 128, 1)
    for p in (0, 1, 2, 19, 20, 21):
        columns(p)
    outer(mm.at[0], va, (3, 2, 1, 18, 19, 20), first_sums)
    outer(va, vb, (4, 3, 2, 17, 18, 19), second_sums)
    for q in (1, 0, 6, 7):
        for i in range(2 + 2 * q, 6 + 2 * q):
            if i not in third_sums:
                third_sums[i] = own_sum(i)
        b = [third_sums[i] for i in range(2 + 2 * q, 6 + 2 * q)]
        rx[q] = residual(3 + 2 * q, *b[:3]) + residual(4 + 2 * q, *b[1:])

    mid_screen((0, 9))

    f1 = dot((rx[:, pl.ds(0, 16, 2), :] + rx[:, pl.ds(1, 16, 2), :]).reshape(128, 128), pool).reshape(8, 16, 128)

    zero8 = jnp.zeros((8, 128), F32)
    f1z = [jnp.concatenate([f1[q], zero8], axis=0) for q in range(8)]
    e_own = [c1r[q + 1] * f1z[q] for q in range(8)]
    for q in range(8):
        ex[q + 1, 0:16, :] = e_own[q][0:16]

    def weigh(b, p):
        terms = [b[i] * w for i, w in ((p - 1, 1.0), (p, 2.0), (p + 1, 1.0)) if i in b]
        return 0.25 * functools.reduce(lambda m, n: m + n, terms)

    sums = {q: plane_sum(e_own[q]) for q in range(8)}
    e_two = {}
    for q in range(-1, 9):
        t = weigh(sums, q)
        if 0 <= q < 8:
            e_two[q] = 0.2 * e_own[q] + c1r[q + 1] * (f1z[q] + t - 2.0 * e_own[q])
        else:
            e_two[q] = c1r[q + 1] * t
    sums = {q: plane_sum(e_two[q]) for q in range(-1, 9)}
    parts = {}
    for q in range(-2, 10):
        r = weigh(sums, q)
        if q in e_two:
            r = r - (CENTER + 2.0 + s1r[q + 1]) * e_two[q]
        if 0 <= q < 8:
            r = r + f1z[q]
        at = (q + 4) // 4
        parts[at] = parts[at] + r if at in parts else r
    y_of = jnp.where(row24 < 16, row24 // 4 + 1, jnp.where(row24 < 18, 5, jnp.where(row24 >= 22, 0, 99)))
    lane_f = (lane24 + 96) % 128
    z_at = lane_f % 20
    keep = (lane_f // 20 == y_of) & ((z_at != 0) | (iz > 0)) & ((z_at != 17) | (iz < gz - 1))
    stacked = dot(jnp.concatenate([parts[i] for i in range(4)], axis=0), gather_f)
    for i in range(4):
        row = jnp.sum(jnp.where(keep, stacked[24 * i : 24 * i + 24], 0.0), axis=0, keepdims=True)
        for k in range(3):
            msg[k, i : i + 1, :] = row if k == 2 else pltpu.roll(row, 96 + 16 * k, 1)

    slot = bf.at[:, iy, ix, pl.ds(0, 5), :]
    def send_parts(to):
        def one(item):
            o = item[1]
            pltpu.make_async_remote_copy(
                src_ref=msg.at[1 - o[2]],
                dst_ref=slot.at[1 - o[2]],
                send_sem=gsem.at[1 + o[2]],
                recv_sem=gsem.at[4 - o[2]],
                device_id=device(o),
                device_id_type=MESH,
            ).start()

        visit([((0, 0, o[2]), o) for o in to], one)

    send_parts([o for o in peers if o[2] and hops(o) > 3])
    send_parts([o for o in peers if hops(o) > 2 and not (o[2] and hops(o) > 3)])
    pltpu.make_async_copy(msg.at[1], slot.at[1], gsem.at[4]).start()

    ztail = jnp.zeros((16, 128), F32)
    for q in range(8):
        ztail = jnp.where(lanes16 == q, pltpu.roll(e_own[q][0:16], (q - 63) % 128, 1), ztail)
        ztail = jnp.where(lanes16 == 64 + q, pltpu.roll(e_own[q][0:16], 64 + q, 1), ztail)
    zpack[...] = ztail
    mid_copies = []

    def mid_of(o):
        dx, dy, dz = o
        (s0, sn), t0 = ((0, 16), 0) if dy == 0 else (((15, 1), 23) if dy == 1 else ((0, 1), 16))
        if dz == 0:
            (p0, n), q0 = ((1, 8), 1) if dx == 0 else (((8, 1), 0) if dx == 1 else ((1, 1), 9))
            return o, lambda: (ex.at[pl.ds(p0, n), pl.ds(s0, sn), :], ex.at[pl.ds(q0, n), pl.ds(t0, sn), :])
        side = 1 if dz == 1 else 0
        return o, lambda: (zpack.at[pl.ds(s0, sn), :], zmid.at[side, 1 - dx, pl.ds(t0, sn), :])

    visit([mid_of(o) for o in NEIGHBOURS], started(mid_copies, (ms, mr)))
    send_parts([o for o in peers if hops(o) <= 2])

    finish(fine_copies + mid_copies, True)

    def wait_sent(dz):
        sent = dummy.at[pl.ds(0, gx * gy - (dz == 0)), pl.ds(0, 5), :]
        pltpu.make_async_copy(sent, sent, gsem.at[1 + dz]).wait()

    wait_sent(0)
    for dz in (1, -1):
        pl.when(has(2, dz))(functools.partial(wait_sent, dz))

    def wait_parts(k):
        landed = bf.at[k, :, :, pl.ds(0, 5), :]
        pltpu.make_async_copy(landed, landed, gsem.at[3 + k]).wait()

    wait_parts(1)
    for k in (0, 2):
        pl.when(has(2, k - 1))(functools.partial(wait_parts, k))

    finish(mid_copies, False)

    row8 = iota((8, 128), 0)
    block = (lane8 // 16) % 4
    z_ok = (block < 3) & ((block > 0) | (iz > 0)) & ((block < 2) | (iz < gz - 1))
    low = lane8 < 64
    total, screens = {}, {}
    for j in range(gy):
        v, c = [], []
        for k in range(3):
            f = w = None
            for i in range(gx):
                tile = bf[k, j, i]
                at = row8 - (2 * i - 1)
                part = jnp.where((at >= 0) & (at < 4), pltpu.roll(tile, (2 * i - 1) % 8, 0), 0.0)
                f = part if f is None else f + part
                row = jnp.broadcast_to(tile[4:5], (8, 128))
                w = row if w is None else jnp.where(row8 < 2 * i, w, row)
            v.append(f)
            c.append(jnp.where(row8 % 2 == 0, w, pltpu.roll(w, 64, 1)))
        for yy in range(4):
            d = (lane8 // 16 - yy + 8) % 8
            w = jnp.where(d == 0, c[0], jnp.where(d == 1, c[1], c[2]))
            y = 4 * j + yy
            shift = (64 * (y // 16) - 16 * yy) % 128
            screens[y] = pltpu.roll(w, shift, 1) if shift else w
        for yy in range(6):
            y = 4 * j + yy - 1
            if not 0 <= y < 32:
                continue
            w = None
            for k in range(3):
                at = (lane8 - (20 * yy + 16 * k) + 256) % 128
                part = jnp.where(at < 18, v[k], 0.0)
                w = part if w is None else w + part
            w = pltpu.roll(w, (64 * (y // 16) - 20 * yy - 1) % 128, 1)
            total[y] = total[y] + w if y in total else w
    for m in range(16):
        cof[m] = jnp.where(z_ok, jnp.where(low, total[m], total[m + 16]), 0.0)
        coc[m] = jnp.where(z_ok, jnp.where(low, screens[m], screens[m + 16]), 0.0)
        cov[m] = coc[m] * cof[m]

    def coarse(i, v):
        twice = [m + m for m in v]
        sums = [twice[m] + pltpu.roll(v[m], 1, 1) + pltpu.roll(v[m], 127, 1) for m in range(16)]

        def other_half(m):
            u = pltpu.roll(v[m], 64, 1)
            return u + u + pltpu.roll(v[m], 65, 1) + pltpu.roll(v[m], 63, 1)

        wrap_up = jnp.where(low, 0.0, other_half(15))
        wrap_down = jnp.where(low, other_half(0), 0.0)
        new = []
        for m in range(16):
            a = (sums[m - 1] if m else wrap_up) + (sums[m + 1] if m < 15 else wrap_down) + (sums[m] + sums[m])
            b = (a + a) + jnp.where(row8 == 0, 0.0, pltpu.roll(a, 1, 0)) + jnp.where(row8 == 7, 0.0, pltpu.roll(a, 7, 0))
            c = coc[m]
            new.append(0.2 * v[m] + c * (cof[m] - twice[m]) + (0.25 * c) * b)
        return tuple(new)

    mid_sums = {}
    for p in range(10):
        if p == 0:
            xs, q, x_ok = 0, 7, ix > 0
        elif p < 9:
            xs, q, x_ok = 1, p - 1, None
        else:
            xs, q, x_ok = 2, 0, ix < gx - 1
        v = ex[p]
        v = jnp.where(lane24 == 64, pltpu.roll(zmid[0, xs], (-q) % 128, 1), v)
        v = jnp.where(lane24 == 127, pltpu.roll(zmid[1, xs], (127 - q) % 128, 1), v)
        ok = ok24 if x_ok is None else ok24 & x_ok
        mid_sums[p] = plane_sum(jnp.where(ok, v, 0.0))
    e1 = []
    for q in range(8):
        t = weigh(mid_sums, q + 1)[0:16]
        e = e_own[q][0:16]
        e1.append(0.2 * e + c1r[q + 1, 0:16] * (f1[q] + t - 2.0 * e))
    e1 = dot(jnp.concatenate(e1, axis=0), copy_mid).reshape(8, 16, 128)
    e1f[:, pl.ds(0, 16, 2), :] = e1
    e1f[:, pl.ds(1, 16, 2), :] = e1
    for p in range(NX):
        base[p] = vb[3 + p, 0:NY, 0:NZ] + e1f[p // 2]

    v = tuple(cov[m] for m in range(16))
    for i in range(ITERS - 1):
        v = coarse(i, v)
    for m in range(16):
        cov[m] = v[m]

    mine = cov[pl.ds(4 * lax.rem(iy, 4), 4)]
    mine = mine.reshape(32, 128)
    eout[...] = dot(mine, copy_coarse).reshape(4, 8, 128)
    for xc in range(2):
        for t in range(4):
            e3 = jnp.broadcast_to(eout[t, pl.ds(2 * ix + xc, 1), :], (8, 128))
            for p in range(8 * xc, 8 * xc + 8):
                rows = slice(8 * t, 8 * t + 8)
                out[p, rows, :] = base[p, rows, :] + e3


def on_device(sizes, guess, right_side, screen):
    vm = pltpu.VMEM
    return pl.pallas_call(
        functools.partial(kernel, sizes),
        out_shape=jax.ShapeDtypeStruct((NX, NY, NZ), F32),
        in_specs=[pl.BlockSpec(memory_space=pltpu.HBM)] * 3,
        out_specs=pl.BlockSpec(memory_space=pltpu.VMEM),
        scratch_shapes=[
            vm((3, PX, PY, PZ), F32),
            vm((PX, PY, PZ), F32),
            vm((PX, PY, PZ), F32),
            vm((PX, PY, PZ), F32),
            vm((2, NY, 128), F32),
            vm((2, 2, 8, 128), F32),
            vm((2, 3, PY, 128), F32),
            vm((2, 2, 8, 128), F32),
            vm((8, NY, 128), F32),
            vm((2, 10, PY, 128), F32),
            vm((2, 10, 24, 128), F32),
            vm((10, 24, 128), F32),
            vm((10, 24, 128), F32),
            vm((10, 24, 128), F32),
            vm((16, 128), F32),
            vm((2, 3, 24, 128), F32),
            vm((8, NY, 128), F32),
            vm((NX, NY, NZ), F32),
            vm((3, 5, 128), F32),
            vm((3, sizes[1], sizes[0], 8, 128), F32),
            vm((16, 8, 128), F32),
            vm((16, 8, 128), F32),
            vm((16, 8, 128), F32),
            vm((4, 8, 128), F32),
            vm((sizes[0] * sizes[1], 8, 128), F32),
            pltpu.SemaphoreType.DMA((3,)),
            pltpu.SemaphoreType.DMA((42,)),
            pltpu.SemaphoreType.DMA((42,)),
            pltpu.SemaphoreType.DMA((26,)),
            pltpu.SemaphoreType.DMA((26,)),
            pltpu.SemaphoreType.DMA((6,)),
            pltpu.SemaphoreType.REGULAR((3,)),
        ],
        compiler_params=pltpu.CompilerParams(
            collective_id=0, has_side_effects=True, vmem_limit_bytes=107 * 512 * 1024
        ),
        name="multigrid",
    )(guess, right_side, screen)


def solution(mesh):
    placed = P("gx", "gy", "gz")
    sizes = tuple(mesh.shape[a] for a in ("gx", "gy", "gz"))
    return jax.shard_map(
        functools.partial(on_device, sizes), mesh=mesh, in_specs=(placed,) * 3, out_specs=placed, check_vma=False
    )
```

```python
import functools
import itertools

import jax
import jax.numpy as jnp
from jax import lax
from jax.experimental import pallas as pl
from jax.experimental.pallas import tpu as pltpu
from jax.sharding import PartitionSpec as P

ITERS = 16
OMEGA = 0.8
CENTER = 14.0
F32 = jnp.float32
MESH = pl.DeviceIdType.MESH

NX, NY, NZ = 16, 32, 128
PX, PY, PZ = 22, 40, 256
NEIGHBOURS = sorted(
    (o for o in itertools.product((-1, 0, 1), repeat=3) if o != (0, 0, 0)),
    key=lambda o: (-sum(abs(v) for v in o)),
)


def iota(shape, dim):
    return lax.broadcasted_iota(jnp.int32, shape, dim)


def row_sum(v):
    rows = v.shape[0]
    return v + v + pltpu.roll(v, 1, 0) + pltpu.roll(v, rows - 1, 0)


def column_sum(v):
    cols = v.shape[1]
    return v + v + pltpu.roll(v, 1, 1) + pltpu.roll(v, cols - 1, 1)


def plane_sum(v):
    rows, cols = v.shape
    a = v + v + pltpu.roll(v, 1, 1) + pltpu.roll(v, cols - 1, 1)
    return a + a + pltpu.roll(a, 1, 0) + pltpu.roll(a, rows - 1, 0)


def kernel(
    sizes,
    guess,
    rhs,
    scr,
    out,
    mm,
    cc,
    va,
    vb,
    packs,
    edges,
    zland,
    eland,
    rx,
    sx,
    s24,
    c1r,
    s1r,
    ex,
    zpack,
    zmid,
    e1f,
    base,
    msg,
    bf,
    cof,
    coc,
    cov,
    eout,
    dummy,
    load_sem,
    fs,
    fr,
    ms,
    mr,
    gsem,
    ready,
):
    gx, gy, gz = sizes
    ix, iy, iz = lax.axis_index("gx"), lax.axis_index("gy"), lax.axis_index("gz")

    def device(o):
        return (
            ix if o[0] == 0 else lax.rem(ix + o[0] % gx, gx),
            iy if o[1] == 0 else lax.rem(iy + o[1] % gy, gy),
            iz if o[2] == 0 else lax.rem(iz + o[2] % gz, gz),
        )

    peers = [
        o
        for o in itertools.product(range(gx), range(gy), (-1, 0, 1))
        if o != (0, 0, 0)
    ]
    peers = [(a - gx if a > gx // 2 else a, b - gy if b > gy // 2 else b, c) for a, b, c in peers]

    def hops(o):
        return abs(o[0]) + (abs(o[1]) + 1) // 2 + abs(o[2])

    peers.sort(key=lambda o: -hops(o))

    def has(axis, d):
        at, n = ((ix, gx), (iy, gy), (iz, gz))[axis]
        return at < n - d if d > 0 else at >= -d

    def visit(items, act, sign=1, far=1):
        def level(items, axis):
            if axis == 3:
                for item in items:
                    act(item)
                return
            for d in sorted({item[0][axis] for item in items}, key=lambda d: (far * abs(d), d)):
                some = [item for item in items if item[0][axis] == d]
                if d == 0:
                    level(some, axis + 1)
                else:
                    pl.when(has(axis, sign * d))(functools.partial(level, some, axis + 1))

        level(items, 0)

    def count(axis, d):
        return 1 + has(axis, d).astype(jnp.int32) + has(axis, -d).astype(jnp.int32)

    rows_off = [(a, b, 0) for a in (0, 1, -1) for b in (2, -2)]
    barrier = pltpu.get_barrier_semaphore()

    def signal(semaphore):
        return lambda item: pl.semaphore_signal(semaphore, inc=1, device_id=device(item[0]), device_id_type=MESH)

    visit([(o,) for o in NEIGHBOURS if 0 in o] + [(o,) for o in rows_off], signal(barrier), far=-1)
    near = count(0, 1) * count(1, 1) * count(2, 1) - 1 + count(0, 1) * (count(1, 2) - 1)
    near = near - (count(0, 1) - 1) * (count(1, 1) - 1) * (count(2, 1) - 1)

    told = [(a, b, 0) for a in (0, 1, -1) for b in (0, 2, -2) if a or b]

    def tell(step):
        visit([(o,) for o in told], signal(ready.at[step]))

    def hear(step):
        pl.semaphore_wait(ready.at[step], count(0, 1) * count(1, 2) - 1)

    own = []
    for a, ref in ((2, scr), (0, guess), (1, rhs)):
        copy = pltpu.make_async_copy(ref, mm.at[a, pl.ds(3, NX), pl.ds(0, NY), pl.ds(0, NZ)], load_sem.at[a])
        copy.start()
        own.append(copy)
    for a in range(3):
        for p in range(PX):
            depth = 2 if a else 3
            mm[a, p, NY + depth : PY - depth, 0:NZ] = jnp.zeros((PY - NY - 2 * depth, NZ), F32)
    for side in range(2):
        for xs in range(3):
            zland[side, xs, NY + 3 : PY - 3, :] = jnp.zeros((PY - NY - 6, 128), F32)
            zmid[side, xs, 17:23, :] = jnp.zeros((6, 128), F32)
    for q in range(10):
        ex[q, 17:23, :] = jnp.zeros((6, 128), F32)
    s24[...] = jnp.zeros_like(s24)

    def blank(ref, *at):
        ref[at] = jnp.zeros(ref.at[at].shape, F32)

    whole = slice(None)
    for e, d in ((0, -1), (1, 1)):

        @pl.when(jnp.logical_not(has(0, d)))
        def _(e=e):
            planes = slice(3 + NX, PX) if e else slice(0, 3)
            for a in range(3):
                blank(mm, a, planes, whole, slice(0, NZ))
            for side in range(2):
                blank(zland, side, 2 * e)
                blank(eland, side, e)
                blank(zmid, side, 2 * e)
            blank(ex, 9 * e)

        @pl.when(jnp.logical_not(has(1, d)))
        def _(e=e):
            rows = slice(NY, NY + 3) if e else slice(PY - 3, PY)
            row = slice(16, 17) if e else slice(23, 24)
            for a in range(3):
                blank(mm, a, whole, rows, slice(0, NZ))
            for side in range(2):
                blank(zland, side, whole, rows)
                blank(zmid, side, whole, row)
            blank(ex, whole, row)

        @pl.when(jnp.logical_not(has(2, d)))
        def _(e=e, d=d):
            blank(zland, 1 - e)
            blank(eland, 1 - e)
            blank(zmid, 1 - e)
            blank(bf, 1 + d)

    r_i, c_i = iota((128, 128), 0), iota((128, 128), 1)
    pool = jnp.where(r_i // 2 == c_i, 0.5, 0.0).astype(F32)
    pool_halo = jnp.where(
        ((r_i < 2) & (c_i == 64)) | ((r_i >= 126) & (c_i == 127)), 0.5, 0.0
    ).astype(F32)
    copy_mid = jnp.where((c_i // 2 == r_i), 1.0, 0.0).astype(F32)
    first = jnp.where(iy < gy // 2, 16, 80)
    copy_coarse = jnp.where((c_i // 8 + first == r_i), 1.0, 0.0).astype(F32)
    z_of = jnp.where(r_i < 64, r_i // 4 + 1, jnp.where(r_i < 68, 17, jnp.where(r_i >= 124, 0, 99)))
    c_f = (c_i + 96) % 128
    gather_f = jnp.where((c_f % 20 == z_of) & (c_f < 120), 0.25, 0.0).astype(F32)
    gather_c = jnp.where((r_i // 4 == c_i % 16) & (r_i < 64), 0.25, 0.0).astype(F32)

    def dot(a, b):
        parts = []
        for i in range(3):
            parts.append(a.astype(jnp.bfloat16))
            a = a - parts[-1].astype(F32)
        b = jnp.concatenate([b.astype(jnp.bfloat16)] * 3, axis=0)
        return jnp.dot(jnp.concatenate(parts, axis=1), b, preferred_element_type=F32)

    for copy in own:
        copy.wait()

    lane = iota((NY, 128), 1)
    head = jnp.zeros((NY, 128), F32)
    tail = jnp.zeros((NY, 128), F32)
    for p in range(NX):
        for a, to, depth in ((0, 0, 3), (1, 3, 2), (2, 5, 2)):
            turned = mm[a, 3 + p, 0:NY, 0:NZ]
            at = 8 * p + to
            turned = pltpu.roll(turned, at, 1) if at else turned
            head = jnp.where((lane >= at) & (lane < at + depth), turned, head)
            behind = (lane >= at - depth) & (lane < at) if at else lane >= 128 - depth
            tail = jnp.where(behind, turned, tail)
    packs[0] = head
    packs[1] = tail
    lane8 = iota((8, 128), 1)
    for side, pack in ((0, head), (1, tail)):
        for e, first in ((0, 0), (1, NX - 3)):
            small = jnp.zeros((8, 128), F32)
            for t in range(4):
                moved = pltpu.roll(pack[8 * t : 8 * t + 8], (32 * t - 8 * first + 8) % 128, 1)
                small = jnp.where(lane8 // 32 == t, moved, small)
            edges[side, e] = small

    pl.semaphore_wait(barrier, near)

    fine_copies = []
    given = (guess, rhs, scr)

    def describe(o, refs, sems, i):
        src, dst = refs()
        return pltpu.make_async_remote_copy(
            src_ref=src,
            dst_ref=dst,
            send_sem=sems[0].at[i],
            recv_sem=sems[1].at[i],
            device_id=device(o),
            device_id_type=MESH,
        )

    def started(copies, sems):
        def start(copy):
            copies.append(copy + (sems, len(copies)))
            describe(*copies[-1]).start()

        return start

    def finish(copies, sending):
        def one(copy):
            describe(*copy).wait_send() if sending else describe(*copy).wait_recv()

        visit(copies, one, 1 if sending else -1)

    def x_part(d, depth):
        if d == 0:
            return (3, NX), (3, NX)
        return ((3 + NX - depth, depth), (3 - depth, depth)) if d == 1 else ((3, depth), (3 + NX, depth))

    def y_part(d, depth):
        if d == 0:
            return (0, NY), (0, NY)
        return ((NY - depth, depth), (PY - depth, depth)) if d == 1 else ((0, depth), (NY, depth))

    def rows_of(o):
        copies = []
        for a, depth in ((0, 3), (1, 2), (2, 2)):
            (p0, n), (q0, _) = x_part(o[0], depth)
            (s0, sn), (t0, _) = y_part(o[1], depth)

            def refs(a=a, p0=p0, n=n, q0=q0, s0=s0, sn=sn, t0=t0):
                return (
                    mm.at[a, pl.ds(p0, n), pl.ds(s0, sn), pl.ds(0, NZ)],
                    mm.at[a, pl.ds(q0, n), pl.ds(t0, sn), pl.ds(0, NZ)],
                )

            copies.append((o, refs))
        return copies


    def pack_of(o):
        dx, dy, dz = o
        (s0, sn), (t0, _) = y_part(dy, 3)
        side = 1 if dz == 1 else 0
        if dx and not dy:
            return o, lambda: (edges.at[side, (dx + 1) // 2], eland.at[side, (1 - dx) // 2])
        return o, lambda: (packs.at[side, pl.ds(s0, sn), :], zland.at[side, 1 - dx, pl.ds(t0, sn), :])

    visit([pack_of(o) for o in NEIGHBOURS if o[2] != 0 and 0 in o], started(fine_copies, (fs, fr)))
    visit([c for o in NEIGHBOURS if o[2] == 0 for c in rows_of(o)], started(fine_copies, (fs, fr)))
    tell(0)
    for q in range(8):
        rx[q] = mm[2, 3 + 2 * q, 0:NY, 0:NZ] + mm[2, 4 + 2 * q, 0:NY, 0:NZ]
    s1_own = dot((rx[:, pl.ds(0, 16, 2), :] + rx[:, pl.ds(1, 16, 2), :]).reshape(128, 128), pool).reshape(8, 16, 128)
    lanes16 = iota((16, 128), 1)
    rows16 = iota((16, 128), 0)
    s4 = [s1_own[4 * i] + s1_own[4 * i + 1] + s1_own[4 * i + 2] + s1_own[4 * i + 3] for i in range(2)]
    s4 = dot(jnp.concatenate(s4, axis=0), gather_c)
    s4 = [jnp.where(lanes16 // 16 == rows16 // 4 + 4 * i, s4[16 * i : 16 * i + 16], 0.0) for i in range(2)]
    c3 = OMEGA / (CENTER + jnp.sum(s4[0] + s4[1], axis=0, keepdims=True))
    for k in range(3):
        msg[k, 4:5, :] = c3 if k == 0 else pltpu.roll(c3, 16 * k, 1)

    for p in range(3, 3 + NX):
        cc[p, 0:NY, 0:NZ] = OMEGA / (CENTER + mm[2, p, 0:NY, 0:NZ])
    hear(0)
    visit([pack_of(o) for o in NEIGHBOURS if 0 not in o], started(fine_copies, (fs, fr)))
    tell(1)

    finish([c for c in fine_copies if c[0][0] == 0], False)
    hear(1)
    tell(2)

    rows_in = iota((PY, 128), 0)
    lane40 = iota((PY, 128), 1)
    row_ok = ((rows_in < 36) | (iy > 0)) & ((rows_in < NY) | (rows_in >= 36) | (iy < gy - 1))
    col_ok = ((lane40 < 64) & (iz < gz - 1)) | ((lane40 >= 64) & (iz > 0))
    both_ok = row_ok & col_ok
    def turn(v, back):
        return pltpu.roll(v, 128 - back, 1) if back else v

    def columns(p):
        if p < 3:
            xs, q, x_ok = 0, NX - 3 + p, ix > 0
        elif p < 3 + NX:
            xs, q, x_ok = 1, p - 3, None
        else:
            xs, q, x_ok = 2, p - 3 - NX, ix < gx - 1
        h = zland[0, xs]
        t = zland[1, xs]
        ok0 = row_ok if x_ok is None else row_ok & x_ok
        ok1 = both_ok if x_ok is None else both_ok & x_ok
        g1 = turn(jnp.where(lane40 % 8 < 3, h, t), 8 * q)
        mm[0, p, :, NZ:PZ] = jnp.where(ok1, g1, 0.0)
        if x_ok is None:
            mm[0, p, NY:PY, 0:NZ] = jnp.where(ok0[NY:PY], mm[0, p, NY:PY, 0:NZ], 0.0)
        else:
            mm[0, p, :, 0:NZ] = jnp.where(ok0, mm[0, p, :, 0:NZ], 0.0)
        if 0 < p < PX - 1:
            f1 = turn(jnp.where((lane40 % 8 == 3) | (lane40 % 8 == 4), h, t), 8 * q + 3)
            s1 = turn(jnp.where((lane40 % 8 == 5) | (lane40 % 8 == 6), h, t), 8 * q + 5)
            s1 = jnp.where((lane40 < 2) | (lane40 >= 126), s1, 0.0)
            mm[1, p, :, NZ:PZ] = f1
            mm[2, p, :, NZ:PZ] = s1
            rows = slice(0, PY) if x_ok is not None else slice(NY, PY)
            cc[p, rows, 0:NZ] = jnp.where(ok0[rows], OMEGA / (CENTER + mm[2, p, rows, 0:NZ]), 0.0)
            cc[p, :, NZ:PZ] = jnp.where(ok1, OMEGA / (CENTER + s1), 0.0)

    for p in range(3, 3 + NX):
        columns(p)

    def update(src, dst, p, b0, b1, b2):
        v = src[p]
        t = column_sum(b0 + b1 + b1 + b2)
        dst[p] = 0.2 * v + cc[p] * (mm[1, p] + 0.25 * t - 2.0 * v)

    def inner(src, dst, first, last):
        def body(p, carry):
            b0, b1 = carry
            b2 = row_sum(src[p + 1])
            update(src, dst, p, b0, b1, b2)
            return b1, b2

        b0, b1 = row_sum(src[first - 1]), row_sum(src[first])
        b2, b3 = b0, b1
        for p in range(first, last):
            b2, b3 = body(p, (b2, b3))
        return {first - 1: b0, first: b1, last - 1: b2, last: b3}

    def outer(src, dst, planes, sums):
        for p in planes:
            for i in (p - 1, p, p + 1):
                if i not in sums:
                    sums[i] = row_sum(src[i])
            update(src, dst, p, sums[p - 1], sums[p], sums[p + 1])

    def own_sum(p):
        return row_sum(vb[p])[0:NY]

    def residual(p, b0, b1, b2):
        t = column_sum(b0 + b1 + b1 + b2)[:, 0:NZ]
        v = vb[p, 0:NY, 0:NZ]
        return mm[1, p, 0:NY, 0:NZ] - (CENTER + 2.0 + mm[2, p, 0:NY, 0:NZ]) * v + 0.25 * t

    def pair(q, carry):
        b0, b1 = carry
        b2 = own_sum(4 + 2 * q)
        b3 = own_sum(5 + 2 * q)
        rx[q] = residual(3 + 2 * q, b0, b1, b2) + residual(4 + 2 * q, b1, b2, b3)
        return b2, b3

    first_sums = inner(mm.at[0], va, 4, 18)
    second_sums = inner(va, vb, 5, 17)
    third_sums = {6: own_sum(6), 7: own_sum(7)}
    sums = third_sums[6], third_sums[7]
    for q in range(2, 6):
        sums = pair(q, sums)
    third_sums[14], third_sums[15] = sums

    row24, lane24 = iota((24, 128), 0), iota((24, 128), 1)
    ok24 = (
        ((row24 < 20) | (iy > 0))
        & ((row24 < 16) | (row24 >= 20) | (iy < gy - 1))
        & ((lane24 < 96) | (iz > 0))
        & ((lane24 < 64) | (lane24 >= 96) | (iz < gz - 1))
    )

    def mid_screen(planes):
        for q in planes:
            sx[0, q] = mm[2, 1 + 2 * q, :, 0:NZ] + mm[2, 2 + 2 * q, :, 0:NZ]
            sx[1, q] = mm[2, 1 + 2 * q, :, NZ:PZ] + mm[2, 2 + 2 * q, :, NZ:PZ]
            for half in range(2):
                v = sx[half, q, pl.ds(0, 20, 2), :] + sx[half, q, pl.ds(1, 20, 2), :]
                s24[half, q, 0:20, :] = v
                s24[half, q, 23:24, :] = v[19:20, :]
        a = [jnp.concatenate([s24[half, q] for q in planes], axis=0) for half in range(2)]
        s1 = dot(a[0], pool) + dot(a[1], pool_halo)
        for i, q in enumerate(planes):
            ok = ok24 & (ix > 0) if q == 0 else (ok24 & (ix < gx - 1) if q == 9 else ok24)
            s1r[q] = s1[24 * i : 24 * i + 24]
            c1r[q] = jnp.where(ok, OMEGA / (CENTER + s1[24 * i : 24 * i + 24]), 0.0)

    mid_screen(tuple(range(1, 9)))

    finish([c for c in fine_copies if c[0][0] != 0], False)
    hear(2)

    for side in range(2):
        for e, first in ((0, NX - 3), (1, 0)):
            for t in range(4):
                zland[side, 2 * e, 8 * t : 8 * t + 8, :] = pltpu.roll(eland[side, e], (8 * first - 8 - 32 * t) % 128, 1)
    for p in (0, 1, 2, 19, 20, 21):
        columns(p)
    outer(mm.at[0], va, (3, 2, 1, 18, 19, 20), first_sums)
    outer(va, vb, (4, 3, 2, 17, 18, 19), second_sums)
    for q in (1, 0, 6, 7):
        for i in range(2 + 2 * q, 6 + 2 * q):
            if i not in third_sums:
                third_sums[i] = own_sum(i)
        b = [third_sums[i] for i in range(2 + 2 * q, 6 + 2 * q)]
        rx[q] = residual(3 + 2 * q, *b[:3]) + residual(4 + 2 * q, *b[1:])

    mid_screen((0, 9))

    f1 = dot((rx[:, pl.ds(0, 16, 2), :] + rx[:, pl.ds(1, 16, 2), :]).reshape(128, 128), pool).reshape(8, 16, 128)

    zero8 = jnp.zeros((8, 128), F32)
    f1z = [jnp.concatenate([f1[q], zero8], axis=0) for q in range(8)]
    e_own = [c1r[q + 1] * f1z[q] for q in range(8)]
    for q in range(8):
        ex[q + 1, 0:16, :] = e_own[q][0:16]

    def weigh(b, p):
        terms = [b[i] * w for i, w in ((p - 1, 1.0), (p, 2.0), (p + 1, 1.0)) if i in b]
        return 0.25 * functools.reduce(lambda m, n: m + n, terms)

    sums = {q: plane_sum(e_own[q]) for q in range(8)}
    e_two = {}
    for q in range(-1, 9):
        t = weigh(sums, q)
        if 0 <= q < 8:
            e_two[q] = 0.2 * e_own[q] + c1r[q + 1] * (f1z[q] + t - 2.0 * e_own[q])
        else:
            e_two[q] = c1r[q + 1] * t
    sums = {q: plane_sum(e_two[q]) for q in range(-1, 9)}
    parts = {}
    for q in range(-2, 10):
        r = weigh(sums, q)
        if q in e_two:
            r = r - (CENTER + 2.0 + s1r[q + 1]) * e_two[q]
        if 0 <= q < 8:
            r = r + f1z[q]
        at = (q + 4) // 4
        parts[at] = parts[at] + r if at in parts else r
    y_of = jnp.where(row24 < 16, row24 // 4 + 1, jnp.where(row24 < 18, 5, jnp.where(row24 >= 22, 0, 99)))
    lane_f = (lane24 + 96) % 128
    z_at = lane_f % 20
    keep = (lane_f // 20 == y_of) & ((z_at != 0) | (iz > 0)) & ((z_at != 17) | (iz < gz - 1))
    stacked = dot(jnp.concatenate([parts[i] for i in range(4)], axis=0), gather_f)
    for i in range(4):
        row = jnp.sum(jnp.where(keep, stacked[24 * i : 24 * i + 24], 0.0), axis=0, keepdims=True)
        for k in range(3):
            msg[k, i : i + 1, :] = row if k == 2 else pltpu.roll(row, 96 + 16 * k, 1)

    slot = bf.at[:, iy, ix, pl.ds(0, 5), :]
    def send_parts(to):
        def one(item):
            o = item[1]
            pltpu.make_async_remote_copy(
                src_ref=msg.at[1 - o[2]],
                dst_ref=slot.at[1 - o[2]],
                send_sem=gsem.at[1 + o[2]],
                recv_sem=gsem.at[4 - o[2]],
                device_id=device(o),
                device_id_type=MESH,
            ).start()

        visit([((0, 0, o[2]), o) for o in to], one)

    send_parts([o for o in peers if o[2] and hops(o) > 3])
    send_parts([o for o in peers if hops(o) > 2 and not (o[2] and hops(o) > 3)])
    pltpu.make_async_copy(msg.at[1], slot.at[1], gsem.at[4]).start()

    ztail = jnp.zeros((16, 128), F32)
    for q in range(8):
        ztail = jnp.where(lanes16 == q, pltpu.roll(e_own[q][0:16], (q - 63) % 128, 1), ztail)
        ztail = jnp.where(lanes16 == 64 + q, pltpu.roll(e_own[q][0:16], 64 + q, 1), ztail)
    zpack[...] = ztail
    mid_copies = []

    def mid_of(o):
        dx, dy, dz = o
        (s0, sn), t0 = ((0, 16), 0) if dy == 0 else (((15, 1), 23) if dy == 1 else ((0, 1), 16))
        if dz == 0:
            (p0, n), q0 = ((1, 8), 1) if dx == 0 else (((8, 1), 0) if dx == 1 else ((1, 1), 9))
            return o, lambda: (ex.at[pl.ds(p0, n), pl.ds(s0, sn), :], ex.at[pl.ds(q0, n), pl.ds(t0, sn), :])
        side = 1 if dz == 1 else 0
        return o, lambda: (zpack.at[pl.ds(s0, sn), :], zmid.at[side, 1 - dx, pl.ds(t0, sn), :])

    visit([mid_of(o) for o in NEIGHBOURS], started(mid_copies, (ms, mr)))
    send_parts([o for o in peers if hops(o) <= 2])

    finish(fine_copies + mid_copies, True)

    def wait_sent(dz):
        sent = dummy.at[pl.ds(0, gx * gy - (dz == 0)), pl.ds(0, 5), :]
        pltpu.make_async_copy(sent, sent, gsem.at[1 + dz]).wait()

    wait_sent(0)
    for dz in (1, -1):
        pl.when(has(2, dz))(functools.partial(wait_sent, dz))

    def wait_parts(k):
        landed = bf.at[k, :, :, pl.ds(0, 5), :]
        pltpu.make_async_copy(landed, landed, gsem.at[3 + k]).wait()

    wait_parts(1)
    for k in (0, 2):
        pl.when(has(2, k - 1))(functools.partial(wait_parts, k))

    finish(mid_copies, False)

    row8 = iota((8, 128), 0)
    block = (lane8 // 16) % 4
    z_ok = (block < 3) & ((block > 0) | (iz > 0)) & ((block < 2) | (iz < gz - 1))
    low = lane8 < 64
    total, screens = {}, {}
    for j in range(gy):
        v, c = [], []
        for k in range(3):
            f = w = None
            for i in range(gx):
                tile = bf[k, j, i]
                at = row8 - (2 * i - 1)
                part = jnp.where((at >= 0) & (at < 4), pltpu.roll(tile, (2 * i - 1) % 8, 0), 0.0)
                f = part if f is None else f + part
                row = jnp.broadcast_to(tile[4:5], (8, 128))
                w = row if w is None else jnp.where(row8 < 2 * i, w, row)
            v.append(f)
            c.append(jnp.where(row8 % 2 == 0, w, pltpu.roll(w, 64, 1)))
        for yy in range(4):
            d = (lane8 // 16 - yy + 8) % 8
            w = jnp.where(d == 0, c[0], jnp.where(d == 1, c[1], c[2]))
            y = 4 * j + yy
            shift = (64 * (y // 16) - 16 * yy) % 128
            screens[y] = pltpu.roll(w, shift, 1) if shift else w
        for yy in range(6):
            y = 4 * j + yy - 1
            if not 0 <= y < 32:
                continue
            w = None
            for k in range(3):
                at = (lane8 - (20 * yy + 16 * k) + 256) % 128
                part = jnp.where(at < 18, v[k], 0.0)
                w = part if w is None else w + part
            w = pltpu.roll(w, (64 * (y // 16) - 20 * yy - 1) % 128, 1)
            total[y] = total[y] + w if y in total else w
    for m in range(16):
        cof[m] = jnp.where(z_ok, jnp.where(low, total[m], total[m + 16]), 0.0)
        coc[m] = jnp.where(z_ok, jnp.where(low, screens[m], screens[m + 16]), 0.0)
        cov[m] = coc[m] * cof[m]

    def coarse(i, v):
        twice = [m + m for m in v]
        sums = [twice[m] + pltpu.roll(v[m], 1, 1) + pltpu.roll(v[m], 127, 1) for m in range(16)]

        def other_half(m):
            u = pltpu.roll(v[m], 64, 1)
            return u + u + pltpu.roll(v[m], 65, 1) + pltpu.roll(v[m], 63, 1)

        wrap_up = jnp.where(low, 0.0, other_half(15))
        wrap_down = jnp.where(low, other_half(0), 0.0)
        new = []
        for m in range(16):
            a = (sums[m - 1] if m else wrap_up) + (sums[m + 1] if m < 15 else wrap_down) + (sums[m] + sums[m])
            b = (a + a) + jnp.where(row8 == 0, 0.0, pltpu.roll(a, 1, 0)) + jnp.where(row8 == 7, 0.0, pltpu.roll(a, 7, 0))
            c = coc[m]
            new.append(0.2 * v[m] + c * (cof[m] - twice[m]) + (0.25 * c) * b)
        return tuple(new)

    mid_sums = {}
    for p in range(10):
        if p == 0:
            xs, q, x_ok = 0, 7, ix > 0
        elif p < 9:
            xs, q, x_ok = 1, p - 1, None
        else:
            xs, q, x_ok = 2, 0, ix < gx - 1
        v = ex[p]
        v = jnp.where(lane24 == 64, pltpu.roll(zmid[0, xs], (-q) % 128, 1), v)
        v = jnp.where(lane24 == 127, pltpu.roll(zmid[1, xs], (127 - q) % 128, 1), v)
        ok = ok24 if x_ok is None else ok24 & x_ok
        mid_sums[p] = plane_sum(jnp.where(ok, v, 0.0))
    e1 = []
    for q in range(8):
        t = weigh(mid_sums, q + 1)[0:16]
        e = e_own[q][0:16]
        e1.append(0.2 * e + c1r[q + 1, 0:16] * (f1[q] + t - 2.0 * e))
    e1 = dot(jnp.concatenate(e1, axis=0), copy_mid).reshape(8, 16, 128)
    e1f[:, pl.ds(0, 16, 2), :] = e1
    e1f[:, pl.ds(1, 16, 2), :] = e1
    for p in range(NX):
        base[p] = vb[3 + p, 0:NY, 0:NZ] + e1f[p // 2]

    v = tuple(cov[m] for m in range(16))
    for i in range(ITERS - 1):
        v = coarse(i, v)
    for m in range(16):
        cov[m] = v[m]

    mine = cov[pl.ds(4 * lax.rem(iy, 4), 4)]
    mine = mine.reshape(32, 128)
    eout[...] = dot(mine, copy_coarse).reshape(4, 8, 128)
    for xc in range(2):
        for t in range(4):
            e3 = jnp.broadcast_to(eout[t, pl.ds(2 * ix + xc, 1), :], (8, 128))
            for p in range(8 * xc, 8 * xc + 8):
                rows = slice(8 * t, 8 * t + 8)
                out[p, rows, :] = base[p, rows, :] + e3


def on_device(sizes, guess, right_side, screen):
    vm = pltpu.VMEM
    return pl.pallas_call(
        functools.partial(kernel, sizes),
        out_shape=jax.ShapeDtypeStruct((NX, NY, NZ), F32),
        in_specs=[pl.BlockSpec(memory_space=pltpu.HBM)] * 3,
        out_specs=pl.BlockSpec(memory_space=pltpu.VMEM),
        scratch_shapes=[
            vm((3, PX, PY, PZ), F32),
            vm((PX, PY, PZ), F32),
            vm((PX, PY, PZ), F32),
            vm((PX, PY, PZ), F32),
            vm((2, NY, 128), F32),
            vm((2, 2, 8, 128), F32),
            vm((2, 3, PY, 128), F32),
            vm((2, 2, 8, 128), F32),
            vm((8, NY, 128), F32),
            vm((2, 10, PY, 128), F32),
            vm((2, 10, 24, 128), F32),
            vm((10, 24, 128), F32),
            vm((10, 24, 128), F32),
            vm((10, 24, 128), F32),
            vm((16, 128), F32),
            vm((2, 3, 24, 128), F32),
            vm((8, NY, 128), F32),
            vm((NX, NY, NZ), F32),
            vm((3, 5, 128), F32),
            vm((3, sizes[1], sizes[0], 8, 128), F32),
            vm((16, 8, 128), F32),
            vm((16, 8, 128), F32),
            vm((16, 8, 128), F32),
            vm((4, 8, 128), F32),
            vm((sizes[0] * sizes[1], 8, 128), F32),
            pltpu.SemaphoreType.DMA((3,)),
            pltpu.SemaphoreType.DMA((42,)),
            pltpu.SemaphoreType.DMA((42,)),
            pltpu.SemaphoreType.DMA((26,)),
            pltpu.SemaphoreType.DMA((26,)),
            pltpu.SemaphoreType.DMA((6,)),
            pltpu.SemaphoreType.REGULAR((3,)),
        ],
        compiler_params=pltpu.CompilerParams(
            collective_id=0, has_side_effects=True, vmem_limit_bytes=107 * 512 * 1024
        ),
        name="multigrid",
    )(guess, right_side, screen)


def solution(mesh):
    placed = P("gx", "gy", "gz")
    sizes = tuple(mesh.shape[a] for a in ("gx", "gy", "gz"))
    return jax.shard_map(
        functools.partial(on_device, sizes), mesh=mesh, in_specs=(placed,) * 3, out_specs=placed, check_vma=False
    )
```

```python
import functools
import itertools

import jax
import jax.numpy as jnp
from jax import lax
from jax.experimental import pallas as pl
from jax.experimental.pallas import tpu as pltpu
from jax.sharding import PartitionSpec as P

ITERS = 16
OMEGA = 0.8
CENTER = 14.0
F32 = jnp.float32
MESH = pl.DeviceIdType.MESH

NX, NY, NZ = 16, 32, 128
PX, PY, PZ = 22, 40, 256
NEIGHBOURS = sorted(
    (o for o in itertools.product((-1, 0, 1), repeat=3) if o != (0, 0, 0)),
    key=lambda o: (-sum(abs(v) for v in o)),
)


def iota(shape, dim):
    return lax.broadcasted_iota(jnp.int32, shape, dim)


def row_sum(v):
    rows = v.shape[0]
    return v + v + pltpu.roll(v, 1, 0) + pltpu.roll(v, rows - 1, 0)


def column_sum(v):
    cols = v.shape[1]
    return v + v + pltpu.roll(v, 1, 1) + pltpu.roll(v, cols - 1, 1)


def plane_sum(v):
    rows, cols = v.shape
    a = v + v + pltpu.roll(v, 1, 1) + pltpu.roll(v, cols - 1, 1)
    return a + a + pltpu.roll(a, 1, 0) + pltpu.roll(a, rows - 1, 0)


def kernel(
    sizes,
    guess,
    rhs,
    scr,
    out,
    mm,
    cc,
    va,
    vb,
    packs,
    edges,
    zland,
    eland,
    rx,
    sx,
    s24,
    c1r,
    s1r,
    ex,
    zpack,
    zmid,
    e1f,
    base,
    msg,
    bf,
    cof,
    coc,
    cov,
    eout,
    dummy,
    load_sem,
    fs,
    fr,
    ms,
    mr,
    gsem,
    ready,
):
    gx, gy, gz = sizes
    ix, iy, iz = lax.axis_index("gx"), lax.axis_index("gy"), lax.axis_index("gz")

    def device(o):
        return (
            ix if o[0] == 0 else lax.rem(ix + o[0] % gx, gx),
            iy if o[1] == 0 else lax.rem(iy + o[1] % gy, gy),
            iz if o[2] == 0 else lax.rem(iz + o[2] % gz, gz),
        )

    peers = [
        o
        for o in itertools.product(range(gx), range(gy), (-1, 0, 1))
        if o != (0, 0, 0)
    ]
    peers = [(a - gx if a > gx // 2 else a, b - gy if b > gy // 2 else b, c) for a, b, c in peers]

    def hops(o):
        return abs(o[0]) + (abs(o[1]) + 1) // 2 + abs(o[2])

    peers.sort(key=lambda o: -hops(o))

    def has(axis, d):
        at, n = ((ix, gx), (iy, gy), (iz, gz))[axis]
        return at < n - d if d > 0 else at >= -d

    def visit(items, act, sign=1, far=1):
        def level(items, axis):
            if axis == 3:
                for item in items:
                    act(item)
                return
            for d in sorted({item[0][axis] for item in items}, key=lambda d: (far * abs(d), d)):
                some = [item for item in items if item[0][axis] == d]
                if d == 0:
                    level(some, axis + 1)
                else:
                    pl.when(has(axis, sign * d))(functools.partial(level, some, axis + 1))

        level(items, 0)

    def count(axis, d):
        return 1 + has(axis, d).astype(jnp.int32) + has(axis, -d).astype(jnp.int32)

    rows_off = [(a, b, 0) for a in (0, 1, -1) for b in (2, -2)]
    barrier = pltpu.get_barrier_semaphore()

    def signal(semaphore):
        return lambda item: pl.semaphore_signal(semaphore, inc=1, device_id=device(item[0]), device_id_type=MESH)

    visit([(o,) for o in NEIGHBOURS if 0 in o] + [(o,) for o in rows_off], signal(barrier), far=-1)
    near = count(0, 1) * count(1, 1) * count(2, 1) - 1 + count(0, 1) * (count(1, 2) - 1)
    near = near - (count(0, 1) - 1) * (count(1, 1) - 1) * (count(2, 1) - 1)

    told = [(a, b, 0) for a in (0, 1, -1) for b in (0, 2, -2) if a or b]

    def tell(step):
        visit([(o,) for o in told], signal(ready.at[step]))

    def hear(step):
        pl.semaphore_wait(ready.at[step], count(0, 1) * count(1, 2) - 1)

    own = []
    for a, ref in ((2, scr), (0, guess), (1, rhs)):
        copy = pltpu.make_async_copy(ref, mm.at[a, pl.ds(3, NX), pl.ds(0, NY), pl.ds(0, NZ)], load_sem.at[a])
        copy.start()
        own.append(copy)
    for a in range(3):
        for p in range(PX):
            depth = 2 if a else 3
            mm[a, p, NY + depth : PY - depth, 0:NZ] = jnp.zeros((PY - NY - 2 * depth, NZ), F32)
    for side in range(2):
        for xs in range(3):
            zland[side, xs, NY + 3 : PY - 3, :] = jnp.zeros((PY - NY - 6, 128), F32)
            zmid[side, xs, 17:23, :] = jnp.zeros((6, 128), F32)
    for q in range(10):
        ex[q, 17:23, :] = jnp.zeros((6, 128), F32)
    s24[...] = jnp.zeros_like(s24)

    def blank(ref, *at):
        ref[at] = jnp.zeros(ref.at[at].shape, F32)

    whole = slice(None)
    for e, d in ((0, -1), (1, 1)):

        @pl.when(jnp.logical_not(has(0, d)))
        def _(e=e):
            planes = slice(3 + NX, PX) if e else slice(0, 3)
            for a in range(3):
                blank(mm, a, planes, whole, slice(0, NZ))
            for side in range(2):
                blank(zland, side, 2 * e)
                blank(eland, side, e)
                blank(zmid, side, 2 * e)
            blank(ex, 9 * e)

        @pl.when(jnp.logical_not(has(1, d)))
        def _(e=e):
            rows = slice(NY, NY + 3) if e else slice(PY - 3, PY)
            row = slice(16, 17) if e else slice(23, 24)
            for a in range(3):
                blank(mm, a, whole, rows, slice(0, NZ))
            for side in range(2):
                blank(zland, side, whole, rows)
                blank(zmid, side, whole, row)
            blank(ex, whole, row)

        @pl.when(jnp.logical_not(has(2, d)))
        def _(e=e, d=d):
            blank(zland, 1 - e)
            blank(eland, 1 - e)
            blank(zmid, 1 - e)
            blank(bf, 1 + d)

    r_i, c_i = iota((128, 128), 0), iota((128, 128), 1)
    pool = jnp.where(r_i // 2 == c_i, 0.5, 0.0).astype(F32)
    pool_halo = jnp.where(
        ((r_i < 2) & (c_i == 64)) | ((r_i >= 126) & (c_i == 127)), 0.5, 0.0
    ).astype(F32)
    copy_mid = jnp.where((c_i // 2 == r_i), 1.0, 0.0).astype(F32)
    first = jnp.where(iy < gy // 2, 16, 80)
    copy_coarse = jnp.where((c_i // 8 + first == r_i), 1.0, 0.0).astype(F32)
    z_of = jnp.where(r_i < 64, r_i // 4 + 1, jnp.where(r_i < 68, 17, jnp.where(r_i >= 124, 0, 99)))
    c_f = (c_i + 96) % 128
    gather_f = jnp.where((c_f % 20 == z_of) & (c_f < 120), 0.25, 0.0).astype(F32)
    gather_c = jnp.where((r_i // 4 == c_i % 16) & (r_i < 64), 0.25, 0.0).astype(F32)

    def dot(a, b):
        parts = []
        for i in range(3):
            parts.append(a.astype(jnp.bfloat16))
            a = a - parts[-1].astype(F32)
        b = jnp.concatenate([b.astype(jnp.bfloat16)] * 3, axis=0)
        return jnp.dot(jnp.concatenate(parts, axis=1), b, preferred_element_type=F32)

    for copy in own:
        copy.wait()

    lane = iota((NY, 128), 1)
    head = jnp.zeros((NY, 128), F32)
    tail = jnp.zeros((NY, 128), F32)
    for p in range(NX):
        for a, to, depth in ((0, 0, 3), (1, 3, 2), (2, 5, 2)):
            turned = mm[a, 3 + p, 0:NY, 0:NZ]
            at = 8 * p + to
            turned = pltpu.roll(turned, at, 1) if at else turned
            head = jnp.where((lane >= at) & (lane < at + depth), turned, head)
            behind = (lane >= at - depth) & (lane < at) if at else lane >= 128 - depth
            tail = jnp.where(behind, turned, tail)
    packs[0] = head
    packs[1] = tail
    lane8 = iota((8, 128), 1)
    for side, pack in ((0, head), (1, tail)):
        for e, first in ((0, 0), (1, NX - 3)):
            small = jnp.zeros((8, 128), F32)
            for t in range(4):
                moved = pltpu.roll(pack[8 * t : 8 * t + 8], (32 * t - 8 * first + 8) % 128, 1)
                small = jnp.where(lane8 // 32 == t, moved, small)
            edges[side, e] = small

    pl.semaphore_wait(barrier, near)

    fine_copies = []
    given = (guess, rhs, scr)

    def describe(o, refs, sems, i):
        src, dst = refs()
        return pltpu.make_async_remote_copy(
            src_ref=src,
            dst_ref=dst,
            send_sem=sems[0].at[i],
            recv_sem=sems[1].at[i],
            device_id=device(o),
            device_id_type=MESH,
        )

    def started(copies, sems):
        def start(copy):
            copies.append(copy + (sems, len(copies)))
            describe(*copies[-1]).start()

        return start

    def finish(copies, sending):
        def one(copy):
            describe(*copy).wait_send() if sending else describe(*copy).wait_recv()

        visit(copies, one, 1 if sending else -1)

    def x_part(d, depth):
        if d == 0:
            return (3, NX), (3, NX)
        return ((3 + NX - depth, depth), (3 - depth, depth)) if d == 1 else ((3, depth), (3 + NX, depth))

    def y_part(d, depth):
        if d == 0:
            return (0, NY), (0, NY)
        return ((NY - depth, depth), (PY - depth, depth)) if d == 1 else ((0, depth), (NY, depth))

    def rows_of(o):
        copies = []
        for a, depth in ((0, 3), (1, 2), (2, 2)):
            (p0, n), (q0, _) = x_part(o[0], depth)
            (s0, sn), (t0, _) = y_part(o[1], depth)

            def refs(a=a, p0=p0, n=n, q0=q0, s0=s0, sn=sn, t0=t0):
                return (
                    mm.at[a, pl.ds(p0, n), pl.ds(s0, sn), pl.ds(0, NZ)],
                    mm.at[a, pl.ds(q0, n), pl.ds(t0, sn), pl.ds(0, NZ)],
                )

            copies.append((o, refs))
        return copies


    def pack_of(o):
        dx, dy, dz = o
        (s0, sn), (t0, _) = y_part(dy, 3)
        side = 1 if dz == 1 else 0
        if dx and not dy:
            return o, lambda: (edges.at[side, (dx + 1) // 2], eland.at[side, (1 - dx) // 2])
        return o, lambda: (packs.at[side, pl.ds(s0, sn), :], zland.at[side, 1 - dx, pl.ds(t0, sn), :])

    visit([pack_of(o) for o in NEIGHBOURS if o[2] != 0 and 0 in o], started(fine_copies, (fs, fr)))
    visit([c for o in NEIGHBOURS if o[2] == 0 for c in rows_of(o)], started(fine_copies, (fs, fr)))
    tell(0)
    hear(0)
    visit([pack_of(o) for o in NEIGHBOURS if 0 not in o], started(fine_copies, (fs, fr)))
    tell(1)

    for q in range(8):
        rx[q] = mm[2, 3 + 2 * q, 0:NY, 0:NZ] + mm[2, 4 + 2 * q, 0:NY, 0:NZ]
    s1_own = dot((rx[:, pl.ds(0, 16, 2), :] + rx[:, pl.ds(1, 16, 2), :]).reshape(128, 128), pool).reshape(8, 16, 128)
    lanes16 = iota((16, 128), 1)
    rows16 = iota((16, 128), 0)
    s4 = [s1_own[4 * i] + s1_own[4 * i + 1] + s1_own[4 * i + 2] + s1_own[4 * i + 3] for i in range(2)]
    s4 = dot(jnp.concatenate(s4, axis=0), gather_c)
    s4 = [jnp.where(lanes16 // 16 == rows16 // 4 + 4 * i, s4[16 * i : 16 * i + 16], 0.0) for i in range(2)]
    c3 = OMEGA / (CENTER + jnp.sum(s4[0] + s4[1], axis=0, keepdims=True))
    for k in range(3):
        msg[k, 4:5, :] = c3 if k == 0 else pltpu.roll(c3, 16 * k, 1)

    for p in range(3, 3 + NX):
        cc[p, 0:NY, 0:NZ] = OMEGA / (CENTER + mm[2, p, 0:NY, 0:NZ])

    finish([c for c in fine_copies if c[0][0] == 0], False)
    hear(1)
    tell(2)

    rows_in = iota((PY, 128), 0)
    lane40 = iota((PY, 128), 1)
    row_ok = ((rows_in < 36) | (iy > 0)) & ((rows_in < NY) | (rows_in >= 36) | (iy < gy - 1))
    col_ok = ((lane40 < 64) & (iz < gz - 1)) | ((lane40 >= 64) & (iz > 0))
    both_ok = row_ok & col_ok
    def turn(v, back):
        return pltpu.roll(v, 128 - back, 1) if back else v

    def columns(p):
        if p < 3:
            xs, q, x_ok = 0, NX - 3 + p, ix > 0
        elif p < 3 + NX:
            xs, q, x_ok = 1, p - 3, None
        else:
            xs, q, x_ok = 2, p - 3 - NX, ix < gx - 1
        h = zland[0, xs]
        t = zland[1, xs]
        ok0 = row_ok if x_ok is None else row_ok & x_ok
        ok1 = both_ok if x_ok is None else both_ok & x_ok
        g1 = turn(jnp.where(lane40 % 8 < 3, h, t), 8 * q)
        mm[0, p, :, NZ:PZ] = jnp.where(ok1, g1, 0.0)
        if x_ok is None:
            mm[0, p, NY:PY, 0:NZ] = jnp.where(ok0[NY:PY], mm[0, p, NY:PY, 0:NZ], 0.0)
        else:
            mm[0, p, :, 0:NZ] = jnp.where(ok0, mm[0, p, :, 0:NZ], 0.0)
        if 0 < p < PX - 1:
            f1 = turn(jnp.where((lane40 % 8 == 3) | (lane40 % 8 == 4), h, t), 8 * q + 3)
            s1 = turn(jnp.where((lane40 % 8 == 5) | (lane40 % 8 == 6), h, t), 8 * q + 5)
            s1 = jnp.where((lane40 < 2) | (lane40 >= 126), s1, 0.0)
            mm[1, p, :, NZ:PZ] = f1
            mm[2, p, :, NZ:PZ] = s1
            rows = slice(0, PY) if x_ok is not None else slice(NY, PY)
            cc[p, rows, 0:NZ] = jnp.where(ok0[rows], OMEGA / (CENTER + mm[2, p, rows, 0:NZ]), 0.0)
            cc[p, :, NZ:PZ] = jnp.where(ok1, OMEGA / (CENTER + s1), 0.0)

    for p in range(3, 3 + NX):
        columns(p)

    def update(src, dst, p, b0, b1, b2):
        v = src[p]
        t = column_sum(b0 + b1 + b1 + b2)
        dst[p] = 0.2 * v + cc[p] * (mm[1, p] + 0.25 * t - 2.0 * v)

    def inner(src, dst, first, last):
        def body(p, carry):
            b0, b1 = carry
            b2 = row_sum(src[p + 1])
            update(src, dst, p, b0, b1, b2)
            return b1, b2

        b0, b1 = row_sum(src[first - 1]), row_sum(src[first])
        b2, b3 = b0, b1
        for p in range(first, last):
            b2, b3 = body(p, (b2, b3))
        return {first - 1: b0, first: b1, last - 1: b2, last: b3}

    def outer(src, dst, planes, sums):
        for p in planes:
            for i in (p - 1, p, p + 1):
                if i not in sums:
                    sums[i] = row_sum(src[i])
            update(src, dst, p, sums[p - 1], sums[p], sums[p + 1])

    def own_sum(p):
        return row_sum(vb[p])[0:NY]

    def residual(p, b0, b1, b2):
        t = column_sum(b0 + b1 + b1 + b2)[:, 0:NZ]
        v = vb[p, 0:NY, 0:NZ]
        return mm[1, p, 0:NY, 0:NZ] - (CENTER + 2.0 + mm[2, p, 0:NY, 0:NZ]) * v + 0.25 * t

    def pair(q, carry):
        b0, b1 = carry
        b2 = own_sum(4 + 2 * q)
        b3 = own_sum(5 + 2 * q)
        rx[q] = residual(3 + 2 * q, b0, b1, b2) + residual(4 + 2 * q, b1, b2, b3)
        return b2, b3

    first_sums = inner(mm.at[0], va, 4, 18)
    second_sums = inner(va, vb, 5, 17)
    third_sums = {6: own_sum(6), 7: own_sum(7)}
    sums = third_sums[6], third_sums[7]
    for q in range(2, 6):
        sums = pair(q, sums)
    third_sums[14], third_sums[15] = sums

    row24, lane24 = iota((24, 128), 0), iota((24, 128), 1)
    ok24 = (
        ((row24 < 20) | (iy > 0))
        & ((row24 < 16) | (row24 >= 20) | (iy < gy - 1))
        & ((lane24 < 96) | (iz > 0))
        & ((lane24 < 64) | (lane24 >= 96) | (iz < gz - 1))
    )

    def mid_screen(planes):
        for q in planes:
            sx[0, q] = mm[2, 1 + 2 * q, :, 0:NZ] + mm[2, 2 + 2 * q, :, 0:NZ]
            sx[1, q] = mm[2, 1 + 2 * q, :, NZ:PZ] + mm[2, 2 + 2 * q, :, NZ:PZ]
            for half in range(2):
                v = sx[half, q, pl.ds(0, 20, 2), :] + sx[half, q, pl.ds(1, 20, 2), :]
                s24[half, q, 0:20, :] = v
                s24[half, q, 23:24, :] = v[19:20, :]
        a = [jnp.concatenate([s24[half, q] for q in planes], axis=0) for half in range(2)]
        s1 = dot(a[0], pool) + dot(a[1], pool_halo)
        for i, q in enumerate(planes):
            ok = ok24 & (ix > 0) if q == 0 else (ok24 & (ix < gx - 1) if q == 9 else ok24)
            s1r[q] = s1[24 * i : 24 * i + 24]
            c1r[q] = jnp.where(ok, OMEGA / (CENTER + s1[24 * i : 24 * i + 24]), 0.0)

    mid_screen(tuple(range(1, 9)))

    finish([c for c in fine_copies if c[0][0] != 0], False)
    hear(2)

    for side in range(2):
        for e, first in ((0, NX - 3), (1, 0)):
            for t in range(4):
                zland[side, 2 * e, 8 * t : 8 * t + 8, :] = pltpu.roll(eland[side, e], (8 * first - 8 - 32 * t) % 128, 1)
    for p in (0, 1, 2, 19, 20, 21):
        columns(p)
    outer(mm.at[0], va, (3, 2, 1, 18, 19, 20), first_sums)
    outer(va, vb, (4, 3, 2, 17, 18, 19), second_sums)
    for q in (1, 0, 6, 7):
        for i in range(2 + 2 * q, 6 + 2 * q):
            if i not in third_sums:
                third_sums[i] = own_sum(i)
        b = [third_sums[i] for i in range(2 + 2 * q, 6 + 2 * q)]
        rx[q] = residual(3 + 2 * q, *b[:3]) + residual(4 + 2 * q, *b[1:])

    mid_screen((0, 9))

    f1 = dot((rx[:, pl.ds(0, 16, 2), :] + rx[:, pl.ds(1, 16, 2), :]).reshape(128, 128), pool).reshape(8, 16, 128)

    zero8 = jnp.zeros((8, 128), F32)
    f1z = [jnp.concatenate([f1[q], zero8], axis=0) for q in range(8)]
    e_own = [c1r[q + 1] * f1z[q] for q in range(8)]
    for q in range(8):
        ex[q + 1, 0:16, :] = e_own[q][0:16]

    def weigh(b, p):
        terms = [b[i] * w for i, w in ((p - 1, 1.0), (p, 2.0), (p + 1, 1.0)) if i in b]
        return 0.25 * functools.reduce(lambda m, n: m + n, terms)

    sums = {q: plane_sum(e_own[q]) for q in range(8)}
    e_two = {}
    for q in range(-1, 9):
        t = weigh(sums, q)
        if 0 <= q < 8:
            e_two[q] = 0.2 * e_own[q] + c1r[q + 1] * (f1z[q] + t - 2.0 * e_own[q])
        else:
            e_two[q] = c1r[q + 1] * t
    sums = {q: plane_sum(e_two[q]) for q in range(-1, 9)}
    parts = {}
    for q in range(-2, 10):
        r = weigh(sums, q)
        if q in e_two:
            r = r - (CENTER + 2.0 + s1r[q + 1]) * e_two[q]
        if 0 <= q < 8:
            r = r + f1z[q]
        at = (q + 4) // 4
        parts[at] = parts[at] + r if at in parts else r
    y_of = jnp.where(row24 < 16, row24 // 4 + 1, jnp.where(row24 < 18, 5, jnp.where(row24 >= 22, 0, 99)))
    lane_f = (lane24 + 96) % 128
    z_at = lane_f % 20
    keep = (lane_f // 20 == y_of) & ((z_at != 0) | (iz > 0)) & ((z_at != 17) | (iz < gz - 1))
    stacked = dot(jnp.concatenate([parts[i] for i in range(4)], axis=0), gather_f)
    for i in range(4):
        row = jnp.sum(jnp.where(keep, stacked[24 * i : 24 * i + 24], 0.0), axis=0, keepdims=True)
        for k in range(3):
            msg[k, i : i + 1, :] = row if k == 2 else pltpu.roll(row, 96 + 16 * k, 1)

    slot = bf.at[:, iy, ix, pl.ds(0, 5), :]
    def send_parts(to):
        def one(item):
            o = item[1]
            pltpu.make_async_remote_copy(
                src_ref=msg.at[1 - o[2]],
                dst_ref=slot.at[1 - o[2]],
                send_sem=gsem.at[1 + o[2]],
                recv_sem=gsem.at[4 - o[2]],
                device_id=device(o),
                device_id_type=MESH,
            ).start()

        visit([((0, 0, o[2]), o) for o in to], one)

    send_parts([o for o in peers if o[2] and hops(o) > 3])
    send_parts([o for o in peers if hops(o) > 2 and not (o[2] and hops(o) > 3)])
    pltpu.make_async_copy(msg.at[1], slot.at[1], gsem.at[4]).start()

    ztail = jnp.zeros((16, 128), F32)
    for q in range(8):
        ztail = jnp.where(lanes16 == q, pltpu.roll(e_own[q][0:16], (q - 63) % 128, 1), ztail)
        ztail = jnp.where(lanes16 == 64 + q, pltpu.roll(e_own[q][0:16], 64 + q, 1), ztail)
    zpack[...] = ztail
    mid_copies = []

    def mid_of(o):
        dx, dy, dz = o
        (s0, sn), t0 = ((0, 16), 0) if dy == 0 else (((15, 1), 23) if dy == 1 else ((0, 1), 16))
        if dz == 0:
            (p0, n), q0 = ((1, 8), 1) if dx == 0 else (((8, 1), 0) if dx == 1 else ((1, 1), 9))
            return o, lambda: (ex.at[pl.ds(p0, n), pl.ds(s0, sn), :], ex.at[pl.ds(q0, n), pl.ds(t0, sn), :])
        side = 1 if dz == 1 else 0
        return o, lambda: (zpack.at[pl.ds(s0, sn), :], zmid.at[side, 1 - dx, pl.ds(t0, sn), :])

    visit([mid_of(o) for o in NEIGHBOURS], started(mid_copies, (ms, mr)))
    send_parts([o for o in peers if hops(o) <= 2])

    finish(fine_copies + mid_copies, True)

    def wait_sent(dz):
        sent = dummy.at[pl.ds(0, gx * gy - (dz == 0)), pl.ds(0, 5), :]
        pltpu.make_async_copy(sent, sent, gsem.at[1 + dz]).wait()

    wait_sent(0)
    for dz in (1, -1):
        pl.when(has(2, dz))(functools.partial(wait_sent, dz))

    def wait_parts(k):
        landed = bf.at[k, :, :, pl.ds(0, 5), :]
        pltpu.make_async_copy(landed, landed, gsem.at[3 + k]).wait()

    wait_parts(1)
    for k in (0, 2):
        pl.when(has(2, k - 1))(functools.partial(wait_parts, k))

    finish(mid_copies, False)

    row8 = iota((8, 128), 0)
    block = (lane8 // 16) % 4
    z_ok = (block < 3) & ((block > 0) | (iz > 0)) & ((block < 2) | (iz < gz - 1))
    low = lane8 < 64
    total, screens = {}, {}
    for j in range(gy):
        v, c = [], []
        for k in range(3):
            f = w = None
            for i in range(gx):
                tile = bf[k, j, i]
                at = row8 - (2 * i - 1)
                part = jnp.where((at >= 0) & (at < 4), pltpu.roll(tile, (2 * i - 1) % 8, 0), 0.0)
                f = part if f is None else f + part
                row = jnp.broadcast_to(tile[4:5], (8, 128))
                w = row if w is None else jnp.where(row8 < 2 * i, w, row)
            v.append(f)
            c.append(jnp.where(row8 % 2 == 0, w, pltpu.roll(w, 64, 1)))
        for yy in range(4):
            d = (lane8 // 16 - yy + 8) % 8
            w = jnp.where(d == 0, c[0], jnp.where(d == 1, c[1], c[2]))
            y = 4 * j + yy
            shift = (64 * (y // 16) - 16 * yy) % 128
            screens[y] = pltpu.roll(w, shift, 1) if shift else w
        for yy in range(6):
            y = 4 * j + yy - 1
            if not 0 <= y < 32:
                continue
            w = None
            for k in range(3):
                at = (lane8 - (20 * yy + 16 * k) + 256) % 128
                part = jnp.where(at < 18, v[k], 0.0)
                w = part if w is None else w + part
            w = pltpu.roll(w, (64 * (y // 16) - 20 * yy - 1) % 128, 1)
            total[y] = total[y] + w if y in total else w
    for m in range(16):
        cof[m] = jnp.where(z_ok, jnp.where(low, total[m], total[m + 16]), 0.0)
        coc[m] = jnp.where(z_ok, jnp.where(low, screens[m], screens[m + 16]), 0.0)
        cov[m] = coc[m] * cof[m]

    def coarse(i, v):
        twice = [m + m for m in v]
        sums = [twice[m] + pltpu.roll(v[m], 1, 1) + pltpu.roll(v[m], 127, 1) for m in range(16)]

        def other_half(m):
            u = pltpu.roll(v[m], 64, 1)
            return u + u + pltpu.roll(v[m], 65, 1) + pltpu.roll(v[m], 63, 1)

        wrap_up = jnp.where(low, 0.0, other_half(15))
        wrap_down = jnp.where(low, other_half(0), 0.0)
        new = []
        for m in range(16):
            a = (sums[m - 1] if m else wrap_up) + (sums[m + 1] if m < 15 else wrap_down) + (sums[m] + sums[m])
            b = (a + a) + jnp.where(row8 == 0, 0.0, pltpu.roll(a, 1, 0)) + jnp.where(row8 == 7, 0.0, pltpu.roll(a, 7, 0))
            c = coc[m]
            new.append(0.2 * v[m] + c * (cof[m] - twice[m]) + (0.25 * c) * b)
        return tuple(new)

    mid_sums = {}
    for p in range(10):
        if p == 0:
            xs, q, x_ok = 0, 7, ix > 0
        elif p < 9:
            xs, q, x_ok = 1, p - 1, None
        else:
            xs, q, x_ok = 2, 0, ix < gx - 1
        v = ex[p]
        v = jnp.where(lane24 == 64, pltpu.roll(zmid[0, xs], (-q) % 128, 1), v)
        v = jnp.where(lane24 == 127, pltpu.roll(zmid[1, xs], (127 - q) % 128, 1), v)
        ok = ok24 if x_ok is None else ok24 & x_ok
        mid_sums[p] = plane_sum(jnp.where(ok, v, 0.0))
    e1 = []
    for q in range(8):
        t = weigh(mid_sums, q + 1)[0:16]
        e = e_own[q][0:16]
        e1.append(0.2 * e + c1r[q + 1, 0:16] * (f1[q] + t - 2.0 * e))
    e1 = dot(jnp.concatenate(e1, axis=0), copy_mid).reshape(8, 16, 128)
    e1f[:, pl.ds(0, 16, 2), :] = e1
    e1f[:, pl.ds(1, 16, 2), :] = e1
    for p in range(NX):
        base[p] = vb[3 + p, 0:NY, 0:NZ] + e1f[p // 2]

    v = tuple(cov[m] for m in range(16))
    for i in range(ITERS - 1):
        v = coarse(i, v)
    for m in range(16):
        cov[m] = v[m]

    mine = cov[pl.ds(4 * lax.rem(iy, 4), 4)]
    mine = mine.reshape(32, 128)
    eout[...] = dot(mine, copy_coarse).reshape(4, 8, 128)
    for xc in range(2):
        for t in range(4):
            e3 = jnp.broadcast_to(eout[t, pl.ds(2 * ix + xc, 1), :], (8, 128))
            for p in range(8 * xc, 8 * xc + 8):
                rows = slice(8 * t, 8 * t + 8)
                out[p, rows, :] = base[p, rows, :] + e3


def on_device(sizes, guess, right_side, screen):
    vm = pltpu.VMEM
    return pl.pallas_call(
        functools.partial(kernel, sizes),
        out_shape=jax.ShapeDtypeStruct((NX, NY, NZ), F32),
        in_specs=[pl.BlockSpec(memory_space=pltpu.HBM)] * 3,
        out_specs=pl.BlockSpec(memory_space=pltpu.VMEM),
        scratch_shapes=[
            vm((3, PX, PY, PZ), F32),
            vm((PX, PY, PZ), F32),
            vm((PX, PY, PZ), F32),
            vm((PX, PY, PZ), F32),
            vm((2, NY, 128), F32),
            vm((2, 2, 8, 128), F32),
            vm((2, 3, PY, 128), F32),
            vm((2, 2, 8, 128), F32),
            vm((8, NY, 128), F32),
            vm((2, 10, PY, 128), F32),
            vm((2, 10, 24, 128), F32),
            vm((10, 24, 128), F32),
            vm((10, 24, 128), F32),
            vm((10, 24, 128), F32),
            vm((16, 128), F32),
            vm((2, 3, 24, 128), F32),
            vm((8, NY, 128), F32),
            vm((NX, NY, NZ), F32),
            vm((3, 5, 128), F32),
            vm((3, sizes[1], sizes[0], 8, 128), F32),
            vm((16, 8, 128), F32),
            vm((16, 8, 128), F32),
            vm((16, 8, 128), F32),
            vm((4, 8, 128), F32),
            vm((sizes[0] * sizes[1], 8, 128), F32),
            pltpu.SemaphoreType.DMA((3,)),
            pltpu.SemaphoreType.DMA((42,)),
            pltpu.SemaphoreType.DMA((42,)),
            pltpu.SemaphoreType.DMA((26,)),
            pltpu.SemaphoreType.DMA((26,)),
            pltpu.SemaphoreType.DMA((6,)),
            pltpu.SemaphoreType.REGULAR((3,)),
        ],
        compiler_params=pltpu.CompilerParams(
            collective_id=0, has_side_effects=True, vmem_limit_bytes=107 * 512 * 1024
        ),
        name="multigrid",
    )(guess, right_side, screen)


def solution(mesh):
    placed = P("gx", "gy", "gz")
    sizes = tuple(mesh.shape[a] for a in ("gx", "gy", "gz"))
    return jax.shard_map(
        functools.partial(on_device, sizes), mesh=mesh, in_specs=(placed,) * 3, out_specs=placed, check_vma=False
    )
```
